32 devices in a mesh: dp: 8 (over z, core), seq: 4 (over y, x).
Axes of the slice: x: 2, y: 2, z: 4, core: 2. Of those that a mesh axis runs over, the one named last changes fastest.
Arguments:
- tokens: bfloat16 [4, 8, 1024, 768], P(None, 'dp', 'seq'), may hold values from -6 to 6
- image_lengths: int32 [4, 8, 5], P(None, 'dp'), may hold values from 1 to 576, 1016 in all within a row
- cotangent: bfloat16 [4, 8, 1024, 768], P(None, 'dp', 'seq'), may hold values from -6 to 6
- attn_gain: float32 [768], replicated, may hold values from 0.5 to 1.5
- attn_shift: float32 [768], replicated, may hold values from -3 to 3
- qkv_weight: bfloat16 [768, 2304], replicated, may hold values from -0.21875 to 0.21875
- qv_bias: float32 [1536], replicated, may hold values from -3 to 3
- out_weight: bfloat16 [768, 768], replicated, may hold values from -2.5 to 2.5
- out_bias: float32 [768], replicated, may hold values from -2 to 2
- mlp_gain: float32 [768], replicated, may hold values from 0.5 to 1.5
- mlp_shift: float32 [768], replicated, may hold values from -3 to 3
- fc1_weight: bfloat16 [768, 3072], replicated, may hold values from -0.21875 to 0.21875
- fc1_bias: float32 [3072], replicated, may hold values from -3 to 3
- fc2_weight: bfloat16 [3072, 768], replicated, may hold values from -0.109375 to 0.109375
- fc2_bias: float32 [768], replicated, may hold values from -2 to 2
Outputs:
- block_out: bfloat16 [4, 8, 1024, 768], P(None, 'dp', 'seq')
- tokens_grad: bfloat16 [4, 8, 1024, 768], P(None, 'dp', 'seq')
- attn_gain_grad: float32 [768], replicated
- attn_shift_grad: float32 [768], replicated
- qkv_weight_grad: float32 [768, 2304], replicated
- qv_bias_grad: float32 [1536], replicated
- out_weight_grad: float32 [768, 768], replicated
- out_bias_grad: float32 [768], replicated
- mlp_gain_grad: float32 [768], replicated
- mlp_shift_grad: float32 [768], replicated
- fc1_weight_grad: float32 [768, 3072], replicated
- fc1_bias_grad: float32 [3072], replicated
- fc2_weight_grad: float32 [3072, 768], replicated
- fc2_bias_grad: float32 [768], replicated
The draws below stay inside these ranges and needn't reach their ends.
Inputs may be any that keep to these rules, and one draw needn't show every extreme that they name: Each row of image_lengths gives the patch counts of the row's 4 images in order, then the count of padding positions at the row's end; a row's entries sum to 1016, and its largest entry is exactly 576.
All inputs are finite; a program needn't handle non-finite values.
Results may differ from the reference program's by a relative error of at most 0.013.
Values may be sent and summed in bfloat16 or wider, within the bound.
A program may use at most 256 MiB of HBM per device.

```python
import math
import jax
import jax.numpy as jnp
import numpy as np
from jax import lax

D = 768
HEADS = 12
HEAD_DIM = 64
FF = 3072
ROW_LEN = 1024
IMGS = 4
MB = 4
ROWS = 8
MOST_LEN = 576


def block_scale(rng, shape, shards, low, top_value):
    gain, own = 1.0, jax.random.fold_in(rng, 6)
    for axis_at, blocks in shards:
        draws = jnp.exp(jax.random.uniform(jax.random.fold_in(own, axis_at), (blocks,), jnp.float32, low / len(shards), top_value / len(shards)))
        gain = gain * jnp.repeat(draws, shape[axis_at] // blocks).reshape([-1 if axis == axis_at else 1 for axis in range(len(shape))])
    return gain


def profile(count, total, limit, slope):
    weights = [(1 << 20) // math.isqrt(grade ** slope) + 1 for grade in range(2, count + 1)]
    surplus, given = total - limit - (count - 1), [1] * (count - 1)
    while surplus > 0:
        movable = [i for i in range(count - 1) if given[i] < limit]
        pool, left = sum([weights[i] for i in movable]), surplus
        for i in movable:
            extra = min(limit - given[i], max(1, left * weights[i] // pool), surplus)
            given[i] = given[i] + extra
            surplus = surplus - extra
    return np.array([limit] + given)


def ragged_sizes(stream_key, number_of, total, limit, lean):
    if number_of == 2:
        one = jax.random.randint(stream_key, (), max(1, total - limit), min(limit, total - 1) + 1)
        return jnp.stack([one, total - one])
    tallies = jnp.asarray(profile(number_of, total, limit, lean), jnp.int32)
    twos = (number_of - 1) // 2
    giver, sink = tallies[1:1 + 2 * twos:2], tallies[2:2 + 2 * twos:2]
    slack = jnp.minimum(giver - 1, limit - sink)
    passed = jax.random.randint(jax.random.fold_in(stream_key, 1), (twos,), 0, 1 << 20) % (slack + 1)
    tallies = tallies.at[1:1 + 2 * twos:2].set(giver - passed).at[2:2 + 2 * twos:2].set(sink + passed)
    return tallies[jax.random.permutation(jax.random.fold_in(stream_key, 2), number_of)]


def centred(key, dims, scale, reach, pieces=(), kind=jnp.bfloat16):
    result = scale * jax.random.normal(key, dims, jnp.float32)
    if pieces:
        result = result * block_scale(key, dims, pieces, -0.22, 0.18)
    return jnp.clip(result, -reach, reach).astype(kind)


def setup_inputs(seed: int = 0) -> dict:
    arg_keys = jax.random.split(jax.random.key(seed), 16)
    tokens = centred(arg_keys[0], (MB, ROWS, ROW_LEN, D), 1.0, 6.0, ((1, 8), (2, 4)))
    image_lengths = jax.vmap(lambda own: ragged_sizes(own, IMGS + 1, ROW_LEN - 2 * IMGS, MOST_LEN, 1))(jax.random.split(arg_keys[1], MB * ROWS)).reshape((MB, ROWS, IMGS + 1)).astype(jnp.int32)
    cotangent = centred(arg_keys[2], (MB, ROWS, ROW_LEN, D), 1.0, 6.0, ((1, 8), (2, 4)))
    attn_gain = jnp.clip(1.0 + 0.1 * jax.random.normal(arg_keys[3], (D,), jnp.float32), 0.5, 1.5)
    attn_shift = centred(arg_keys[4], (D,), 0.5, 3.0, (), jnp.float32)
    qkv_weight = centred(arg_keys[5], (D, 3 * D), D ** -0.5, 0.21875)
    qv_bias = centred(arg_keys[6], (2 * D,), 0.5, 3.0, (), jnp.float32)
    out_weight = centred(arg_keys[7], (D, D), (max(D // 128, 1)) ** -0.5, 2.5)
    out_bias = centred(arg_keys[8], (D,), 0.3, 2.0, (), jnp.float32)
    mlp_gain = jnp.clip(1.0 + 0.1 * jax.random.normal(arg_keys[9], (D,), jnp.float32), 0.5, 1.5)
    mlp_shift = centred(arg_keys[10], (D,), 0.5, 3.0, (), jnp.float32)
    fc1_weight = centred(arg_keys[11], (D, FF), D ** -0.5, 0.21875)
    fc1_bias = centred(arg_keys[12], (FF,), 0.5, 3.0, (), jnp.float32)
    fc2_weight = centred(arg_keys[13], (FF, D), FF ** -0.5, 0.109375)
    fc2_bias = centred(arg_keys[14], (D,), 0.3, 2.0, (), jnp.float32)
    return dict(tokens=tokens, image_lengths=image_lengths, cotangent=cotangent, attn_gain=attn_gain, attn_shift=attn_shift, qkv_weight=qkv_weight, qv_bias=qv_bias, out_weight=out_weight, out_bias=out_bias, mlp_gain=mlp_gain, mlp_shift=mlp_shift, fc1_weight=fc1_weight, fc1_bias=fc1_bias, fc2_weight=fc2_weight, fc2_bias=fc2_bias)


EPS = 1e-06
NEG = -1e+30
HIGH = lax.Precision.HIGHEST

@jax.custom_vjp
def low(v):
    return lax.optimization_barrier(v.astype(jnp.bfloat16)).astype(jnp.float32)

@jax.custom_vjp
def low_back(v):
    return v

def low_keep(v):
    return (low(v), None)

def low_pass(kept, grad):
    return (grad,)

def back_keep(v):
    return (v, None)

def back_low(kept, grad):
    return (low(grad),)
low.defvjp(low_keep, low_pass)
low_back.defvjp(back_keep, back_low)

def layer_norm(values, scale_row, shift_row):
    center = values - lax.optimization_barrier(jnp.mean(values, axis=-1, keepdims=True))
    spread = lax.optimization_barrier(jnp.mean(center * center, axis=-1, keepdims=True))
    return center * lax.rsqrt(spread + EPS) * scale_row + shift_row

def segment_ids(lengths):
    positions = jnp.arange(ROW_LEN, dtype=jnp.int32)
    ends = jnp.cumsum(lengths, axis=-1).astype(jnp.int32) + 2 * IMGS
    patches = lax.optimization_barrier(jnp.sum((positions[:, None] >= ends[..., None, :]).astype(jnp.int32), axis=-1))
    return jnp.where(positions < 2 * IMGS, positions // 2, patches).astype(jnp.int32)

def block(inputs, segment, attn_gain, attn_shift, qkv_weight, qv_bias, out_weight, out_bias, mlp_gain, mlp_shift, fc1_weight, fc1_bias, fc2_weight, fc2_bias):
    normed = low(layer_norm(inputs, attn_gain, attn_shift))
    zero_keys = jnp.zeros((D,), jnp.float32)
    full_bias = jnp.concatenate([qv_bias[:D], zero_keys, qv_bias[D:]])
    projected = jnp.dot(normed, qkv_weight, precision=HIGH) + full_bias
    projected = low(low_back(projected)).reshape(ROW_LEN, 3, HEADS, HEAD_DIM)
    queries = projected[:, 0]
    keys_part = projected[:, 1]
    values_part = projected[:, 2]
    scores = jnp.einsum('qhd,khd->hqk', queries, keys_part, precision=HIGH) * HEAD_DIM ** (-0.5)
    scores = low_back(scores)
    allowed = segment[:, None] == segment[None, :]
    scores = jnp.where(allowed[None], scores, NEG)
    largest = lax.optimization_barrier(jnp.max(scores, axis=-1, keepdims=True))
    expo = jnp.exp(scores - largest)
    weights_low = low(expo / lax.optimization_barrier(jnp.sum(expo, axis=-1, keepdims=True)))
    attended = jnp.einsum('hqk,khd->qhd', weights_low, values_part, precision=HIGH).reshape(ROW_LEN, D)
    attended = low(low_back(attended))
    branch = low_back(jnp.dot(attended, out_weight, precision=HIGH) + out_bias)
    middle = inputs + branch
    normed_two = low(layer_norm(middle, mlp_gain, mlp_shift))
    hidden_pre = low_back(jnp.dot(normed_two, fc1_weight, precision=HIGH) + fc1_bias)
    hidden = low(jax.nn.gelu(hidden_pre, approximate=False))
    return middle + jnp.dot(hidden, fc2_weight, precision=HIGH) + fc2_bias

def reference(tokens, image_lengths, cotangent, attn_gain, attn_shift, qkv_weight, qv_bias, out_weight, out_bias, mlp_gain, mlp_shift, fc1_weight, fc1_bias, fc2_weight, fc2_bias):
    params = (attn_gain.astype(jnp.float32), attn_shift.astype(jnp.float32), qkv_weight.astype(jnp.float32), qv_bias.astype(jnp.float32), out_weight.astype(jnp.float32), out_bias.astype(jnp.float32), mlp_gain.astype(jnp.float32), mlp_shift.astype(jnp.float32), fc1_weight.astype(jnp.float32), fc1_bias.astype(jnp.float32), fc2_weight.astype(jnp.float32), fc2_bias.astype(jnp.float32))
    flat_tokens = tokens.astype(jnp.float32).reshape(MB * ROWS, ROW_LEN, D)
    flat_cot = cotangent.astype(jnp.float32).reshape(MB * ROWS, ROW_LEN, D)
    segments = segment_ids(image_lengths.reshape(MB * ROWS, IMGS + 1))

    def one_row(running, item):
        row_in, row_cot, segment = item

        def run_block(row, *weights):
            return block(row, segment, *weights)
        row_out, pull = jax.vjp(run_block, row_in, *params)
        pulled = pull(row_cot)
        running = tuple((before + member for before, member in zip(running, pulled[1:])))
        return (running, (row_out.astype(jnp.bfloat16), pulled[0].astype(jnp.bfloat16)))
    start = tuple((jnp.zeros_like(weight) for weight in params))
    totals, (outputs, input_grads) = lax.scan(one_row, start, (flat_tokens, flat_cot, segments))
    return (outputs.reshape(tokens.shape), input_grads.reshape(tokens.shape), totals[0], totals[1], totals[2], totals[3], totals[4], totals[5], totals[6], totals[7], totals[8], totals[9], totals[10], totals[11])
```

```python
import functools

import jax
import jax.numpy as jnp
from jax import lax
from jax.experimental import pallas as pl
from jax.experimental.pallas import tpu as pltpu
from jax.sharding import PartitionSpec as P

HEADS = 12


EPS = 1e-06
NEG = -1e30


def layer_norm(values, scale_row, shift_row):
    center = values - jnp.mean(values, axis=-1, keepdims=True)
    spread = jnp.mean(center * center, axis=-1, keepdims=True)
    return center * lax.rsqrt(spread + EPS) * scale_row + shift_row


def gelu_exact(values):
    return jax.nn.gelu(values, approximate=False)


def segment_ids(lengths, row_len, images):
    positions = jnp.arange(row_len, dtype=jnp.int32)
    ends = jnp.cumsum(lengths, axis=-1) + 2 * images
    patches = jnp.sum((positions[:, None] >= ends[..., None, :]).astype(jnp.int32), axis=-1)
    return jnp.where(positions < 2 * images, positions // 2, patches)


def matmul(first_op, second_op, pattern):
    return jnp.einsum(pattern, first_op, second_op, preferred_element_type=jnp.float32)


def general_shards(
    tokens,
    image_lengths,
    cotangent,
    attn_gain,
    attn_shift,
    qkv_weight,
    qv_bias,
    out_weight,
    out_bias,
    mlp_gain,
    mlp_shift,
    fc1_weight,
    fc1_bias,
    fc2_weight,
    fc2_bias,
):
    micro_count, row_count, shard_len, features = tokens.shape
    row_len = shard_len * lax.axis_size("seq")
    images = image_lengths.shape[2] - 1
    head_dim = features // HEADS
    score_scale = head_dim ** (-0.5)
    offset = lax.axis_index("seq") * shard_len
    tok_count = row_count * shard_len
    zero_keys = jnp.zeros((features,), jnp.float32)
    full_bias = jnp.concatenate([qv_bias[:features], zero_keys, qv_bias[features:]])
    totals = [
        jnp.zeros(weight.shape, jnp.float32)
        for weight in (
            attn_gain,
            attn_shift,
            qkv_weight,
            qv_bias,
            out_weight,
            out_bias,
            mlp_gain,
            mlp_shift,
            fc1_weight,
            fc1_bias,
            fc2_weight,
            fc2_bias,
        )
    ]
    outputs_list = []
    grads_list = []
    for micro_step in range(micro_count):
        inputs = tokens[micro_step].astype(jnp.float32)
        seg_all = segment_ids(image_lengths[micro_step], row_len, images)
        seg_here = lax.dynamic_slice_in_dim(seg_all, offset, shard_len, 1)
        allowed = seg_here[:, None, :, None] == seg_all[:, None, None, :]
        normed, first_pull = jax.vjp(layer_norm, inputs, attn_gain, attn_shift)
        normed_low = normed.astype(jnp.bfloat16).reshape(tok_count, features)
        projected = (matmul(normed_low, qkv_weight, "td,de->te") + full_bias).astype(jnp.bfloat16)
        projected = projected.reshape(row_count, shard_len, 3 * features)
        queries = projected[:, :, :features].reshape(row_count, shard_len, HEADS, head_dim)
        keys_all, values_all = (
            lax.all_gather(projected[:, :, features : 2 * features], "seq", axis=1, tiled=True),
            lax.all_gather(projected[:, :, 2 * features :], "seq", axis=1, tiled=True),
        )
        keys_all = keys_all.reshape(row_count, row_len, HEADS, head_dim)
        values_all = values_all.reshape(row_count, row_len, HEADS, head_dim)
        scores = jnp.where(allowed, matmul(queries, keys_all, "rqhd,rkhd->rhqk") * score_scale, NEG)
        largest = jnp.max(scores, axis=-1, keepdims=True)
        log_total = largest + jnp.log(jnp.sum(jnp.exp(scores - largest), axis=-1, keepdims=True))
        weights_low = jnp.exp(scores - log_total).astype(jnp.bfloat16)
        attended = (
            matmul(weights_low, values_all, "rhqk,rkhd->rqhd")
            .astype(jnp.bfloat16)
            .reshape(tok_count, features)
        )
        branch = matmul(attended, out_weight, "td,de->te") + out_bias
        middle = inputs + branch.reshape(inputs.shape)
        normed_two, second_pull = jax.vjp(layer_norm, middle, mlp_gain, mlp_shift)
        normed_two_low = normed_two.astype(jnp.bfloat16).reshape(tok_count, features)
        hidden_pre = matmul(normed_two_low, fc1_weight, "td,df->tf") + fc1_bias
        hidden, gelu_pull = jax.vjp(gelu_exact, hidden_pre)
        hidden_low = hidden.astype(jnp.bfloat16)
        result = middle + (matmul(hidden_low, fc2_weight, "tf,fd->td") + fc2_bias).reshape(
            inputs.shape
        )
        outputs_list.append(result.astype(jnp.bfloat16))
        incoming = cotangent[micro_step].reshape(tok_count, features)
        fc2_weight_part = matmul(hidden_low, incoming, "tf,td->fd")
        fc2_bias_part = jnp.sum(incoming.astype(jnp.float32), axis=0)
        hidden_grad = gelu_pull(matmul(incoming, fc2_weight, "td,fd->tf"))[0].astype(jnp.bfloat16)
        fc1_weight_part = matmul(normed_two_low, hidden_grad, "td,tf->df")
        fc1_bias_part = jnp.sum(hidden_grad.astype(jnp.float32), axis=0)
        back_two = matmul(hidden_grad, fc1_weight, "tf,df->td").reshape(inputs.shape)
        middle_norm, mlp_gain_part, mlp_shift_part = second_pull(back_two)
        middle_grad = incoming.astype(jnp.float32).reshape(inputs.shape) + middle_norm
        branch_grad = middle_grad.astype(jnp.bfloat16).reshape(tok_count, features)
        out_weight_part = matmul(attended, branch_grad, "td,te->de")
        out_bias_part = jnp.sum(branch_grad.astype(jnp.float32), axis=0)
        attended_grad = matmul(branch_grad, out_weight, "te,de->td").astype(jnp.bfloat16)
        attended_grad = attended_grad.reshape(row_count, shard_len, HEADS, head_dim)
        scores_again = jnp.where(
            allowed, matmul(queries, keys_all, "rqhd,rkhd->rhqk") * score_scale, NEG
        )
        chances = jnp.exp(scores_again - log_total)
        chances_low = chances.astype(jnp.bfloat16)
        chance_grad = matmul(attended_grad, values_all, "rqhd,rkhd->rhqk")
        row_delta = jnp.sum(chances * chance_grad, axis=-1, keepdims=True)
        score_grad = (chances * (chance_grad - row_delta)).astype(jnp.bfloat16)
        query_grad = matmul(score_grad, keys_all, "rhqk,rkhd->rqhd") * score_scale
        key_terms = matmul(score_grad, queries, "rhqk,rqhd->rkhd") * score_scale
        value_terms = matmul(chances_low, attended_grad, "rhqk,rqhd->rkhd")
        key_grad, value_grad = (
            lax.psum_scatter(
                key_terms.reshape(row_count, row_len, features).astype(jnp.bfloat16),
                "seq",
                scatter_dimension=1,
                tiled=True,
            ).astype(jnp.float32),
            lax.psum_scatter(
                value_terms.reshape(row_count, row_len, features).astype(jnp.bfloat16),
                "seq",
                scatter_dimension=1,
                tiled=True,
            ).astype(jnp.float32),
        )
        projected_grad = jnp.concatenate(
            [query_grad.reshape(row_count, shard_len, features), key_grad, value_grad], axis=-1
        )
        projected_grad = projected_grad.astype(jnp.bfloat16).reshape(tok_count, 3 * features)
        qkv_weight_part = matmul(normed_low, projected_grad, "td,te->de")
        bias_sums = jnp.sum(projected_grad.astype(jnp.float32), axis=0)
        qv_bias_part = jnp.concatenate([bias_sums[:features], bias_sums[2 * features :]])
        back_one = matmul(projected_grad, qkv_weight, "te,de->td").reshape(inputs.shape)
        inputs_norm, attn_gain_part, attn_shift_part = first_pull(back_one)
        grads_list.append((middle_grad + inputs_norm).astype(jnp.bfloat16))
        pieces = (
            attn_gain_part,
            attn_shift_part,
            qkv_weight_part,
            qv_bias_part,
            out_weight_part,
            out_bias_part,
            mlp_gain_part,
            mlp_shift_part,
            fc1_weight_part,
            fc1_bias_part,
            fc2_weight_part,
            fc2_bias_part,
        )
        totals = [running + member for running, member in zip(totals, pieces)]
    (
        attn_gain_sum,
        attn_shift_sum,
        qkv_weight_sum,
        qv_bias_sum,
        out_weight_sum,
        out_bias_sum,
        mlp_gain_sum,
        mlp_shift_sum,
        fc1_weight_sum,
        fc1_bias_sum,
        fc2_weight_sum,
        fc2_bias_sum,
    ) = totals
    summed = lax.psum(
        (
            attn_gain_sum,
            attn_shift_sum,
            qkv_weight_sum,
            qv_bias_sum,
            out_weight_sum,
            out_bias_sum,
            mlp_gain_sum,
            mlp_shift_sum,
            fc1_weight_sum,
            fc1_bias_sum,
            fc2_weight_sum,
            fc2_bias_sum,
        ),
        ("dp", "seq"),
    )
    return (jnp.stack(outputs_list), jnp.stack(grads_list)) + tuple(summed)

F32 = jnp.float32
BF = jnp.bfloat16
BIG = 1e30


def dot_rows(first_op, second_op):
    return lax.dot_general(first_op, second_op, (((1,), (1,)), ((), ())), preferred_element_type=F32)


def dot_plain(first_op, second_op):
    return lax.dot_general(first_op, second_op, (((1,), (0,)), ((), ())), preferred_element_type=F32)


def dot_tokens(first_op, second_op):
    return lax.dot_general(first_op, second_op, (((0,), (0,)), ((), ())), preferred_element_type=F32)


def attention_forward_kernel(block, q_ref, k_ref, v_ref, miss_ref, own_ref, out_ref, lse_ref):
    lane = lax.broadcasted_iota(jnp.int32, (1, 128), 1)
    first = lane < 64
    keys, values, own = k_ref[...], v_ref[...], own_ref[...]
    ones = jnp.ones_like(values)
    keys_aug = [jnp.where(first, keys, own), jnp.where(first, own, keys)]
    values_aug = [jnp.where(first, values, ones), jnp.where(first, ones, values)]
    for step in range(q_ref.shape[0] // block):
        rows = pl.ds(step * block, block)
        queries, miss = q_ref[rows, :] * BF(0.125), miss_ref[rows, :]
        outs, logs = [], []
        for head in range(2):
            queries_aug = jnp.where(first, queries, miss) if head == 0 else jnp.where(first, miss, queries)
            scores = dot_rows(queries_aug, keys_aug[head])
            largest = jnp.max(scores, axis=1, keepdims=True)
            weights = jnp.exp(scores - largest).astype(BF)
            mixed = dot_plain(weights, values_aug[head])
            total = mixed[:, 64:65] if head == 0 else mixed[:, 0:1]
            outs.append(mixed / total)
            logs.append(largest + jnp.log(total))
        out_ref[rows, :] = jnp.where(first, outs[0], outs[1]).astype(BF)
        lse_ref[0, rows, :] = jnp.where(first, logs[0], logs[1])


def attention_forward(projected, miss, own, block=256):
    count, width = projected.shape
    pairs = width // 384
    column = lambda base: pl.BlockSpec((count, 128), lambda i: (0, i + base))
    full = pl.BlockSpec((count, 128), lambda i: (0, 0))
    return pl.pallas_call(
        functools.partial(attention_forward_kernel, block),
        grid=(pairs,),
        in_specs=[column(0), column(pairs), column(2 * pairs), full, full],
        out_specs=[column(0), pl.BlockSpec((1, count, 128), lambda i: (i, 0, 0))],
        out_shape=[
            jax.ShapeDtypeStruct((count, width // 3), BF),
            jax.ShapeDtypeStruct((pairs, count, 128), F32),
        ],
        compiler_params=pltpu.CompilerParams(vmem_limit_bytes=40 * 2**20),
        cost_estimate=pl.CostEstimate(flops=24 * 10**9, bytes_accessed=8 * 2**20, transcendentals=12 * 2**20),
        name="attention_forward",
    )(projected, projected, projected, miss, own)


def three_parts(column):
    high = column.astype(BF)
    rest = column - high.astype(F32)
    middle = rest.astype(BF)
    return high, middle, (rest - middle.astype(F32)).astype(BF)


def attention_backward_kernel(
    block, q_ref, k_ref, v_ref, att_ref, grad_ref, lse_ref, miss_ref, own_ref,
    dq_ref, dk_ref, dv_ref, dk_acc, dv_acc,
):
    lane = lax.broadcasted_iota(jnp.int32, (1, 128), 1)
    first = lane < 64
    half = lane % 64
    keys, values, own = k_ref[...], v_ref[...], own_ref[...]
    unit = jnp.where((half >= 8) & (half < 11), 1.0, 0.0).astype(BF)
    own = own + unit
    unit_rows = jnp.broadcast_to(unit, values.shape)
    keys_aug = [jnp.where(first, keys, own), jnp.where(first, own, keys)]
    values_aug = [jnp.where(first, values, unit_rows), jnp.where(first, unit_rows, values)]
    keys_only = [jnp.where(first, keys, BF(0)), jnp.where(first, BF(0), keys)]
    dk_acc[...] = jnp.zeros_like(dk_acc)
    dv_acc[...] = jnp.zeros_like(dv_acc)

    def spread(column):
        high, middle, low = [part.astype(F32) for part in three_parts(-column)]
        wide = jnp.where(half == 8, high, jnp.where(half == 9, middle, jnp.where(half == 10, low, 0.0)))
        return wide.astype(BF)

    def body(step, carry):
        rows = pl.ds(pl.multiple_of(step * block, block), block)
        queries, miss, grad = q_ref[rows, :] * BF(0.125), miss_ref[rows, :], grad_ref[rows, :]
        both = att_ref[rows, :].astype(F32) * grad.astype(F32)
        logs = lse_ref[0, rows, :]
        queries_t, grad_t = queries.T, grad.T
        dq = jnp.zeros((block, 128), F32)
        for head in range(2):
            mine = first if head == 0 else jnp.logical_not(first)
            span = pl.ds(64 * head, 64)
            delta = jnp.sum(jnp.where(mine, both, 0.0), axis=1, keepdims=True)
            total = logs[:, 0:1] if head == 0 else logs[:, 64:65]
            queries_aug = jnp.where(mine, queries, spread(total) + miss)
            grad_aug = jnp.where(mine, grad, spread(delta))
            probs = jnp.exp(dot_rows(queries_aug, keys_aug[head]))
            score_grad = (probs * dot_rows(grad_aug, values_aug[head])).astype(BF)
            dq = dq + dot_plain(score_grad, keys_only[head])
            dk_acc[span, :] += dot_plain(queries_t[64 * head : 64 * head + 64], score_grad)
            dv_acc[span, :] += dot_plain(grad_t[64 * head : 64 * head + 64], probs.astype(BF))
        dq_ref[rows, :] = (dq * 0.125).astype(BF)
        return carry

    lax.fori_loop(0, q_ref.shape[0] // block, body, 0)
    dk_ref[...] = dk_acc[...].T.astype(BF)
    dv_ref[...] = dv_acc[...].T.astype(BF)


def attention_backward(projected, attended, attended_grad, logs, miss, own, block=256):
    count, width = projected.shape
    pairs = width // 384
    column = lambda base: pl.BlockSpec((count, 128), lambda i: (0, i + base))
    full = pl.BlockSpec((count, 128), lambda i: (0, 0))
    return pl.pallas_call(
        functools.partial(attention_backward_kernel, block),
        grid=(pairs,),
        in_specs=[
            column(0), column(pairs), column(2 * pairs), column(0), column(0),
            pl.BlockSpec((1, count, 128), lambda i: (i, 0, 0)), full, full,
        ],
        out_specs=[column(0)] * 3,
        out_shape=[jax.ShapeDtypeStruct((count, width // 3), BF)] * 3,
        scratch_shapes=[pltpu.VMEM((128, count), F32)] * 2,
        compiler_params=pltpu.CompilerParams(vmem_limit_bytes=40 * 2**20),
        cost_estimate=pl.CostEstimate(flops=40 * 10**9, bytes_accessed=16 * 2**20, transcendentals=12 * 2**20),
        name="attention_backward",
    )(projected, projected, projected, attended, attended_grad, logs, miss, own)


def segment_features(segment):
    lane = jnp.arange(128) % 64
    same = lane[None, :] == segment[:, None]
    live = (lane < 8)[None, :]
    return jnp.where(live & ~same, -BIG, 0.0).astype(BF), jnp.where(live & same, 1.0, 0.0).astype(BF)


def gelu_parts(values):
    size = jnp.abs(values)
    bell = jnp.exp(-0.5 * values * values)
    part = 1.0 / (1.0 + 0.3275911 * 0.7071067811865476 * size)
    series = part * (
        0.254829592
        + part * (-0.284496736 + part * (1.421413741 + part * (-1.453152027 + part * 1.061405429)))
    )
    tail = 0.5 * series * bell
    below = jnp.where(values >= 0, 1.0 - tail, tail)
    return values * below, below + values * bell * 0.3989422804014327


def swap(array, axis, bit):
    count = lax.axis_size(axis)
    return lax.ppermute(array, axis, [(i, i ^ bit) for i in range(count)])


def pick(array, index):
    return lax.dynamic_index_in_dim(array, index, 0, keepdims=False)


def half_of(array, index):
    size = array.shape[0] // 2
    return lax.dynamic_slice_in_dim(array, index * size, size, 0)


def join(own, other, bit):
    size = own.shape[0]
    both = jnp.zeros((2 * size,) + own.shape[1:], own.dtype)
    both = lax.dynamic_update_slice_in_dim(both, own, bit * size, 0)
    return lax.dynamic_update_slice_in_dim(both, other, (1 - bit) * size, 0)


def reduce_everywhere(send, keep, stages):
    axis, bit, mine = stages[0]
    got = swap(send, axis, bit)
    core = mine
    for axis, bit, mine in stages[1:]:
        out = (half_of(keep, 1 - mine).astype(F32) + half_of(got, 1 - mine).astype(F32)).astype(BF)
        keep = (half_of(keep, mine).astype(F32) + half_of(got, mine).astype(F32)).astype(BF)
        got = swap(out, axis, bit)
    total = (keep.astype(F32) + got.astype(F32)).astype(BF)
    for axis, bit, mine in reversed(stages[1:]):
        total = join(total, swap(total, axis, bit), mine)
    axis, bit, mine = stages[0]
    return total, swap(total, axis, bit)


def split_grad(left, right, core, stages):
    size = right.shape[1] // 2
    parts = [
        dot_tokens(left, lax.dynamic_slice_in_dim(right, index * size, size, 1)).astype(BF)
        for index in (1 - core, core)
    ]
    own, other = reduce_everywhere(parts[0], parts[1], stages)
    low = jnp.where(core == 0, own, other)
    high = jnp.where(core == 0, other, own)
    return jnp.concatenate([low, high], axis=1).astype(F32)


def fast_shards(
    tokens, image_lengths, cotangent, attn_gain, attn_shift, qkv_weight, qv_bias, out_weight,
    out_bias, mlp_gain, mlp_shift, fc1_weight, fc1_bias, fc2_weight, fc2_bias,
):
    micro_count, _, shard_len, features = tokens.shape
    parties = micro_count
    row_len = shard_len * parties
    images = image_lengths.shape[2] - 1
    me = lax.axis_index("seq")
    depth = lax.axis_index("dp")
    core = depth % 2

    def bits(axis, index, low):
        count = lax.axis_size(axis)
        return [(axis, 1 << k, (index >> k) & 1) for k in range(low, count.bit_length() - 1)]

    core_stage = [("dp", 1, core)]
    flat_bits, deep_bits = bits("seq", me, 0), bits("dp", depth, 1)
    orders = [core_stage + flat_bits + deep_bits, core_stage + flat_bits[::-1] + deep_bits]

    def gather_row(array):
        pieces = [pick(array, me)[0]]
        for k in range(1, parties):
            pieces.append(swap(pick(array, me ^ k)[0], "seq", k))
        return jnp.concatenate(pieces, axis=0)

    def scatter_row(array):
        out = jnp.zeros(tokens.shape, BF)
        for k in range(parties):
            piece = array[k * shard_len : (k + 1) * shard_len]
            if k:
                piece = swap(piece, "seq", k)
            out = lax.dynamic_update_slice(out, piece[None, None], (me ^ k, 0, 0, 0))
        return out

    seg_row = segment_ids(pick(image_lengths, me), row_len, images).reshape(parties, shard_len)
    segment = jnp.concatenate([pick(seg_row, me ^ k) for k in range(parties)], axis=0)
    miss, own = segment_features(segment)

    inputs = gather_row(tokens).astype(F32)
    incoming = gather_row(cotangent)
    full_bias = jnp.concatenate([qv_bias[:features], jnp.zeros((features,), F32), qv_bias[features:]])
    normed, first_pull = jax.vjp(layer_norm, inputs, attn_gain, attn_shift)
    normed_low = normed.astype(BF)
    projected = (dot_plain(normed_low, qkv_weight) + full_bias).astype(BF)
    attended, logs = attention_forward(projected, miss, own)
    middle = inputs + dot_plain(attended, out_weight) + out_bias
    normed_two, second_pull = jax.vjp(layer_norm, middle, mlp_gain, mlp_shift)
    normed_two_low = normed_two.astype(BF)
    hidden_pre = dot_plain(normed_two_low, fc1_weight) + fc1_bias
    hidden, slope = gelu_parts(hidden_pre)
    hidden_low = hidden.astype(BF)
    result = (middle + dot_plain(hidden_low, fc2_weight) + fc2_bias).astype(BF)
    block_out = scatter_row(result)
    hidden_grad = (dot_rows(incoming, fc2_weight) * slope).astype(BF)

    half_hidden = hidden_low.shape[1] // 2
    fc2_parts = [
        dot_tokens(lax.dynamic_slice_in_dim(hidden_low, index * half_hidden, half_hidden, 1), incoming).astype(BF)
        for index in (1 - core, core)
    ]
    fc2_own, fc2_other = reduce_everywhere(fc2_parts[0], fc2_parts[1], orders[0])
    fc2_grad = jnp.concatenate(
        [jnp.where(core == 0, fc2_own, fc2_other), jnp.where(core == 0, fc2_other, fc2_own)], axis=0
    ).astype(F32)
    fc1_grad = split_grad(normed_two_low, hidden_grad, core, orders[1])

    back_two = dot_rows(hidden_grad, fc1_weight)
    middle_norm, mlp_gain_part, mlp_shift_part = second_pull(back_two)
    middle_grad = incoming.astype(F32) + middle_norm
    branch_grad = middle_grad.astype(BF)
    out_grad = split_grad(attended, branch_grad, core, orders[0])
    attended_grad = dot_rows(branch_grad, out_weight).astype(BF)
    pieces = attention_backward(projected, attended, attended_grad, logs, miss, own)
    projected_grad = jnp.concatenate(pieces, axis=1)
    qkv_grads = [split_grad(normed_low, piece, core, orders[i % 2]) for i, piece in enumerate(pieces)]
    back_one = dot_rows(projected_grad, qkv_weight)
    inputs_norm, attn_gain_part, attn_shift_part = first_pull(back_one)
    tokens_grad = scatter_row((middle_grad + inputs_norm).astype(BF))

    column = lambda array: jnp.sum(array.astype(F32), axis=0)
    sums = [
        attn_gain_part, attn_shift_part, column(pieces[0]), column(pieces[2]), column(branch_grad),
        mlp_gain_part, mlp_shift_part, column(hidden_grad), column(incoming),
    ]
    vector = jnp.concatenate(sums)
    for axis, bit, _ in orders[0]:
        vector = vector + swap(vector, axis, bit)
    cuts = []
    for part in sums:
        cuts.append(vector[: part.shape[0]])
        vector = vector[part.shape[0] :]
    return (
        block_out, tokens_grad, cuts[0], cuts[1], jnp.concatenate(qkv_grads, axis=1),
        jnp.concatenate(cuts[2:4]), out_grad, cuts[4], cuts[5], cuts[6], fc1_grad, cuts[7],
        fc2_grad, cuts[8],
    )


def shards(tokens, *rest):
    micro_count, row_count, shard_len, features = tokens.shape
    sizes = (lax.axis_size("dp"), lax.axis_size("seq"))
    powers = all(size & (size - 1) == 0 for size in sizes) and sizes[0] > 1
    whole_rows = micro_count == sizes[1] and row_count == 1
    if powers and whole_rows and shard_len % 128 == 0 and features == 64 * HEADS and HEADS % 2 == 0:
        return fast_shards(tokens, *rest)
    return general_shards(tokens, *rest)


def solution(mesh):
    placed = (
        P(None, "dp", "seq", None),
        P(None, "dp", None),
        P(None, "dp", "seq", None),
        P(),
        P(),
        P(),
        P(),
        P(),
        P(),
        P(),
        P(),
        P(),
        P(),
        P(),
        P(),
    )
    return jax.shard_map(
        shards,
        mesh=mesh,
        in_specs=placed,
        out_specs=(
            P(None, "dp", "seq", None),
            P(None, "dp", "seq", None),
            P(),
            P(),
            P(),
            P(),
            P(),
            P(),
            P(),
            P(),
            P(),
            P(),
            P(),
            P(),
        ),
        check_vma=False,
    )
```

```python
import functools

import jax
import jax.numpy as jnp
from jax import lax
from jax.experimental import pallas as pl
from jax.experimental.pallas import tpu as pltpu
from jax.sharding import PartitionSpec as P

HEADS = 12


EPS = 1e-06
NEG = -1e30


def layer_norm(values, scale_row, shift_row):
    center = values - jnp.mean(values, axis=-1, keepdims=True)
    spread = jnp.mean(center * center, axis=-1, keepdims=True)
    return center * lax.rsqrt(spread + EPS) * scale_row + shift_row


def gelu_exact(values):
    return jax.nn.gelu(values, approximate=False)


def segment_ids(lengths, row_len, images):
    positions = jnp.arange(row_len, dtype=jnp.int32)
    ends = jnp.cumsum(lengths, axis=-1) + 2 * images
    patches = jnp.sum((positions[:, None] >= ends[..., None, :]).astype(jnp.int32), axis=-1)
    return jnp.where(positions < 2 * images, positions // 2, patches)


def matmul(first_op, second_op, pattern):
    return jnp.einsum(pattern, first_op, second_op, preferred_element_type=jnp.float32)


def general_shards(
    tokens,
    image_lengths,
    cotangent,
    attn_gain,
    attn_shift,
    qkv_weight,
    qv_bias,
    out_weight,
    out_bias,
    mlp_gain,
    mlp_shift,
    fc1_weight,
    fc1_bias,
    fc2_weight,
    fc2_bias,
):
    micro_count, row_count, shard_len, features = tokens.shape
    row_len = shard_len * lax.axis_size("seq")
    images = image_lengths.shape[2] - 1
    head_dim = features // HEADS
    score_scale = head_dim ** (-0.5)
    offset = lax.axis_index("seq") * shard_len
    tok_count = row_count * shard_len
    zero_keys = jnp.zeros((features,), jnp.float32)
    full_bias = jnp.concatenate([qv_bias[:features], zero_keys, qv_bias[features:]])
    totals = [
        jnp.zeros(weight.shape, jnp.float32)
        for weight in (
            attn_gain,
            attn_shift,
            qkv_weight,
            qv_bias,
            out_weight,
            out_bias,
            mlp_gain,
            mlp_shift,
            fc1_weight,
            fc1_bias,
            fc2_weight,
            fc2_bias,
        )
    ]
    outputs_list = []
    grads_list = []
    for micro_step in range(micro_count):
        inputs = tokens[micro_step].astype(jnp.float32)
        seg_all = segment_ids(image_lengths[micro_step], row_len, images)
        seg_here = lax.dynamic_slice_in_dim(seg_all, offset, shard_len, 1)
        allowed = seg_here[:, None, :, None] == seg_all[:, None, None, :]
        normed, first_pull = jax.vjp(layer_norm, inputs, attn_gain, attn_shift)
        normed_low = normed.astype(jnp.bfloat16).reshape(tok_count, features)
        projected = (matmul(normed_low, qkv_weight, "td,de->te") + full_bias).astype(jnp.bfloat16)
        projected = projected.reshape(row_count, shard_len, 3 * features)
        queries = projected[:, :, :features].reshape(row_count, shard_len, HEADS, head_dim)
        keys_all, values_all = (
            lax.all_gather(projected[:, :, features : 2 * features], "seq", axis=1, tiled=True),
            lax.all_gather(projected[:, :, 2 * features :], "seq", axis=1, tiled=True),
        )
        keys_all = keys_all.reshape(row_count, row_len, HEADS, head_dim)
        values_all = values_all.reshape(row_count, row_len, HEADS, head_dim)
        scores = jnp.where(allowed, matmul(queries, keys_all, "rqhd,rkhd->rhqk") * score_scale, NEG)
        largest = jnp.max(scores, axis=-1, keepdims=True)
        log_total = largest + jnp.log(jnp.sum(jnp.exp(scores - largest), axis=-1, keepdims=True))
        weights_low = jnp.exp(scores - log_total).astype(jnp.bfloat16)
        attended = (
            matmul(weights_low, values_all, "rhqk,rkhd->rqhd")
            .astype(jnp.bfloat16)
            .reshape(tok_count, features)
        )
        branch = matmul(attended, out_weight, "td,de->te") + out_bias
        middle = inputs + branch.reshape(inputs.shape)
        normed_two, second_pull = jax.vjp(layer_norm, middle, mlp_gain, mlp_shift)
        normed_two_low = normed_two.astype(jnp.bfloat16).reshape(tok_count, features)
        hidden_pre = matmul(normed_two_low, fc1_weight, "td,df->tf") + fc1_bias
        hidden, gelu_pull = jax.vjp(gelu_exact, hidden_pre)
        hidden_low = hidden.astype(jnp.bfloat16)
        result = middle + (matmul(hidden_low, fc2_weight, "tf,fd->td") + fc2_bias).reshape(
            inputs.shape
        )
        outputs_list.append(result.astype(jnp.bfloat16))
        incoming = cotangent[micro_step].reshape(tok_count, features)
        fc2_weight_part = matmul(hidden_low, incoming, "tf,td->fd")
        fc2_bias_part = jnp.sum(incoming.astype(jnp.float32), axis=0)
        hidden_grad = gelu_pull(matmul(incoming, fc2_weight, "td,fd->tf"))[0].astype(jnp.bfloat16)
        fc1_weight_part = matmul(normed_two_low, hidden_grad, "td,tf->df")
        fc1_bias_part = jnp.sum(hidden_grad.astype(jnp.float32), axis=0)
        back_two = matmul(hidden_grad, fc1_weight, "tf,df->td").reshape(inputs.shape)
        middle_norm, mlp_gain_part, mlp_shift_part = second_pull(back_two)
        middle_grad = incoming.astype(jnp.float32).reshape(inputs.shape) + middle_norm
        branch_grad = middle_grad.astype(jnp.bfloat16).reshape(tok_count, features)
        out_weight_part = matmul(attended, branch_grad, "td,te->de")
        out_bias_part = jnp.sum(branch_grad.astype(jnp.float32), axis=0)
        attended_grad = matmul(branch_grad, out_weight, "te,de->td").astype(jnp.bfloat16)
        attended_grad = attended_grad.reshape(row_count, shard_len, HEADS, head_dim)
        scores_again = jnp.where(
            allowed, matmul(queries, keys_all, "rqhd,rkhd->rhqk") * score_scale, NEG
        )
        chances = jnp.exp(scores_again - log_total)
        chances_low = chances.astype(jnp.bfloat16)
        chance_grad = matmul(attended_grad, values_all, "rqhd,rkhd->rhqk")
        row_delta = jnp.sum(chances * chance_grad, axis=-1, keepdims=True)
        score_grad = (chances * (chance_grad - row_delta)).astype(jnp.bfloat16)
        query_grad = matmul(score_grad, keys_all, "rhqk,rkhd->rqhd") * score_scale
        key_terms = matmul(score_grad, queries, "rhqk,rqhd->rkhd") * score_scale
        value_terms = matmul(chances_low, attended_grad, "rhqk,rqhd->rkhd")
        key_grad, value_grad = (
            lax.psum_scatter(
                key_terms.reshape(row_count, row_len, features).astype(jnp.bfloat16),
                "seq",
                scatter_dimension=1,
                tiled=True,
            ).astype(jnp.float32),
            lax.psum_scatter(
                value_terms.reshape(row_count, row_len, features).astype(jnp.bfloat16),
                "seq",
                scatter_dimension=1,
                tiled=True,
            ).astype(jnp.float32),
        )
        projected_grad = jnp.concatenate(
            [query_grad.reshape(row_count, shard_len, features), key_grad, value_grad], axis=-1
        )
        projected_grad = projected_grad.astype(jnp.bfloat16).reshape(tok_count, 3 * features)
        qkv_weight_part = matmul(normed_low, projected_grad, "td,te->de")
        bias_sums = jnp.sum(projected_grad.astype(jnp.float32), axis=0)
        qv_bias_part = jnp.concatenate([bias_sums[:features], bias_sums[2 * features :]])
        back_one = matmul(projected_grad, qkv_weight, "te,de->td").reshape(inputs.shape)
        inputs_norm, attn_gain_part, attn_shift_part = first_pull(back_one)
        grads_list.append((middle_grad + inputs_norm).astype(jnp.bfloat16))
        pieces = (
            attn_gain_part,
            attn_shift_part,
            qkv_weight_part,
            qv_bias_part,
            out_weight_part,
            out_bias_part,
            mlp_gain_part,
            mlp_shift_part,
            fc1_weight_part,
            fc1_bias_part,
            fc2_weight_part,
            fc2_bias_part,
        )
        totals = [running + member for running, member in zip(totals, pieces)]
    (
        attn_gain_sum,
        attn_shift_sum,
        qkv_weight_sum,
        qv_bias_sum,
        out_weight_sum,
        out_bias_sum,
        mlp_gain_sum,
        mlp_shift_sum,
        fc1_weight_sum,
        fc1_bias_sum,
        fc2_weight_sum,
        fc2_bias_sum,
    ) = totals
    summed = lax.psum(
        (
            attn_gain_sum,
            attn_shift_sum,
            qkv_weight_sum,
            qv_bias_sum,
            out_weight_sum,
            out_bias_sum,
            mlp_gain_sum,
            mlp_shift_sum,
            fc1_weight_sum,
            fc1_bias_sum,
            fc2_weight_sum,
            fc2_bias_sum,
        ),
        ("dp", "seq"),
    )
    return (jnp.stack(outputs_list), jnp.stack(grads_list)) + tuple(summed)

F32 = jnp.float32
BF = jnp.bfloat16
BIG = 1e30
MESH = pl.DeviceIdType.MESH
VMEM_GRANT = 60 * 2**20
ANY = pl.BlockSpec(memory_space=pl.ANY)


def dot_rows(first_op, second_op):
    return lax.dot_general(first_op, second_op, (((1,), (1,)), ((), ())), preferred_element_type=F32)


def dot_plain(first_op, second_op):
    return lax.dot_general(first_op, second_op, (((1,), (0,)), ((), ())), preferred_element_type=F32)


def dot_tokens(first_op, second_op):
    return lax.dot_general(first_op, second_op, (((0,), (0,)), ((), ())), preferred_element_type=F32)


def once(shape, index=None):
    place = index if index is not None else (lambda *_: (0,) * len(shape))
    return pl.BlockSpec(shape, place, pipeline_mode=pl.Buffered(1))


def total_rows(array):
    return jnp.sum(array, axis=0, keepdims=True)


def unit_norm(values):
    center = values - jnp.mean(values, axis=-1, keepdims=True)
    inverse = lax.rsqrt(jnp.mean(center * center, axis=-1, keepdims=True) + EPS)
    return center * inverse, inverse


def norm_back(unit, inverse, incoming, gain):
    scaled = incoming * gain
    return inverse * (
        scaled
        - jnp.mean(scaled, axis=-1, keepdims=True)
        - unit * jnp.mean(scaled * unit, axis=-1, keepdims=True)
    )


def enter_kernel(
    tokens_ref, cot_ref, gain_ref, shift_ref, weight_ref, bias_ref,
    row_ref, normed_ref, projected_ref, cot0, cot1, cot2, cot3,
    landed, send_sem, recv_sem, local_sem, cot_sem,
):
    me, depth = lax.axis_index("seq"), lax.axis_index("dp")
    high, low = me // 2, me % 2
    peers = [me, 2 * high + 1 - low, 2 * (1 - high) + low, 3 - me]
    barrier = pltpu.get_barrier_semaphore()
    for peer in peers[1:]:
        pl.semaphore_signal(barrier, inc=1, device_id=(depth, peer), device_id_type=MESH)
    pl.semaphore_wait(barrier, 3)
    copies = [pltpu.make_async_copy(tokens_ref.at[me, 0], landed.at[0], local_sem)]
    for k in (1, 2, 3):
        copies.append(
            pltpu.make_async_remote_copy(
                src_ref=tokens_ref.at[peers[k], 0],
                dst_ref=landed.at[k],
                send_sem=send_sem.at[k - 1],
                recv_sem=recv_sem.at[k - 1],
                device_id=(depth, peers[k]),
                device_id_type=MESH,
            )
        )
    for copy in copies:
        copy.start()
    cots = [
        pltpu.make_async_copy(cot_ref.at[peers[k], 0], out, cot_sem.at[k])
        for k, out in enumerate((cot0, cot1, cot2, cot3))
    ]
    for copy in cots:
        copy.start()
    shard = landed.shape[1]
    for k in range(4):
        if k == 0:
            copies[0].wait()
        else:
            copies[k].wait_recv()
        block = landed[k]
        unit, _ = unit_norm(block.astype(F32))
        normed = (unit * gain_ref[...] + shift_ref[...]).astype(BF)
        rows = pl.ds(k * shard, shard)
        row_ref[rows, :] = block
        normed_ref[rows, :] = normed
        projected_ref[rows, :] = (dot_plain(normed, weight_ref[...]) + bias_ref[...]).astype(BF)
    for copy in cots:
        copy.wait()
    for copy in copies[1:]:
        copy.wait_send()


def enter(tokens, cotangent, gain, shift, weight, bias):
    _, _, shard, features = tokens.shape
    count, wide = 4 * shard, weight.shape[1]
    shape = jax.ShapeDtypeStruct
    vmem = pl.BlockSpec(memory_space=pltpu.VMEM)
    return pl.pallas_call(
        enter_kernel,
        in_specs=[ANY, ANY, vmem, vmem, vmem, vmem],
        out_specs=[vmem] * 7,
        out_shape=[shape((count, features), BF), shape((count, features), BF), shape((count, wide), BF)]
        + [shape((shard, features), BF)] * 4,
        scratch_shapes=[
            pltpu.VMEM((4, shard, features), BF),
            pltpu.SemaphoreType.DMA((3,)),
            pltpu.SemaphoreType.DMA((3,)),
            pltpu.SemaphoreType.DMA,
            pltpu.SemaphoreType.DMA((4,)),
        ],
        compiler_params=pltpu.CompilerParams(
            collective_id=0, has_side_effects=True, vmem_limit_bytes=VMEM_GRANT
        ),
        cost_estimate=pl.CostEstimate(flops=4 * 10**9, bytes_accessed=20 * 2**20, transcendentals=0),
        name="enter",
    )(tokens, cotangent, gain, shift, weight, bias)


def attention_forward_kernel(block, q_ref, k_ref, v_ref, miss_ref, own_ref, out_ref, lse_ref):
    lane = lax.broadcasted_iota(jnp.int32, (1, 128), 1)
    first = lane < 64
    keys, values, own = k_ref[...], v_ref[...], own_ref[...]
    ones = jnp.ones_like(values)
    keys_aug = [jnp.where(first, keys, own), jnp.where(first, own, keys)]
    values_aug = [jnp.where(first, values, ones), jnp.where(first, ones, values)]
    for step in range(q_ref.shape[0] // block):
        rows = pl.ds(step * block, block)
        queries, miss = q_ref[rows, :] * BF(0.125), miss_ref[rows, :]
        outs, logs = [], []
        for head in range(2):
            queries_aug = jnp.where(first, queries, miss) if head == 0 else jnp.where(first, miss, queries)
            scores = dot_rows(queries_aug, keys_aug[head])
            largest = jnp.max(scores, axis=1, keepdims=True)
            weights = jnp.exp(scores - largest).astype(BF)
            mixed = dot_plain(weights, values_aug[head])
            total = mixed[:, 64:65] if head == 0 else mixed[:, 0:1]
            outs.append(mixed / total)
            logs.append(largest + jnp.log(total))
        out_ref[rows, :] = jnp.where(first, outs[0], outs[1]).astype(BF)
        lse_ref[0, rows, :] = jnp.where(first, logs[0], logs[1])


def attention_forward(projected, miss, own, block=256):
    count, width = projected.shape
    pairs = width // 384
    column = lambda base: pl.BlockSpec((count, 128), lambda i: (0, i + base))
    full = pl.BlockSpec((count, 128), lambda i: (0, 0))
    return pl.pallas_call(
        functools.partial(attention_forward_kernel, block),
        grid=(pairs,),
        in_specs=[column(0), column(pairs), column(2 * pairs), full, full],
        out_specs=[column(0), pl.BlockSpec((1, count, 128), lambda i: (i, 0, 0))],
        out_shape=[
            jax.ShapeDtypeStruct((count, width // 3), BF),
            jax.ShapeDtypeStruct((pairs, count, 128), F32),
        ],
        compiler_params=pltpu.CompilerParams(vmem_limit_bytes=VMEM_GRANT),
        cost_estimate=pl.CostEstimate(flops=24 * 10**9, bytes_accessed=8 * 2**20, transcendentals=12 * 2**20),
        name="attention_forward",
    )(projected, projected, projected, miss, own)


def three_parts(column):
    high = column.astype(BF)
    rest = column - high.astype(F32)
    middle = rest.astype(BF)
    return high, middle, (rest - middle.astype(F32)).astype(BF)


def flipped(static, bits):
    total = 0
    for at, bit in enumerate(bits):
        weight = 1 << (len(bits) - 1 - at)
        total = total + weight * ((1 - bit) if static & weight else bit)
    return total


def scatter_groups(out_ref, values, bits, base=0):
    groups = 1 << len(bits)
    size = values.shape[0] // groups
    for a in range(groups):
        rows = pl.ds(pl.multiple_of(flipped(a, bits) * size, 16), size)
        out_ref[rows, base : base + values.shape[1]] = values[a * size : (a + 1) * size].astype(out_ref.dtype)


def own_bits(place_ref, order):
    me, deep = place_ref[2], place_ref[3]
    parts = {"low": [me % 2], "high": [me // 2], "deep": [deep // 2, deep % 2]}
    return [bit for name in order for bit in parts[name]]


LOW_FIRST = ("low", "high", "deep")
HIGH_FIRST = ("high", "low", "deep")
DEEP_FIRST = ("deep", "high", "low")

SECOND_FC2 = HIGH_FIRST

def segment_features(segment):
    lane = jnp.arange(128) % 64
    same = lane[None, :] == segment[:, None]
    live = (lane < 8)[None, :]
    return jnp.where(live & ~same, -BIG, 0.0).astype(BF), jnp.where(live & same, 1.0, 0.0).astype(BF)


def gelu_parts(values):
    size = jnp.abs(values)
    bell = jnp.exp(-0.5 * values * values)
    part = 1.0 / (1.0 + 0.3275911 * 0.7071067811865476 * size)
    series = part * (
        0.127414796
        + part * (-0.142248368 + part * (0.7107068705 + part * (-0.7265760135 + part * 0.5307027145)))
    )
    tail = series * bell
    below = jnp.where(values >= 0, 1.0 - tail, tail)
    return values * below, below + values * (bell * 0.3989422804014327)


def chunk_block(n2, grad, w1, bias, w2, rows, hidden_ref, hidden_grad_ref):
    pre = dot_plain(n2, w1) + bias
    back = dot_rows(grad, w2)
    hidden, slope = gelu_parts(pre)
    hidden, hidden_grad = hidden.astype(BF), (back * slope).astype(BF)
    hidden_ref[rows, :] = hidden
    hidden_grad_ref[rows, :] = hidden_grad
    return dot_plain(hidden, w2), dot_rows(hidden_grad, w1), total_rows(hidden_grad.astype(F32))


def ff_first_kernel(
    place_ref, row_ref, att_ref, g0, g1, g2, g3, out_weight_ref, out_bias_ref, gain_ref, shift_ref,
    fc2_bias_ref, w1_ref, bias_ref, w2_ref,
    n2_out, mid_out, acc_out, back_out, d1_send, d1_keep, d2_send, d2_keep, vec_ref,
    n2_s, mid_s, acc_s, back_s, hidden_s, hidden_grad_s, d1_s, d2_s, sems,
):
    step = pl.program_id(0)
    count = row_ref.shape[0]
    shard = g0.shape[0]
    blocks = [pl.ds(i * shard, shard) for i in range(count // shard)]
    early = [
        pltpu.make_async_copy(n2_s, n2_out, sems.at[0]),
        pltpu.make_async_copy(mid_s, mid_out, sems.at[1]),
    ]
    late = [
        pltpu.make_async_copy(acc_s, acc_out, sems.at[2]),
        pltpu.make_async_copy(back_s, back_out, sems.at[3]),
    ]
    grads = [
        [pltpu.make_async_copy(d1_s.at[0], d1_send, sems.at[4]), pltpu.make_async_copy(d2_s.at[0], d2_send, sems.at[5])],
        [pltpu.make_async_copy(d1_s.at[1], d1_keep, sems.at[6]), pltpu.make_async_copy(d2_s.at[1], d2_keep, sems.at[7])],
    ]

    @pl.when(step == 0)
    def _():
        vec_ref[...] = jnp.zeros_like(vec_ref)
        for rows in blocks:
            mid = row_ref[rows, :].astype(F32) + (dot_plain(att_ref[rows, :], out_weight_ref[...]) + out_bias_ref[...])
            mid_s[rows, :] = mid
            acc_s[rows, :] = mid + fc2_bias_ref[...]
            unit, _ = unit_norm(mid)
            n2_s[rows, :] = (unit * gain_ref[...] + shift_ref[...]).astype(BF)
        back_s[...] = jnp.zeros_like(back_s)
        for copy in early:
            copy.start()

    @pl.when(step > 0)
    def _():
        w1, w2, bias = w1_ref[...], w2_ref[...], bias_ref[...]
        total = jnp.zeros((1, w1.shape[1]), F32)
        for rows, grad in zip(blocks, (g0, g1, g2, g3)):
            out_part, back_part, sums = chunk_block(
                n2_s[rows, :], grad[...], w1, bias, w2, rows, hidden_s, hidden_grad_s
            )
            acc_s[rows, :] += out_part
            back_s[rows, :] += back_part
            total = total + sums
        vec_ref[pl.ds(place_ref[step - 1], 1), :] = total

        @pl.when(step == 2)
        def _():
            for copy in late:
                copy.start()

        scatter_groups(d1_s.at[step - 1], dot_tokens(n2_s[...], hidden_grad_s[...]), own_bits(place_ref, LOW_FIRST))
        grad = jnp.concatenate([g0[...], g1[...], g2[...], g3[...]], axis=0)
        scatter_groups(d2_s.at[step - 1], dot_tokens(hidden_s[...], grad), own_bits(place_ref, HIGH_FIRST))
        for k in range(2):

            @pl.when(step == k + 1)
            def _():
                for copy in grads[k]:
                    copy.start()

    @pl.when(step == 2)
    def _():
        for copy in early + late + grads[0] + grads[1]:
            copy.wait()


def ff_specs(features, size, unit, lag):
    chunk = lambda i, place: 2 * unit + place[jnp.maximum(i - lag, 0)]
    return [
        pl.BlockSpec((features, size), lambda i, place: (0, chunk(i, place))),
        pl.BlockSpec((1, size), lambda i, place: (0, chunk(i, place))),
        pl.BlockSpec((size, features), lambda i, place: (chunk(i, place), 0)),
    ]


def ff_first(place, row, attended, grads, out_weight, out_bias, gain, shift, fc1_weight, fc1_bias, fc2_weight, fc2_bias):
    count, features = row.shape
    size = fc1_weight.shape[1] // 4
    shape = jax.ShapeDtypeStruct
    wide, line = once((count, features)), once((1, features))
    return pl.pallas_call(
        ff_first_kernel,
        grid_spec=pltpu.PrefetchScalarGridSpec(
            num_scalar_prefetch=1,
            grid=(3,),
            in_specs=[wide, wide] + [once(grads[0].shape)] * 4 + [once(out_weight.shape), line, line, line, line]
            + ff_specs(features, size, 0, 1),
            out_specs=[ANY] * 8 + [once((8, size))],
            scratch_shapes=[
                pltpu.VMEM((count, features), BF),
                pltpu.VMEM((count, features), F32),
                pltpu.VMEM((count, features), F32),
                pltpu.VMEM((count, features), F32),
                pltpu.VMEM((count, size), BF),
                pltpu.VMEM((count, size), BF),
                pltpu.VMEM((2, features, size), BF),
                pltpu.VMEM((2, size, features), BF),
                pltpu.SemaphoreType.DMA((8,)),
            ],
        ),
        out_shape=[shape((count, features), BF)] + [shape((count, features), F32)] * 3
        + [shape((features, size), BF)] * 2 + [shape((size, features), BF)] * 2 + [shape((8, size), F32)],
        compiler_params=pltpu.CompilerParams(vmem_limit_bytes=VMEM_GRANT),
        cost_estimate=pl.CostEstimate(flops=17 * 10**9, bytes_accessed=24 * 2**20, transcendentals=0),
        name="ff_first",
    )(place, row, attended, *grads, out_weight, out_bias, gain, shift, fc2_bias, fc1_weight, fc1_bias, fc2_weight)


def ff_second_kernel(
    place_ref, n2_ref, mid_ref, acc_ref, back_ref, att_ref, g0, g1, g2, g3, out_weight_ref, gain_ref,
    w1_ref, bias_ref, w2_ref,
    out0, out1, out2, out3, branch_out, att_grad_out, d1_send, d1_keep, d2_send, d2_keep, do_send, do_keep, vec_ref,
    acc_s, back_s, hidden_s, hidden_grad_s, d1_s, d2_s, do_s, result_s, branch_s, att_grad_s, sems,
):
    step = pl.program_id(0)
    count = n2_ref.shape[0]
    shard = g0.shape[0]
    half = do_s.shape[2]
    blocks = [pl.ds(i * shard, shard) for i in range(count // shard)]
    grad_refs = (g0, g1, g2, g3)
    grads = [
        [pltpu.make_async_copy(d1_s.at[0], d1_send, sems.at[0]), pltpu.make_async_copy(d2_s.at[0], d2_send, sems.at[1])],
        [
            pltpu.make_async_copy(d1_s.at[1], d1_keep, sems.at[2]),
            pltpu.make_async_copy(d2_s.at[1], d2_keep, sems.at[3]),
            pltpu.make_async_copy(do_s.at[0], do_send, sems.at[4]),
            pltpu.make_async_copy(do_s.at[1], do_keep, sems.at[5]),
        ],
    ]
    rest = [
        pltpu.make_async_copy(result_s.at[rows], out, sems.at[6 + k])
        for k, (rows, out) in enumerate(zip(blocks, (out0, out1, out2, out3)))
    ] + [
        pltpu.make_async_copy(branch_s, branch_out, sems.at[10]),
        pltpu.make_async_copy(att_grad_s, att_grad_out, sems.at[11]),
    ]

    def weight_grads(slot):
        scatter_groups(d1_s.at[slot], dot_tokens(n2_ref[...], hidden_grad_s[...]), own_bits(place_ref, LOW_FIRST))
        grad = jnp.concatenate([ref[...] for ref in grad_refs], axis=0)
        scatter_groups(d2_s.at[slot], dot_tokens(hidden_s[...], grad), own_bits(place_ref, SECOND_FC2))

    @pl.when(step == 0)
    def _():
        vec_ref[...] = jnp.zeros_like(vec_ref)
        w1, w2, bias = w1_ref[...], w2_ref[...], bias_ref[...]
        total = jnp.zeros((1, w1.shape[1]), F32)
        for rows, grad in zip(blocks, grad_refs):
            out_part, back_part, sums = chunk_block(
                n2_ref[rows, :], grad[...], w1, bias, w2, rows, hidden_s, hidden_grad_s
            )
            acc_s[rows, :] = acc_ref[rows, :] + out_part
            back_s[rows, :] = back_ref[rows, :] + back_part
            total = total + sums
        vec_ref[pl.ds(place_ref[0], 1), :] = total
        weight_grads(0)
        for copy in grads[0]:
            copy.start()

    @pl.when(step == 1)
    def _():
        w1, w2, bias = w1_ref[...], w2_ref[...], bias_ref[...]
        total = jnp.zeros((1, w1.shape[1]), F32)
        gain_sum, shift_sum, branch_sum, grad_sum = [jnp.zeros((1, n2_ref.shape[1]), F32) for _ in range(4)]
        for rows, grad_ref in zip(blocks, grad_refs):
            grad = grad_ref[...]
            out_part, back_part, sums = chunk_block(
                n2_ref[rows, :], grad, w1, bias, w2, rows, hidden_s, hidden_grad_s
            )
            total = total + sums
            result_s[rows, :] = (acc_s[rows, :] + out_part).astype(BF)
            back = back_s[rows, :] + back_part
            unit, inverse = unit_norm(mid_ref[rows, :])
            gain_sum = gain_sum + total_rows(back * unit)
            shift_sum = shift_sum + total_rows(back)
            wide = grad.astype(F32)
            grad_sum = grad_sum + total_rows(wide)
            branch = (wide + norm_back(unit, inverse, back, gain_ref[...])).astype(BF)
            branch_s[rows, :] = branch
            branch_sum = branch_sum + total_rows(branch.astype(F32))
            att_grad_s[rows, :] = dot_rows(branch, out_weight_ref[...]).astype(BF)
        vec_ref[pl.ds(place_ref[1], 1), :] = total
        for at, sums in enumerate((gain_sum, shift_sum, branch_sum, grad_sum)):
            vec_ref[at + 2 : at + 3, :] = sums
        for copy in rest:
            copy.start()
        weight_grads(1)
        for slot in range(2):
            columns = pl.ds(pl.multiple_of(place_ref[slot] * half, 128), half)
            scatter_groups(do_s.at[slot], dot_tokens(att_ref[...], branch_s[:, columns]), own_bits(place_ref, LOW_FIRST))
        for copy in grads[1]:
            copy.start()
        for copy in rest + grads[0] + grads[1]:
            copy.wait()


def ff_second(place, n2, mid, acc, back, attended, grads, out_weight, gain, fc1_weight, fc1_bias, fc2_weight):
    count, features = n2.shape
    size = fc1_weight.shape[1] // 4
    half = features // 2
    shape = jax.ShapeDtypeStruct
    wide, line = once((count, features)), once((1, features))
    return pl.pallas_call(
        ff_second_kernel,
        grid_spec=pltpu.PrefetchScalarGridSpec(
            num_scalar_prefetch=1,
            grid=(2,),
            in_specs=[wide] * 5 + [once(grads[0].shape)] * 4 + [once(out_weight.shape), line]
            + ff_specs(features, size, 1, 0),
            out_specs=[ANY] * 12 + [once((8, size))],
            scratch_shapes=[
                pltpu.VMEM((count, features), F32),
                pltpu.VMEM((count, features), F32),
                pltpu.VMEM((count, size), BF),
                pltpu.VMEM((count, size), BF),
                pltpu.VMEM((2, features, size), BF),
                pltpu.VMEM((2, size, features), BF),
                pltpu.VMEM((2, features, half), BF),
                pltpu.VMEM((count, features), BF),
                pltpu.VMEM((count, features), BF),
                pltpu.VMEM((count, features), BF),
                pltpu.SemaphoreType.DMA((12,)),
            ],
        ),
        out_shape=[shape(grads[0].shape, BF)] * 4 + [shape((count, features), BF)] * 2
        + [shape((features, size), BF)] * 2 + [shape((size, features), BF)] * 2
        + [shape((features, half), BF)] * 2 + [shape((8, size), F32)],
        compiler_params=pltpu.CompilerParams(vmem_limit_bytes=VMEM_GRANT),
        cost_estimate=pl.CostEstimate(flops=18 * 10**9, bytes_accessed=32 * 2**20, transcendentals=0),
        name="ff_second",
    )(place, n2, mid, acc, back, attended, *grads, out_weight, gain, fc1_weight, fc1_bias, fc2_weight)


def peer_ids():
    me, depth = lax.axis_index("seq"), lax.axis_index("dp")
    high, low = me // 2, me % 2
    core, deep = depth % 2, depth // 2
    upper, lower = deep // 2, deep % 2
    return {
        ("core", 1): (2 * deep + 1 - core, me),
        ("low", 1): (depth, 2 * high + 1 - low),
        ("high", 1): (depth, 2 * (1 - high) + low),
        ("both", 1): (depth, 3 - me),
        ("deep", 1): (2 * (2 * upper + 1 - lower) + core, me),
        ("deep", 2): (2 * (2 * (1 - upper) + lower) + core, me),
        ("deep", 3): (2 * (3 - deep) + core, me),
    }


FAN = {"low": 2, "high": 2, "deep": 4}
SEMS = 12


class Sum:
    def __init__(self, order, send, keep, core_buf, bufs, own, other, send_sems, recv_sems, local_sem):
        self.order, self.send, self.keep, self.core_buf, self.bufs = order, send, keep, core_buf, bufs
        self.own, self.other = own, other
        self.send_sems, self.recv_sems, self.local_sem = send_sems, recv_sems, local_sem
        rows = keep.shape[0]
        self.sizes = []
        for name in order:
            rows //= FAN[name]
            self.sizes.append(rows)
        self.peers = peer_ids()

    def stage(self, at):
        if at == 0:
            moves = [(self.send, self.core_buf, ("core", 1))]
        elif at <= 3:
            name, size, buf = self.order[at - 1], self.sizes[at - 1], self.bufs[at - 1]
            moves = [
                (self.keep.at[pl.ds(k * size, size)], buf.at[pl.ds((k - 1) * size, size)], (name, k))
                for k in range(1, FAN[name])
            ]
        elif at <= 6:
            name, size = self.order[6 - at], self.sizes[6 - at]
            src = self.keep if at == 4 else self.own
            moves = [
                (src.at[pl.ds(0, size)], self.own.at[pl.ds(k * size, size)], (name, k)) for k in range(1, FAN[name])
            ]
        else:
            moves = [(self.own, self.other, ("core", 1))]
        counts = [1] + [FAN[name] - 1 for name in self.order]
        base = sum((counts + counts[:0:-1])[:at])
        return [
            pltpu.make_async_remote_copy(
                src_ref=src, dst_ref=dst, send_sem=self.send_sems.at[base + k], recv_sem=self.recv_sems.at[base + k],
                device_id=self.peers[peer], device_id_type=MESH,
            )
            for k, (src, dst, peer) in enumerate(moves)
        ]

    def local(self):
        rows = pl.ds(0, self.sizes[2])
        return pltpu.make_async_copy(self.keep.at[rows], self.own.at[rows], self.local_sem)

    def arrived(self, stage):
        for copy in self.stage(stage):
            copy.wait_recv()

    def add(self, start, size, sources):
        rows = pl.ds(start, size)
        total = self.keep[rows, :].astype(F32)
        for buf, offset in sources:
            total = total + buf[pl.ds(offset + start, size), :].astype(F32)
        self.keep[rows, :] = total.astype(self.keep.dtype)

    def tick(self, at):
        if at > 0:
            self.arrived(at - 1)
        if 1 <= at <= 4:
            if at == 1:
                sources = [(self.core_buf, 0)]
            else:
                name, size, buf = self.order[at - 2], self.sizes[at - 2], self.bufs[at - 2]
                sources = [(buf, k * size) for k in range(FAN[name] - 1)]
            held = self.keep.shape[0] if at == 1 else self.sizes[at - 2]
            if at <= 3:
                size = self.sizes[at - 1]
                self.add(size, held - size, sources)
                for copy in self.stage(at):
                    copy.start()
                self.add(0, size, sources)
                return
            self.add(0, held, sources)
            self.local().start()
        if at == 5:
            self.local().wait()
        if at <= 7:
            for copy in self.stage(at):
                copy.start()
        else:
            for stage in range(8):
                for copy in self.stage(stage):
                    copy.wait_send()


FC = (0, 1, 2, 3)
OUT = 4
QKV = (5, 6, 7)
PLAN = {
    0: [(0, 0), (1, 0), (2, 0), (3, 0), (4, 0)],
    1: [(0, 1), (1, 1)],
    2: [(2, 1), (3, 1), (5, 0)],
    3: [(0, 2), (1, 2), (4, 1), (5, 1)],
    4: [(2, 2), (3, 2), (0, 3), (1, 3), (6, 0)],
    5: [(0, 4), (1, 4), (2, 3), (3, 3), (4, 2), (5, 2)],
    6: [(7, 0), (0, 5), (1, 5), (2, 4), (3, 4), (4, 3), (5, 3), (6, 1)],
    7: [
        (7, 1), (0, 6), (1, 6), (2, 5), (3, 5), (6, 2), (4, 4), (5, 4), (7, 2), (2, 6), (3, 6), (0, 7), (1, 7),
        (6, 3), (7, 3), (4, 5), (5, 5), (6, 4), (7, 4), (2, 7), (3, 7), (4, 6), (5, 6), (6, 5), (7, 5),
        (4, 7), (5, 7), (6, 6), (7, 6), (6, 7), (7, 7),
        (0, 8), (1, 8), (2, 8), (3, 8), (4, 8), (5, 8), (6, 8), (7, 8),
    ],
}
ORDERS = (LOW_FIRST, HIGH_FIRST, LOW_FIRST, SECOND_FC2, LOW_FIRST, LOW_FIRST, HIGH_FIRST, LOW_FIRST)


def three_parts(column):
    high = column.astype(BF)
    rest = column - high.astype(F32)
    middle = rest.astype(BF)
    return high, middle, (rest - middle.astype(F32)).astype(BF)


def pair_backward(refs, outs, dk_acc, dv_acc, pair, block):
    q_ref, k_ref, v_ref, att_ref, grad_ref, lse_ref, miss_ref, own_ref = refs
    lane = lax.broadcasted_iota(jnp.int32, (1, 128), 1)
    first = lane < 64
    half = lane % 64
    keys, values, own = k_ref[...], v_ref[...], own_ref[...]
    unit = jnp.where((half >= 8) & (half < 11), 1.0, 0.0).astype(BF)
    own = own + unit
    unit_rows = jnp.broadcast_to(unit, values.shape)
    keys_aug = [jnp.where(first, keys, own), jnp.where(first, own, keys)]
    values_aug = [jnp.where(first, values, unit_rows), jnp.where(first, unit_rows, values)]
    keys_only = [jnp.where(first, keys, BF(0)), jnp.where(first, BF(0), keys)]
    dk_acc[...] = jnp.zeros_like(dk_acc)
    dv_acc[...] = jnp.zeros_like(dv_acc)
    columns = pl.ds(pl.multiple_of(pair * 128, 128), 128)

    def spread(column):
        high, middle, low = [part.astype(F32) for part in three_parts(-column)]
        wide = jnp.where(half == 8, high, jnp.where(half == 9, middle, jnp.where(half == 10, low, 0.0)))
        return wide.astype(BF)

    def body(step, carry):
        rows = pl.ds(pl.multiple_of(step * block, block), block)
        queries, miss, grad = q_ref[rows, :] * BF(0.125), miss_ref[rows, :], grad_ref[rows, :]
        both = att_ref[rows, :].astype(F32) * grad.astype(F32)
        logs = lse_ref[0, rows, :]
        queries_t, grad_t = queries.T, grad.T
        dq = jnp.zeros((block, 128), F32)
        for head in range(2):
            mine = first if head == 0 else jnp.logical_not(first)
            span = pl.ds(64 * head, 64)
            delta = jnp.sum(jnp.where(mine, both, 0.0), axis=1, keepdims=True)
            total = logs[:, 0:1] if head == 0 else logs[:, 64:65]
            queries_aug = jnp.where(mine, queries, spread(total) + miss)
            grad_aug = jnp.where(mine, grad, spread(delta))
            probs = jnp.exp(dot_rows(queries_aug, keys_aug[head]))
            score_grad = (probs * dot_rows(grad_aug, values_aug[head])).astype(BF)
            dq = dq + dot_plain(score_grad, keys_only[head])
            dk_acc[span, :] += dot_plain(queries_t[64 * head : 64 * head + 64], score_grad)
            dv_acc[span, :] += dot_plain(grad_t[64 * head : 64 * head + 64], probs.astype(BF))
        outs[0][rows, columns] = (dq * 0.125).astype(BF)
        return carry

    lax.fori_loop(0, q_ref.shape[0] // block, body, 0)
    outs[1][:, columns] = dk_acc[...].T.astype(BF)
    outs[2][:, columns] = dv_acc[...].T.astype(BF)


def backward_kernel(*refs):
    (
        q_ref, k_ref, v_ref, att_ref, grad_ref, lse_ref, miss_ref, own_ref, normed_ref,
        weight_ref, row_ref, branch_ref, gain_ref, vec_one_ref, vec_two_ref,
    ) = refs[:15]
    results = refs[15:19]
    sends, keeps = refs[19:24], refs[24:29]
    outs = refs[29:]
    block_out, tokens_out, vec_out = outs[:3]
    owns, others = outs[3:11], outs[11:19]
    (
        dq_s, dk_s, dv_s, dk_acc, dv_acc, qkv_send, qkv_keep,
        keep_s, core_s, buf0, buf1, buf2, keep_o, core_o, buf0_o, buf1_o, buf2_o,
        core_q, buf0_q, buf1_q, buf2_q, own_result, grad_s, vec_s, vec_got,
        send_sems, recv_sems, local_sems, load_sems, side_send, side_recv, vec_send, vec_recv,
    ) = outs[19:]
    step = pl.program_id(0)
    me, depth = lax.axis_index("seq"), lax.axis_index("dp")
    core, deep = depth % 2, depth // 2
    peers = peer_ids()
    shard = results[0].shape[0]
    features = row_ref.shape[1]

    def job(n):
        sems = send_sems.at[n], recv_sems.at[n], local_sems.at[n]
        if n < 4:
            parts = sends[n], keep_s.at[n], core_s.at[n], [buf0.at[n], buf1.at[n], buf2.at[n]]
        elif n == 4:
            parts = sends[4], keep_o, core_o, [buf0_o, buf1_o, buf2_o]
        else:
            g = n - 5
            parts = qkv_send.at[g], qkv_keep.at[g], core_q.at[g], [buf0_q.at[g], buf1_q.at[g], buf2_q.at[g]]
        return Sum(ORDERS[n], *parts, owns[n], others[n], *sems)

    def load(n):
        if n == 5:
            return pltpu.make_async_copy(results[0], own_result, load_sems.at[5])
        return pltpu.make_async_copy(keeps[n], keep_s.at[n] if n < 4 else keep_o, load_sems.at[n])

    def store():
        return pltpu.make_async_copy(own_result, block_out.at[me, 0], load_sems.at[5])

    kinds = [("low", 1), ("high", 1), ("both", 1)]

    def spread_rows(number, pieces, out):
        return [
            pltpu.make_async_remote_copy(
                src_ref=piece, dst_ref=out.at[me, 0], send_sem=side_send.at[number, k], recv_sem=side_recv.at[number, k],
                device_id=peers[kinds[k]], device_id_type=MESH,
            )
            for k, piece in enumerate(pieces)
        ]

    def block_copies():
        return spread_rows(0, results[1:], block_out)

    def token_copies():
        return spread_rows(1, [grad_s.at[k] for k in (1, 2, 3)], tokens_out)

    def token_store():
        return pltpu.make_async_copy(grad_s.at[0], tokens_out.at[me, 0], load_sems.at[6])

    def vec_copies(stage, names):
        return [
            pltpu.make_async_remote_copy(
                src_ref=vec_s.at[stage], dst_ref=vec_got.at[stage, k],
                send_sem=vec_send.at[stage, k], recv_sem=vec_recv.at[stage, k],
                device_id=peers[name], device_id_type=MESH,
            )
            for k, name in enumerate(names)
        ]

    vec_names = [[("core", 1)], kinds, [("deep", 1), ("deep", 2), ("deep", 3)]]

    def vec_stage(stage):
        return vec_copies(stage, vec_names[stage])

    @pl.when(step == 0)
    def _():
        barrier = pltpu.get_barrier_semaphore()
        for peer in peers.values():
            pl.semaphore_signal(barrier, inc=1, device_id=peer, device_id_type=MESH)
        for n in range(6):
            load(n).start()
        pl.semaphore_wait(barrier, len(peers))

    for at, ticks in PLAN.items():

        @pl.when(step == at)
        def _():
            for n, tick in ticks:
                if n < 5 and tick == 1:
                    load(n).wait()
                if at < 7:
                    job(n).tick(tick)

    @pl.when(step == 2)
    def _():
        load(5).wait()
        store().start()

    @pl.when(step == 4)
    def _():
        for copy in block_copies():
            copy.start()

    @pl.when(step < 6)
    def _():
        pair = 2 * (step // 2) + (core + 1 + step % 2) % 2
        pair_backward(
            (q_ref, k_ref, v_ref, att_ref, grad_ref, lse_ref, miss_ref, own_ref),
            (dq_s, dk_s, dv_s), dk_acc, dv_acc, pair, 256,
        )

    for at in range(6):

        @pl.when(step == at)
        def _():
            group, keeping = at // 2, at % 2
            pair = 2 * group + (core + 1 + keeping) % 2
            columns = pl.ds(pl.multiple_of(pair * 128, 128), 128)
            target = (qkv_keep if keeping else qkv_send).at[group]
            place = {"low": [me % 2], "high": [me // 2], "deep": [deep // 2, deep % 2]}
            bits = [bit for name in ORDERS[5 + group] for bit in place[name]]
            for index, part in enumerate((dq_s, dk_s, dv_s)):
                grads = part[:, columns]
                scatter_groups(target, dot_tokens(normed_ref[...], grads), bits, 128 * index)
                if index != 1:
                    vec_out[2 + index // 2 : 3 + index // 2, columns] = total_rows(grads.astype(F32))

    @pl.when(step == 6)
    def _():
        gain_sum, shift_sum = jnp.zeros((1, features), F32), jnp.zeros((1, features), F32)
        for k in (3, 1, 2, 0):
            rows = pl.ds(k * shard, shard)
            back = dot_rows(dq_s[rows, :], weight_ref[:, :features])
            back = back + dot_rows(dk_s[rows, :], weight_ref[:, features : 2 * features])
            back = back + dot_rows(dv_s[rows, :], weight_ref[:, 2 * features :])
            unit, inverse = unit_norm(row_ref[rows, :].astype(F32))
            gain_sum = gain_sum + total_rows(back * unit)
            shift_sum = shift_sum + total_rows(back)
            grad_s[k] = (branch_ref[rows, :].astype(F32) + norm_back(unit, inverse, back, gain_ref[...])).astype(BF)
            if k:
                pltpu.make_async_remote_copy(
                    src_ref=grad_s.at[k], dst_ref=tokens_out.at[me, 0],
                    send_sem=side_send.at[1, k - 1], recv_sem=side_recv.at[1, k - 1],
                    device_id=peers[kinds[k - 1]], device_id_type=MESH,
                ).start()
            else:
                token_store().start()
        vec_s[0, 0:1, :] = gain_sum
        vec_s[0, 1:2, :] = shift_sum
        vec_s[0, 2:4, :] = vec_out[2:4, :]
        vec_s[0, 4:6, :] = vec_one_ref[0:2, :]
        vec_s[0, 6:12, :] = vec_two_ref[0:6, :]
        vec_s[0, 12:16, :] = jnp.zeros((4, features), F32)
        vec_stage(0)[0].start()

    @pl.when(step == 7)
    def _():
        def vec_step(stage):
            for copy in vec_stage(stage):
                copy.wait_recv()
            total = vec_s[stage]
            for k in range(len(vec_names[stage])):
                total = total + vec_got[stage, k]
            if stage == 2:
                vec_out[...] = total
            else:
                vec_s[stage + 1] = total
                for copy in vec_stage(stage + 1):
                    copy.start()

        for index, (n, tick) in enumerate(PLAN[7]):
            if index in (1, 5, 9):
                vec_step((index - 1) // 4)
            job(n).tick(tick)
        store().wait()
        token_store().wait()
        for copy in block_copies() + token_copies():
            copy.wait()
        for stage in range(3):
            for copy in vec_stage(stage):
                copy.wait_send()


def backward(
    projected, attended, attended_grad, logs, miss, own, normed, qkv_weight, row, branch, gain, vec_one, vec_two,
    results, sends, keeps,
):
    count, width = projected.shape
    features = width // 3
    pairs = width // 384
    half = features // 2
    shard = count // 4

    def pair(i):
        at = jnp.minimum(i, 5)
        return 2 * (at // 2) + (lax.axis_index("dp") % 2 + 1 + at % 2) % 2

    column = lambda base: pl.BlockSpec((count, 128), lambda i: (0, pair(i) + base))
    shape = jax.ShapeDtypeStruct
    wide = once((count, features))
    full = once((count, 128))
    sizes = [sends[0].shape] * 4 + [(features, half)] * 4
    buffers = lambda rows, cols, order: [rows // 2, rows // 4, 3 * (rows // 16)]
    vmem = pltpu.VMEM
    dma = pltpu.SemaphoreType.DMA
    return pl.pallas_call(
        backward_kernel,
        grid=(8,),
        in_specs=[
            column(0), column(pairs), column(2 * pairs), column(0), column(0),
            pl.BlockSpec((1, count, 128), lambda i: (pair(i), 0, 0)),
            full, full, wide, once(qkv_weight.shape), wide, wide, once((1, features)), once((8, features)),
            once((8, features)),
        ]
        + [ANY] * 14,
        out_specs=[ANY, ANY, once((16, features))] + [ANY] * 16,
        out_shape=[shape((4, 1, shard, features), BF)] * 2 + [shape((16, features), F32)]
        + [shape(size, BF) for size in sizes] * 2,
        scratch_shapes=[vmem((count, features), BF)] * 3
        + [vmem((128, count), F32)] * 2
        + [vmem((3, features, half), BF)] * 2
        + [vmem((4, features, features), BF)] * 2
        + [vmem((4, rows, features), BF) for rows in (features // 2, features // 4, 3 * features // 16)]
        + [vmem((features, half), BF)] * 2
        + [vmem((rows, half), BF) for rows in (features // 2, features // 4, 3 * features // 16)]
        + [vmem((3, features, half), BF)]
        + [vmem((3, rows, half), BF) for rows in (features // 2, features // 4, 3 * features // 16)]
        + [
            vmem((shard, features), BF), vmem((4, shard, features), BF),
            vmem((3, 16, features), F32), vmem((3, 3, 16, features), F32),
            dma((8, SEMS)), dma((8, SEMS)), dma((8,)), dma((7,)), dma((2, 3)), dma((2, 3)), dma((3, 3)), dma((3, 3)),
        ],
        compiler_params=pltpu.CompilerParams(
            collective_id=1, has_side_effects=True, vmem_limit_bytes=VMEM_GRANT
        ),
        cost_estimate=pl.CostEstimate(flops=60 * 10**9, bytes_accessed=60 * 2**20, transcendentals=12 * 2**20),
        name="backward",
    )(
        projected, projected, projected, attended, attended_grad, logs, miss, own, normed, qkv_weight, row, branch,
        gain, vec_one, vec_two, *results, *sends, *keeps,
    )


def ordered(ref, which, groups=4):
    size = ref.shape[0] // groups
    return jnp.concatenate(
        [ref[pl.ds(pl.multiple_of((a ^ which) * size, 16), size), :] for a in range(groups)], axis=0
    )


def assemble_ff_kernel(place_ref, *refs):
    ins, (d1_ref, d2_ref) = refs[:8], refs[8:]
    core, deep = place_ref[1], place_ref[3]
    size = ins[0].shape[1]
    for unit in range(2):
        for side in range(2):
            home = core if side == 0 else 1 - core
            columns = pl.ds(pl.multiple_of((2 * unit + home) * size, 128), size)
            d1_ref[:, columns] = ordered(ins[4 * unit + side], deep).astype(F32)
            d2_ref[unit, home] = ordered(ins[4 * unit + 2 + side], deep).astype(F32)


def assemble_ff(place, parts):
    features, size = parts[0].shape
    block = features // 4
    shape = jax.ShapeDtypeStruct
    first = pl.BlockSpec((block, size), lambda i, place: (i ^ place[4], 0))
    second = pl.BlockSpec((block, size), lambda i, place: (i ^ place[2], 0))
    d1, d2 = pl.pallas_call(
        assemble_ff_kernel,
        grid_spec=pltpu.PrefetchScalarGridSpec(
            num_scalar_prefetch=1,
            grid=(4,),
            in_specs=[first, first, second, second] * 2,
            out_specs=[
                pl.BlockSpec((block, 4 * size), lambda i, place: (i, 0)),
                pl.BlockSpec((2, 2, block, size), lambda i, place: (0, 0, i, 0)),
            ],
        ),
        out_shape=[shape((features, 4 * size), F32), shape((2, 2, features, size), F32)],
        compiler_params=pltpu.CompilerParams(vmem_limit_bytes=VMEM_GRANT),
        cost_estimate=pl.CostEstimate(flops=0, bytes_accessed=30 * 2**20, transcendentals=0),
        name="assemble_ff",
    )(place, *parts)
    return d1, d2.reshape(4 * features, size)


def assemble_qkv_kernel(place_ref, *refs):
    ins, (out_ref, qkv_ref) = refs[:8], refs[8:]
    core, deep = place_ref[1], place_ref[3]
    features = out_ref.shape[1]
    for side in range(2):
        home = core if side == 0 else 1 - core
        half = features // 2
        out_ref[:, pl.ds(pl.multiple_of(home * half, 128), half)] = ordered(ins[side], deep).astype(F32)
        for group in range(3):
            values = ordered(ins[2 + 2 * group + side], deep).astype(F32)
            for part in range(3):
                at = part * features + (2 * group + home) * 128
                qkv_ref[:, pl.ds(pl.multiple_of(at, 128), 128)] = values[:, part * 128 : (part + 1) * 128]


def assemble_qkv(place, parts):
    features, half = parts[0].shape
    block = features // 4
    shape = jax.ShapeDtypeStruct
    spec = lambda order: pl.BlockSpec(
        (block, half), lambda i, place: (i ^ place[4 if order == LOW_FIRST else 2], 0)
    )
    return pl.pallas_call(
        assemble_qkv_kernel,
        grid_spec=pltpu.PrefetchScalarGridSpec(
            num_scalar_prefetch=1,
            grid=(4,),
            in_specs=[spec(order) for order in ORDERS[4:] for _ in range(2)],
            out_specs=[
                pl.BlockSpec((block, 2 * half), lambda i, place: (i, 0)),
                pl.BlockSpec((block, 6 * half), lambda i, place: (i, 0)),
            ],
        ),
        out_shape=[shape((features, 2 * half), F32), shape((features, 6 * half), F32)],
        compiler_params=pltpu.CompilerParams(vmem_limit_bytes=VMEM_GRANT),
        cost_estimate=pl.CostEstimate(flops=0, bytes_accessed=15 * 2**20, transcendentals=0),
        name="assemble_qkv",
    )(place, *parts)


def swap(array, axis, bit):
    count = lax.axis_size(axis)
    return lax.ppermute(array, axis, [(i, i ^ bit) for i in range(count)])


def fast_shards(
    tokens, image_lengths, cotangent, attn_gain, attn_shift, qkv_weight, qv_bias, out_weight,
    out_bias, mlp_gain, mlp_shift, fc1_weight, fc1_bias, fc2_weight, fc2_bias,
):
    shard_len, features = tokens.shape[2:]
    parties = lax.axis_size("seq")
    row_len = shard_len * parties
    images = image_lengths.shape[2] - 1
    me, depth = lax.axis_index("seq"), lax.axis_index("dp")
    core, deep = depth % 2, depth // 2
    turned = (me % 2) * 2 + me // 2
    place = jnp.stack([1 - core, core, me, deep, turned]).astype(jnp.int32)
    line = lambda array: array.reshape(1, -1)

    full_bias = jnp.concatenate([qv_bias[:features], jnp.zeros((features,), F32), qv_bias[features:]])
    row, normed, projected, *cots = enter(
        tokens, cotangent, line(attn_gain), line(attn_shift), qkv_weight, line(full_bias)
    )
    seg_row = segment_ids(lax.dynamic_index_in_dim(image_lengths, me, 0, keepdims=False), row_len, images)
    seg_row = seg_row.reshape(parties, shard_len)
    segment = jnp.concatenate([seg_row[me ^ k] for k in range(parties)], axis=0)
    miss, own = segment_features(segment)
    attended, logs = attention_forward(projected, miss, own)
    grads = [cots[0]] + [swap(cots[k], "seq", k) for k in (1, 2, 3)]

    n2, mid, acc, back, d1_send, d1_keep, d2_send, d2_keep, vec_first = ff_first(
        place, row, attended, grads, out_weight, line(out_bias), line(mlp_gain), line(mlp_shift),
        fc1_weight, line(fc1_bias), fc2_weight, line(fc2_bias),
    )
    sends, keeps = [d1_send, d2_send], [d1_keep, d2_keep]
    *results, branch, attended_grad, d1_send, d1_keep, d2_send, d2_keep, do_send, do_keep, vec_second = ff_second(
        place, n2, mid, acc, back, attended, grads, out_weight, line(mlp_gain), fc1_weight, line(fc1_bias), fc2_weight
    )
    sends, keeps = sends + [d1_send, d2_send, do_send], keeps + [d1_keep, d2_keep, do_keep]
    block_out, tokens_grad, vector, *summed = backward(
        projected, attended, attended_grad, logs, miss, own, normed, qkv_weight, row, branch, line(attn_gain),
        vec_first, vec_second, results, sends, keeps,
    )
    paired = [part for n in range(8) for part in (summed[n], summed[8 + n])]
    fc1_grad, fc2_grad = assemble_ff(place, paired[:8])
    out_grad, qkv_grad = assemble_qkv(place, paired[8:])
    return (
        block_out, tokens_grad, vector[0], vector[1], qkv_grad, vector[2:4].reshape(-1), out_grad, vector[10],
        vector[8], vector[9], fc1_grad, vector[4:8].reshape(-1), fc2_grad, vector[11],
    )


def shards(tokens, *rest):
    micro_count, row_count, shard_len, features = tokens.shape
    whole_rows = micro_count == 4 and row_count == 1 and shard_len % 128 == 0
    sizes = lax.axis_size("dp") == 8 and lax.axis_size("seq") == 4
    if sizes and whole_rows and features == 64 * HEADS and features % 768 == 0:
        return fast_shards(tokens, *rest)
    return general_shards(tokens, *rest)


def solution(mesh):
    placed = (
        P(None, "dp", "seq", None),
        P(None, "dp", None),
        P(None, "dp", "seq", None),
        P(),
        P(),
        P(),
        P(),
        P(),
        P(),
        P(),
        P(),
        P(),
        P(),
        P(),
        P(),
    )
    return jax.shard_map(
        shards,
        mesh=mesh,
        in_specs=placed,
        out_specs=(
            P(None, "dp", "seq", None),
            P(None, "dp", "seq", None),
            P(),
            P(),
            P(),
            P(),
            P(),
            P(),
            P(),
            P(),
            P(),
            P(),
            P(),
            P(),
        ),
        check_vma=False,
    )
```

```python
import functools

import jax
import jax.numpy as jnp
from jax import lax
from jax.experimental import pallas as pl
from jax.experimental.pallas import tpu as pltpu
from jax.sharding import PartitionSpec as P

HEADS = 12


EPS = 1e-06
NEG = -1e30


def layer_norm(values, scale_row, shift_row):
    center = values - jnp.mean(values, axis=-1, keepdims=True)
    spread = jnp.mean(center * center, axis=-1, keepdims=True)
    return center * lax.rsqrt(spread + EPS) * scale_row + shift_row


def gelu_exact(values):
    return jax.nn.gelu(values, approximate=False)


def segment_ids(lengths, row_len, images):
    positions = jnp.arange(row_len, dtype=jnp.int32)
    ends = jnp.cumsum(lengths, axis=-1) + 2 * images
    patches = jnp.sum((positions[:, None] >= ends[..., None, :]).astype(jnp.int32), axis=-1)
    return jnp.where(positions < 2 * images, positions // 2, patches)


def matmul(first_op, second_op, pattern):
    return jnp.einsum(pattern, first_op, second_op, preferred_element_type=jnp.float32)


def general_shards(
    tokens,
    image_lengths,
    cotangent,
    attn_gain,
    attn_shift,
    qkv_weight,
    qv_bias,
    out_weight,
    out_bias,
    mlp_gain,
    mlp_shift,
    fc1_weight,
    fc1_bias,
    fc2_weight,
    fc2_bias,
):
    micro_count, row_count, shard_len, features = tokens.shape
    row_len = shard_len * lax.axis_size("seq")
    images = image_lengths.shape[2] - 1
    head_dim = features // HEADS
    score_scale = head_dim ** (-0.5)
    offset = lax.axis_index("seq") * shard_len
    tok_count = row_count * shard_len
    zero_keys = jnp.zeros((features,), jnp.float32)
    full_bias = jnp.concatenate([qv_bias[:features], zero_keys, qv_bias[features:]])
    totals = [
        jnp.zeros(weight.shape, jnp.float32)
        for weight in (
            attn_gain,
            attn_shift,
            qkv_weight,
            qv_bias,
            out_weight,
            out_bias,
            mlp_gain,
            mlp_shift,
            fc1_weight,
            fc1_bias,
            fc2_weight,
            fc2_bias,
        )
    ]
    outputs_list = []
    grads_list = []
    for micro_step in range(micro_count):
        inputs = tokens[micro_step].astype(jnp.float32)
        seg_all = segment_ids(image_lengths[micro_step], row_len, images)
        seg_here = lax.dynamic_slice_in_dim(seg_all, offset, shard_len, 1)
        allowed = seg_here[:, None, :, None] == seg_all[:, None, None, :]
        normed, first_pull = jax.vjp(layer_norm, inputs, attn_gain, attn_shift)
        normed_low = normed.astype(jnp.bfloat16).reshape(tok_count, features)
        projected = (matmul(normed_low, qkv_weight, "td,de->te") + full_bias).astype(jnp.bfloat16)
        projected = projected.reshape(row_count, shard_len, 3 * features)
        queries = projected[:, :, :features].reshape(row_count, shard_len, HEADS, head_dim)
        keys_all, values_all = (
            lax.all_gather(projected[:, :, features : 2 * features], "seq", axis=1, tiled=True),
            lax.all_gather(projected[:, :, 2 * features :], "seq", axis=1, tiled=True),
        )
        keys_all = keys_all.reshape(row_count, row_len, HEADS, head_dim)
        values_all = values_all.reshape(row_count, row_len, HEADS, head_dim)
        scores = jnp.where(allowed, matmul(queries, keys_all, "rqhd,rkhd->rhqk") * score_scale, NEG)
        largest = jnp.max(scores, axis=-1, keepdims=True)
        log_total = largest + jnp.log(jnp.sum(jnp.exp(scores - largest), axis=-1, keepdims=True))
        weights_low = jnp.exp(scores - log_total).astype(jnp.bfloat16)
        attended = (
            matmul(weights_low, values_all, "rhqk,rkhd->rqhd")
            .astype(jnp.bfloat16)
            .reshape(tok_count, features)
        )
        branch = matmul(attended, out_weight, "td,de->te") + out_bias
        middle = inputs + branch.reshape(inputs.shape)
        normed_two, second_pull = jax.vjp(layer_norm, middle, mlp_gain, mlp_shift)
        normed_two_low = normed_two.astype(jnp.bfloat16).reshape(tok_count, features)
        hidden_pre = matmul(normed_two_low, fc1_weight, "td,df->tf") + fc1_bias
        hidden, gelu_pull = jax.vjp(gelu_exact, hidden_pre)
        hidden_low = hidden.astype(jnp.bfloat16)
        result = middle + (matmul(hidden_low, fc2_weight, "tf,fd->td") + fc2_bias).reshape(
            inputs.shape
        )
        outputs_list.append(result.astype(jnp.bfloat16))
        incoming = cotangent[micro_step].reshape(tok_count, features)
        fc2_weight_part = matmul(hidden_low, incoming, "tf,td->fd")
        fc2_bias_part = jnp.sum(incoming.astype(jnp.float32), axis=0)
        hidden_grad = gelu_pull(matmul(incoming, fc2_weight, "td,fd->tf"))[0].astype(jnp.bfloat16)
        fc1_weight_part = matmul(normed_two_low, hidden_grad, "td,tf->df")
        fc1_bias_part = jnp.sum(hidden_grad.astype(jnp.float32), axis=0)
        back_two = matmul(hidden_grad, fc1_weight, "tf,df->td").reshape(inputs.shape)
        middle_norm, mlp_gain_part, mlp_shift_part = second_pull(back_two)
        middle_grad = incoming.astype(jnp.float32).reshape(inputs.shape) + middle_norm
        branch_grad = middle_grad.astype(jnp.bfloat16).reshape(tok_count, features)
        out_weight_part = matmul(attended, branch_grad, "td,te->de")
        out_bias_part = jnp.sum(branch_grad.astype(jnp.float32), axis=0)
        attended_grad = matmul(branch_grad, out_weight, "te,de->td").astype(jnp.bfloat16)
        attended_grad = attended_grad.reshape(row_count, shard_len, HEADS, head_dim)
        scores_again = jnp.where(
            allowed, matmul(queries, keys_all, "rqhd,rkhd->rhqk") * score_scale, NEG
        )
        chances = jnp.exp(scores_again - log_total)
        chances_low = chances.astype(jnp.bfloat16)
        chance_grad = matmul(attended_grad, values_all, "rqhd,rkhd->rhqk")
        row_delta = jnp.sum(chances * chance_grad, axis=-1, keepdims=True)
        score_grad = (chances * (chance_grad - row_delta)).astype(jnp.bfloat16)
        query_grad = matmul(score_grad, keys_all, "rhqk,rkhd->rqhd") * score_scale
        key_terms = matmul(score_grad, queries, "rhqk,rqhd->rkhd") * score_scale
        value_terms = matmul(chances_low, attended_grad, "rhqk,rqhd->rkhd")
        key_grad, value_grad = (
            lax.psum_scatter(
                key_terms.reshape(row_count, row_len, features).astype(jnp.bfloat16),
                "seq",
                scatter_dimension=1,
                tiled=True,
            ).astype(jnp.float32),
            lax.psum_scatter(
                value_terms.reshape(row_count, row_len, features).astype(jnp.bfloat16),
                "seq",
                scatter_dimension=1,
                tiled=True,
            ).astype(jnp.float32),
        )
        projected_grad = jnp.concatenate(
            [query_grad.reshape(row_count, shard_len, features), key_grad, value_grad], axis=-1
        )
        projected_grad = projected_grad.astype(jnp.bfloat16).reshape(tok_count, 3 * features)
        qkv_weight_part = matmul(normed_low, projected_grad, "td,te->de")
        bias_sums = jnp.sum(projected_grad.astype(jnp.float32), axis=0)
        qv_bias_part = jnp.concatenate([bias_sums[:features], bias_sums[2 * features :]])
        back_one = matmul(projected_grad, qkv_weight, "te,de->td").reshape(inputs.shape)
        inputs_norm, attn_gain_part, attn_shift_part = first_pull(back_one)
        grads_list.append((middle_grad + inputs_norm).astype(jnp.bfloat16))
        pieces = (
            attn_gain_part,
            attn_shift_part,
            qkv_weight_part,
            qv_bias_part,
            out_weight_part,
            out_bias_part,
            mlp_gain_part,
            mlp_shift_part,
            fc1_weight_part,
            fc1_bias_part,
            fc2_weight_part,
            fc2_bias_part,
        )
        totals = [running + member for running, member in zip(totals, pieces)]
    (
        attn_gain_sum,
        attn_shift_sum,
        qkv_weight_sum,
        qv_bias_sum,
        out_weight_sum,
        out_bias_sum,
        mlp_gain_sum,
        mlp_shift_sum,
        fc1_weight_sum,
        fc1_bias_sum,
        fc2_weight_sum,
        fc2_bias_sum,
    ) = totals
    summed = lax.psum(
        (
            attn_gain_sum,
            attn_shift_sum,
            qkv_weight_sum,
            qv_bias_sum,
            out_weight_sum,
            out_bias_sum,
            mlp_gain_sum,
            mlp_shift_sum,
            fc1_weight_sum,
            fc1_bias_sum,
            fc2_weight_sum,
            fc2_bias_sum,
        ),
        ("dp", "seq"),
    )
    return (jnp.stack(outputs_list), jnp.stack(grads_list)) + tuple(summed)

F32 = jnp.float32
BF = jnp.bfloat16
BIG = 1e30
MESH = pl.DeviceIdType.MESH
VMEM_GRANT = 60 * 2**20
ANY = pl.BlockSpec(memory_space=pl.ANY)


def dot_rows(first_op, second_op):
    return lax.dot_general(first_op, second_op, (((1,), (1,)), ((), ())), preferred_element_type=F32)


def dot_plain(first_op, second_op):
    return lax.dot_general(first_op, second_op, (((1,), (0,)), ((), ())), preferred_element_type=F32)


def dot_tokens(first_op, second_op):
    return lax.dot_general(first_op, second_op, (((0,), (0,)), ((), ())), preferred_element_type=F32)


def once(shape, index=None):
    place = index if index is not None else (lambda *_: (0,) * len(shape))
    return pl.BlockSpec(shape, place, pipeline_mode=pl.Buffered(1))


def total_rows(array):
    return jnp.sum(array, axis=0, keepdims=True)


def unit_norm(values):
    center = values - jnp.mean(values, axis=-1, keepdims=True)
    inverse = lax.rsqrt(jnp.mean(center * center, axis=-1, keepdims=True) + EPS)
    return center * inverse, inverse


def norm_back(unit, inverse, incoming, gain):
    scaled = incoming * gain
    return inverse * (
        scaled
        - jnp.mean(scaled, axis=-1, keepdims=True)
        - unit * jnp.mean(scaled * unit, axis=-1, keepdims=True)
    )


def row_of(ref):
    return ref[...].reshape(1, -1)


def enter_kernel(
    tokens_ref, cot_ref, gain_ref, shift_ref, weight_ref, bias_ref,
    row_out, normed_out, projected_out, cot0, cot1, cot2, cot3,
    landed, weight_s, normed_s, projected_s, cot_s, send_sem, recv_sem, load_sem, cot_sem, out_sem,
):
    me, depth = lax.axis_index("seq"), lax.axis_index("dp")
    high, low = me // 2, me % 2
    peers = [me, 2 * high + 1 - low, 2 * (1 - high) + low, 3 - me]
    shard, features = landed.shape[1:]
    barrier = pltpu.get_barrier_semaphore()
    for peer in peers[1:]:
        pl.semaphore_signal(barrier, inc=1, device_id=(depth, peer), device_id_type=MESH)
    own = pltpu.make_async_copy(tokens_ref.at[me, 0], landed.at[0], load_sem.at[0])
    weight = pltpu.make_async_copy(weight_ref, weight_s, load_sem.at[1])
    own.start()
    weight.start()
    pl.semaphore_wait(barrier, 3)

    def remote(at, k, start, size):
        rows = pl.ds(start, size)
        return pltpu.make_async_remote_copy(
            src_ref=tokens_ref.at[peers[k], 0, rows], dst_ref=landed.at[k, rows],
            send_sem=send_sem.at[at], recv_sem=recv_sem.at[at], device_id=(depth, peers[k]), device_id_type=MESH,
        )

    copies = [remote(k - 1, k, 0, shard) for k in (1, 2, 3)]
    for copy in copies[:2]:
        copy.start()
    loads = [pltpu.make_async_copy(cot_ref.at[peers[k], 0], cot_s.at[k], cot_sem.at[k]) for k in range(4)]
    stores = [
        pltpu.make_async_copy(cot_s.at[k], out, cot_sem.at[k]) for k, out in enumerate((cot0, cot1, cot2, cot3))
    ]
    for copy in loads:
        copy.start()
    bias = row_of(bias_ref)
    bias = jnp.concatenate([bias[:, :features], jnp.zeros((1, features), F32), bias[:, features:]], axis=1)

    def outs(k):
        rows = pl.ds(pl.multiple_of(k * shard, shard), shard)
        pairs = (
            (landed.at[k], row_out), (normed_s.at[rows], normed_out), (projected_s.at[rows], projected_out),
        )
        return [
            pltpu.make_async_copy(src, dst.at[rows], out_sem.at[3 * k + n]) for n, (src, dst) in enumerate(pairs)
        ]

    def body(k, carry):
        @pl.when(k == 0)
        def _():
            own.wait()
            weight.wait()

        @pl.when(k == 1)
        def _():
            for load, store in zip(loads, stores):
                load.wait()
                store.start()
            for copy in copies[:2]:
                copy.wait_send()
            copies[2].start()

        for piece in (1, 2, 3):

            @pl.when(k == piece)
            def _():
                copies[piece - 1].wait_recv()

        unit, _ = unit_norm(landed[k].astype(F32))
        normed = (unit * row_of(gain_ref) + row_of(shift_ref)).astype(BF)
        rows = pl.ds(pl.multiple_of(k * shard, shard), shard)
        normed_s[rows, :] = normed
        projected_s[rows, :] = (dot_plain(normed, weight_s[...]) + bias).astype(BF)
        for copy in outs(k):
            copy.start()
        return carry

    lax.fori_loop(0, 4, body, 0)
    for copy in stores:
        copy.wait()
    for k in range(4):
        for copy in outs(k):
            copy.wait()
    copies[2].wait_send()


def enter(tokens, cotangent, gain, shift, weight, bias):
    _, _, shard, features = tokens.shape
    count, wide = 4 * shard, weight.shape[1]
    shape = jax.ShapeDtypeStruct
    vmem = pl.BlockSpec(memory_space=pltpu.VMEM)
    dma = pltpu.SemaphoreType.DMA
    return pl.pallas_call(
        enter_kernel,
        in_specs=[ANY, ANY, vmem, vmem, ANY, vmem],
        out_specs=[ANY] * 7,
        out_shape=[shape((count, features), BF), shape((count, features), BF), shape((count, wide), BF)]
        + [shape((shard, features), BF)] * 4,
        scratch_shapes=[
            pltpu.VMEM((4, shard, features), BF), pltpu.VMEM(weight.shape, BF), pltpu.VMEM((count, features), BF),
            pltpu.VMEM((count, wide), BF), pltpu.VMEM((4, shard, features), BF),
            dma((3,)), dma((3,)), dma((2,)), dma((4,)), dma((12,)),
        ],
        compiler_params=pltpu.CompilerParams(collective_id=0, has_side_effects=True, vmem_limit_bytes=VMEM_GRANT),
        cost_estimate=pl.CostEstimate(flops=4 * 10**9, bytes_accessed=20 * 2**20, transcendentals=0),
        name="enter",
    )(tokens, cotangent, gain, shift, weight, bias)


def attention_forward_kernel(block, q_ref, k_ref, v_ref, miss_ref, own_ref, out_ref, lse_ref):
    lane = lax.broadcasted_iota(jnp.int32, (1, 128), 1)
    first = lane < 64
    keys, values, own = k_ref[...], v_ref[...], own_ref[...]
    ones = jnp.ones_like(values)
    keys_aug = [jnp.where(first, keys, own), jnp.where(first, own, keys)]
    values_aug = [jnp.where(first, values, ones), jnp.where(first, ones, values)]

    def body(step, carry):
        rows = pl.ds(pl.multiple_of(step * block, block), block)
        queries, miss = q_ref[rows, :] * BF(0.125), miss_ref[rows, :]
        outs, logs = [], []
        for head in range(2):
            queries_aug = jnp.where(first, queries, miss) if head == 0 else jnp.where(first, miss, queries)
            scores = dot_rows(queries_aug, keys_aug[head])
            largest = jnp.max(scores, axis=1, keepdims=True)
            weights = jnp.exp(scores - largest).astype(BF)
            mixed = dot_plain(weights, values_aug[head])
            total = mixed[:, 64:65] if head == 0 else mixed[:, 0:1]
            outs.append(mixed / total)
            logs.append(largest + jnp.log(total))
        out_ref[rows, :] = jnp.where(first, outs[0], outs[1]).astype(BF)
        lse_ref[0, rows, :] = jnp.where(first, logs[0], logs[1])
        return carry

    lax.fori_loop(0, q_ref.shape[0] // block, body, 0)


def attention_forward(projected, miss, own, block=256):
    count, width = projected.shape
    pairs = width // 384
    column = lambda base: pl.BlockSpec((count, 128), lambda i: (0, i + base))
    full = pl.BlockSpec((count, 128), lambda i: (0, 0))
    return pl.pallas_call(
        functools.partial(attention_forward_kernel, block),
        grid=(pairs,),
        in_specs=[column(0), column(pairs), column(2 * pairs), full, full],
        out_specs=[column(0), pl.BlockSpec((1, count, 128), lambda i: (i, 0, 0))],
        out_shape=[
            jax.ShapeDtypeStruct((count, width // 3), BF),
            jax.ShapeDtypeStruct((pairs, count, 128), F32),
        ],
        compiler_params=pltpu.CompilerParams(vmem_limit_bytes=VMEM_GRANT),
        cost_estimate=pl.CostEstimate(flops=24 * 10**9, bytes_accessed=8 * 2**20, transcendentals=12 * 2**20),
        name="attention_forward",
    )(projected, projected, projected, miss, own)


def three_parts(column):
    high = column.astype(BF)
    rest = column - high.astype(F32)
    middle = rest.astype(BF)
    return high, middle, (rest - middle.astype(F32)).astype(BF)


def segment_features(segment):
    lane = jnp.arange(128) % 64
    same = lane[None, :] == segment[:, None]
    live = (lane < 8)[None, :]
    return jnp.where(live & ~same, -BIG, 0.0).astype(BF), jnp.where(live & same, 1.0, 0.0).astype(BF)


def flipped(static, bits):
    total = 0
    for at, bit in enumerate(bits):
        weight = 1 << (len(bits) - 1 - at)
        total = total + weight * ((1 - bit) if static & weight else bit)
    return total


def own_bits(order):
    me, deep = lax.axis_index("seq"), lax.axis_index("dp") // 2
    parts = {"low": [me % 2], "high": [me // 2], "deep": [deep // 2, deep % 2]}
    return [bit for name in order for bit in parts[name]]


def scatter_part(out_ref, values, order, part, base=0):
    size = values.shape[0] // 8
    top, *bits = own_bits(order)
    first = 8 * (part + top - 2 * part * top)
    for a in range(8):
        rows = pl.ds(pl.multiple_of((first + flipped(a, bits)) * size, 16), size)
        out_ref[rows, base : base + values.shape[1]] = values[a * size : (a + 1) * size].astype(out_ref.dtype)


def peer_ids():
    me, depth = lax.axis_index("seq"), lax.axis_index("dp")
    high, low = me // 2, me % 2
    core, deep = depth % 2, depth // 2
    upper, lower = deep // 2, deep % 2
    return {
        ("core", 1): (2 * deep + 1 - core, me),
        ("low", 1): (depth, 2 * high + 1 - low),
        ("high", 1): (depth, 2 * (1 - high) + low),
        ("both", 1): (depth, 3 - me),
        ("deep", 1): (2 * (2 * upper + 1 - lower) + core, me),
        ("deep", 2): (2 * (2 * (1 - upper) + lower) + core, me),
        ("deep", 3): (2 * (3 - deep) + core, me),
    }


LOW_FIRST = ("low", "high", "deep")
HIGH_FIRST = ("high", "low", "deep")
DEEP_FIRST = ("deep", "high", "low")
FAN = {"low": 2, "high": 2, "deep": 4}
SEMS = 12


def landing_rows(order, rows):
    sizes = []
    for name in order:
        rows //= FAN[name]
        sizes.append((FAN[name] - 1) * rows)
    return sizes


class Sum:
    def __init__(self, order, rows, send, keep, core_buf, bufs, own, other, send_sems, recv_sems, local_sem):
        self.order, self.rows, self.send, self.keep = order, rows, send, keep
        self.core_buf, self.bufs, self.own, self.other = core_buf, bufs, own, other
        self.send_sems, self.recv_sems, self.local_sem = send_sems, recv_sems, local_sem
        self.sizes = []
        for name in order:
            rows //= FAN[name]
            self.sizes.append(rows)
        self.peers = peer_ids()

    def stage(self, at):
        if at == 0:
            moves = [(self.send, self.core_buf, ("core", 1))]
        elif at <= 3:
            name, size, buf = self.order[at - 1], self.sizes[at - 1], self.bufs[at - 1]
            moves = [
                (self.keep.at[pl.ds(k * size, size)], buf.at[pl.ds((k - 1) * size, size)], (name, k))
                for k in range(1, FAN[name])
            ]
        elif at <= 6:
            name, size = self.order[6 - at], self.sizes[6 - at]
            src = self.keep if at == 4 else self.own
            moves = [
                (src.at[pl.ds(0, size)], self.own.at[pl.ds(k * size, size)], (name, k)) for k in range(1, FAN[name])
            ]
        else:
            moves = [(self.own, self.other, ("core", 1))]
        counts = [1] + [FAN[name] - 1 for name in self.order]
        base = sum((counts + counts[:0:-1])[:at])
        return [
            pltpu.make_async_remote_copy(
                src_ref=src, dst_ref=dst, send_sem=self.send_sems.at[base + k], recv_sem=self.recv_sems.at[base + k],
                device_id=self.peers[peer], device_id_type=MESH,
            )
            for k, (src, dst, peer) in enumerate(moves)
        ]

    def local(self):
        rows = pl.ds(0, self.sizes[2])
        return pltpu.make_async_copy(self.keep.at[rows], self.own.at[rows], self.local_sem)

    def start(self, stage):
        for copy in self.stage(stage):
            copy.start()

    def arrived(self, stage):
        for copy in self.stage(stage):
            copy.wait_recv()

    def left(self, first, last):
        for stage in range(first, last):
            for copy in self.stage(stage):
                copy.wait_send()

    def add(self, start, size, sources):
        chunk = next(rows for rows in (64, 48, 32) if size % rows == 0)

        def body(at, carry):
            rows = lambda base: pl.ds(pl.multiple_of(base + at * chunk, 16), chunk)
            total = self.keep[rows(start), :].astype(F32)
            for buf, offset in sources:
                total = total + buf[rows(offset + start), :].astype(F32)
            self.keep[rows(start), :] = total.astype(self.keep.dtype)
            return carry

        lax.fori_loop(0, size // chunk, body, 0)

    def sources(self, stage):
        if stage == 0:
            return [(self.core_buf, 0)]
        size = self.sizes[stage - 1]
        return [(self.bufs[stage - 1], k * size) for k in range(FAN[self.order[stage - 1]] - 1)]

    def settle(self, stage):
        self.arrived(stage)
        self.add(0, self.rows if stage == 0 else self.sizes[stage - 1], self.sources(stage))

    def tick(self, at, resumed=False):
        if at == 0 or resumed:
            self.start(at)
        elif at <= 3:
            self.arrived(at - 1)
            sources, size = self.sources(at - 1), self.sizes[at - 1]
            self.add(size, (self.rows if at == 1 else self.sizes[at - 2]) - size, sources)
            self.start(at)
            self.add(0, size, sources)
        elif at == 4:
            self.settle(3)
            self.local().start()
            self.start(4)
        elif at <= 7:
            self.arrived(at - 1)
            if at == 5:
                self.local().wait()
            self.start(at)
        else:
            self.arrived(7)


UNITS = 3


def gelu_parts(values):
    size = jnp.abs(values)
    bell = jnp.exp(-0.5 * values * values)
    part = 1.0 / (1.0 + 0.3275911 * 0.7071067811865476 * size)
    series = part * (
        0.127414796
        + part * (-0.142248368 + part * (0.7107068705 + part * (-0.7265760135 + part * 0.5307027145)))
    )
    tail = series * bell
    below = jnp.where(values >= 0, 1.0 - tail, tail)
    return values * below, below + values * (bell * 0.3989422804014327)


FEED_PLAN = {
    (3, 0): [(0, 0)],
    (3, 1): [(0, 1)],
    (5, 0): [(1, 0)],
    (5, 1): [(1, 1), (0, 2)],
    (6, 1): [(1, 2)],
}


def feed_kernel(
    row_ref, att_ref, g0, g1, g2, g3, out_weight_ref, out_bias_ref, gain_ref, shift_ref, fc2_bias_ref,
    w1_ref, bias_ref, w2_ref, *refs
):
    outs, refs = refs[:17], refs[17:]
    results, (branch_out, att_grad_out), sums_out = outs[:4], outs[4:6], outs[6:10]
    last_out, vec_ref = outs[10:16], outs[16]
    (
        n2_s, mid_s, acc_s, back_s, grad_s, hidden_s, hidden_grad_s, result_s, branch_s, att_grad_s,
        d1_s, d2_s, do_s, bias_s, core1, core2, near1, near2, next1, next2, send_sems, recv_sems, load_sems, out_sems,
    ) = refs
    step = pl.program_id(0)
    core = lax.axis_index("dp") % 2
    count = row_ref.shape[0]
    size = w1_ref.shape[1]
    shard = count // 4
    half = do_s.shape[2]
    blocks = [pl.ds(i * shard, shard) for i in range(4)]
    peers = peer_ids()

    def job(unit, which):
        slot = 2 * unit + which
        d, bufs = (d1_s, (core1, near1, next1)) if which == 0 else (d2_s, (core2, near2, next2))
        return Sum(
            (LOW_FIRST, HIGH_FIRST)[which], d.shape[1], d.at[2 * unit], d.at[2 * unit + 1], bufs[0].at[unit],
            [bufs[1].at[unit], bufs[2].at[unit], None], None, None, send_sems.at[slot], recv_sems.at[slot], None,
        )

    def ticks(at, place):
        for unit, tick in FEED_PLAN.get((at, place), []):
            for which in range(2):
                job(unit, which).tick(tick)

    def load(k):
        return pltpu.make_async_copy((g0, g1, g2, g3)[k], grad_s.at[blocks[k]], load_sems.at[k])

    def stores(first, last_store):
        pairs = [(result_s.at[rows], out) for rows, out in zip(blocks, results)]
        pairs += [(branch_s, branch_out), (att_grad_s, att_grad_out)]
        last = 2 * (UNITS - 1)
        pairs += [(d1_s.at[last], last_out[0]), (d1_s.at[last + 1], last_out[1])]
        pairs += [(d2_s.at[last], last_out[2]), (d2_s.at[last + 1], last_out[3])]
        pairs += [(do_s.at[0], last_out[4]), (do_s.at[1], last_out[5])]
        for unit in range(2):
            for which, d in enumerate((d1_s, d2_s)):
                rows = pl.ds(0, d.shape[1] // 4)
                pairs.append((d.at[2 * unit + 1, rows], sums_out[2 * unit + which]))
        return [pltpu.make_async_copy(src, dst, out_sems.at[n]) for n, (src, dst) in enumerate(pairs) if first <= n < last_store]

    @pl.when(step == 0)
    def _():
        barrier = pltpu.get_barrier_semaphore()
        for name in ("core", "low", "high"):
            pl.semaphore_signal(barrier, inc=1, device_id=peers[name, 1], device_id_type=MESH)
        for k in range(4):
            load(k).start()
        vec_ref[...] = jnp.zeros_like(vec_ref)
        for at in range(2 * UNITS):
            bias_s[at : at + 1, :] = bias_ref[at * size : (at + 1) * size].reshape(1, -1)

        def project(i, carry):
            rows = pl.ds(pl.multiple_of(i * shard, shard), shard)
            mid = row_ref[rows, :].astype(F32) + (dot_plain(att_ref[rows, :], out_weight_ref[...]) + row_of(out_bias_ref))
            mid_s[rows, :] = mid
            acc_s[rows, :] = mid + row_of(fc2_bias_ref)
            unit, _ = unit_norm(mid)
            n2_s[rows, :] = (unit * row_of(gain_ref) + row_of(shift_ref)).astype(BF)
            return carry

        lax.fori_loop(0, 4, project, 0)
        back_s[...] = jnp.zeros_like(back_s)
        for k in range(4):
            load(k).wait()

    @pl.when(step == 2)
    def _():
        pl.semaphore_wait(pltpu.get_barrier_semaphore(), 3)

    for at in range(1, 2 * UNITS + 1):
        unit, keeping = (at - 1) // 2, (at - 1) % 2

        @pl.when(step == at)
        def _():
            ticks(at, 0)

    last_step = step == 2 * UNITS

    at_chunk = jnp.maximum(step - 1, 0)
    chunk_row = 2 * (at_chunk // 2) + (core + 1 + at_chunk % 2) % 2

    @pl.when(step > 0)
    def _():
        bias = bias_s[pl.ds(chunk_row, 1), :]

        def body(i, total):
            rows = pl.ds(pl.multiple_of(i * shard, shard), shard)
            pre = dot_plain(n2_s[rows, :], w1_ref[...]) + bias
            back = dot_rows(grad_s[rows, :], w2_ref[...])
            hidden, slope = gelu_parts(pre)
            hidden, hidden_grad = hidden.astype(BF), (back * slope).astype(BF)
            hidden_s[rows, :] = hidden
            hidden_grad_s[rows, :] = hidden_grad
            acc_s[rows, :] += dot_plain(hidden, w2_ref[...])
            back_s[rows, :] += dot_rows(hidden_grad, w1_ref[...])
            return total + total_rows(hidden_grad.astype(F32))

        total = lax.fori_loop(0, 4, body, jnp.zeros((1, size), F32))
        vec_ref[pl.ds(4 + chunk_row, 1), 0:size] = total

    @pl.when(last_step)
    def _():
        def body(i, sums):
            rows = pl.ds(pl.multiple_of(i * shard, shard), shard)
            result_s[rows, :] = acc_s[rows, :].astype(BF)
            back = back_s[rows, :]
            unit, inverse = unit_norm(mid_s[rows, :])
            wide = grad_s[rows, :].astype(F32)
            branch = (wide + norm_back(unit, inverse, back, row_of(gain_ref))).astype(BF)
            branch_s[rows, :] = branch
            att_grad_s[rows, :] = dot_rows(branch, out_weight_ref[...]).astype(BF)
            parts = (back * unit, back, branch.astype(F32), wide)
            return tuple(old + total_rows(part) for old, part in zip(sums, parts))

        sums = lax.fori_loop(0, 4, body, (jnp.zeros((1, n2_s.shape[1]), F32),) * 4)
        for at, part in enumerate(sums):
            vec_ref[at + 10 : at + 11, :] = part
        for copy in stores(0, 6):
            copy.start()

    for at in range(1, 2 * UNITS + 1):

        @pl.when(step == at)
        def _():
            ticks(at, 1)

    @pl.when(step > 0)
    def _():
        def body(part, carry):
            wide, narrow = n2_s.shape[1] // 2, size // 2
            left = n2_s[:, pl.ds(pl.multiple_of(part * wide, 128), wide)]
            scatter_part(d1_s.at[step - 1], dot_tokens(left, hidden_grad_s[...]), LOW_FIRST, part)
            left = hidden_s[:, pl.ds(pl.multiple_of(part * narrow, 128), narrow)]
            scatter_part(d2_s.at[step - 1], dot_tokens(left, grad_s[...]), HIGH_FIRST, part)
            return carry

        lax.fori_loop(0, 2, body, 0)

    @pl.when(last_step)
    def _():
        def body(at, carry):
            slot, part = at // 2, at % 2
            wide = att_ref.shape[1] // 2
            columns = pl.ds(pl.multiple_of(((core + 1 + slot) % 2) * half, 128), half)
            left = att_ref[:, pl.ds(pl.multiple_of(part * wide, 128), wide)]
            scatter_part(do_s.at[slot], dot_tokens(left, branch_s[:, columns]), ORDERS[6], part)
            return carry

        lax.fori_loop(0, 4, body, 0)
        for copy in stores(6, 12):
            copy.start()
        for unit in range(2):
            for which in range(2):
                job(unit, which).settle(2)
        for copy in stores(12, 16):
            copy.start()
        for copy in stores(0, 16):
            copy.wait()
        for unit in range(2):
            for which in range(2):
                job(unit, which).left(0, 3)


def feed(row, attended, grads, out_weight, out_bias, gain, shift, fc1_weight, fc1_bias, fc2_weight, fc2_bias):
    count, features = row.shape
    size = fc1_weight.shape[1] // (2 * UNITS)
    half = features // 2
    shape = jax.ShapeDtypeStruct
    wide, line = once((count, features)), once((features,))
    vmem, dma = pltpu.VMEM, pltpu.SemaphoreType.DMA

    def chunk(i):
        at = jnp.maximum(i - 1, 0)
        return 2 * (at // 2) + (lax.axis_index("dp") % 2 + 1 + at % 2) % 2

    return pl.pallas_call(
        feed_kernel,
        grid=(2 * UNITS + 1,),
        in_specs=[wide, wide] + [ANY] * 4 + [once(out_weight.shape), line, line, line, line]
        + [
            pl.BlockSpec((features, size), lambda i: (0, chunk(i))),
            once(fc1_bias.shape),
            pl.BlockSpec((size, features), lambda i: (chunk(i), 0)),
        ],
        out_specs=[ANY] * 16 + [once((16, features))],
        out_shape=[shape(grads[0].shape, BF)] * 4 + [shape((count, features), BF)] * 2
        + [shape((features // 4, size), BF), shape((size // 4, features), BF)] * 2
        + [shape((features, size), BF)] * 2 + [shape((size, features), BF)] * 2
        + [shape((features, half), BF)] * 2 + [shape((16, features), F32)],
        scratch_shapes=[vmem((count, features), BF)] + [vmem((count, features), F32)] * 3
        + [vmem((count, features), BF), vmem((count, size), BF), vmem((count, size), BF)]
        + [vmem((count, features), BF)] * 3
        + [
            vmem((2 * UNITS, features, size), BF), vmem((2 * UNITS, size, features), BF), vmem((2, features, half), BF),
            vmem((8, size), F32),
            vmem((2, features, size), BF), vmem((2, size, features), BF),
            vmem((2, features // 2, size), BF), vmem((2, size // 2, features), BF),
            vmem((2, features // 4, size), BF), vmem((2, size // 4, features), BF),
            dma((4, SEMS)), dma((4, SEMS)), dma((4,)), dma((16,)),
        ],
        compiler_params=pltpu.CompilerParams(collective_id=2, has_side_effects=True, vmem_limit_bytes=VMEM_GRANT),
        cost_estimate=pl.CostEstimate(flops=35 * 10**9, bytes_accessed=40 * 2**20, transcendentals=0),
        name="feed",
    )(
        row, attended, *grads, out_weight, out_bias, gain, shift, fc2_bias, fc1_weight, fc1_bias, fc2_weight,
    )


ORDERS = (
    LOW_FIRST, HIGH_FIRST, LOW_FIRST, HIGH_FIRST, LOW_FIRST, HIGH_FIRST, DEEP_FIRST, LOW_FIRST, LOW_FIRST, LOW_FIRST
)
PLAN = {
    (0, 0): [(4, 0), (5, 0), (6, 0), (0, 3), (1, 3), (2, 3), (3, 3)],
    (0, 1): [(4, 1), (5, 1), (6, 1), (0, 4)],
    (1, 0): [(1, 4)],
    (1, 1): [(4, 2), (5, 2), (2, 4), (3, 4)],
    (2, 0): [(7, 0)],
    (2, 1): [(7, 1)],
    (3, 1): [(6, 2), (0, 5)],
    (4, 0): [(8, 0), (4, 3), (5, 3), (1, 5)],
    (4, 1): [(8, 1), (7, 2), (6, 3), (2, 5), (3, 5), (0, 6)],
    (5, 0): [(1, 6)],
    (5, 1): [(8, 2), (7, 3), (4, 4), (5, 4), (6, 4), (2, 6)],
    (6, 0): [(9, 0)],
    "tail": [
        (9, 1), (7, 4), (4, 5), (3, 6), (1, 7), (8, 3), (0, 7), (6, 5), (5, 5), (7, 5), (8, 4), (2, 7),
        (8, 5), (4, 6), (3, 7), (6, 6), (9, 2), (7, 6), (8, 6), (5, 6), (9, 3), (6, 7), (4, 7), (9, 4),
        (5, 7), (7, 7), (9, 5), (9, 6), (8, 7), (9, 7),
    ],
}
BLOCK_OUT_AT = 0


def three_parts(column):
    high = column.astype(BF)
    rest = column - high.astype(F32)
    middle = rest.astype(BF)
    return high, middle, (rest - middle.astype(F32)).astype(BF)


def pair_backward(refs, outs, dk_acc, dv_acc, pair, block):
    q_ref, k_ref, v_ref, att_ref, grad_ref, lse_ref, miss_ref, own_ref = refs
    lane = lax.broadcasted_iota(jnp.int32, (1, 128), 1)
    first = lane < 64
    half = lane % 64
    keys, values, own = k_ref[...], v_ref[...], own_ref[...]
    unit = jnp.where((half >= 8) & (half < 11), 1.0, 0.0).astype(BF)
    own = own + unit
    unit_rows = jnp.broadcast_to(unit, values.shape)
    keys_aug = [jnp.where(first, keys, own), jnp.where(first, own, keys)]
    values_aug = [jnp.where(first, values, unit_rows), jnp.where(first, unit_rows, values)]
    keys_only = [jnp.where(first, keys, BF(0)), jnp.where(first, BF(0), keys)]
    dk_acc[...] = jnp.zeros_like(dk_acc)
    dv_acc[...] = jnp.zeros_like(dv_acc)
    columns = pl.ds(pl.multiple_of(pair * 128, 128), 128)

    def spread(column):
        high, middle, low = [part.astype(F32) for part in three_parts(-column)]
        wide = jnp.where(half == 8, high, jnp.where(half == 9, middle, jnp.where(half == 10, low, 0.0)))
        return wide.astype(BF)

    def body(step, carry):
        rows = pl.ds(pl.multiple_of(step * block, block), block)
        queries, miss, grad = q_ref[rows, :] * BF(0.125), miss_ref[rows, :], grad_ref[rows, :]
        both = att_ref[rows, :].astype(F32) * grad.astype(F32)
        logs = lse_ref[0, rows, :]
        queries_t, grad_t = queries.T, grad.T
        dq = jnp.zeros((block, 128), F32)
        for head in range(2):
            mine = first if head == 0 else jnp.logical_not(first)
            span = pl.ds(64 * head, 64)
            delta = jnp.sum(jnp.where(mine, both, 0.0), axis=1, keepdims=True)
            total = logs[:, 0:1] if head == 0 else logs[:, 64:65]
            queries_aug = jnp.where(mine, queries, spread(total) + miss)
            grad_aug = jnp.where(mine, grad, spread(delta))
            probs = jnp.exp(dot_rows(queries_aug, keys_aug[head]))
            score_grad = (probs * dot_rows(grad_aug, values_aug[head])).astype(BF)
            dq = dq + dot_plain(score_grad, keys_only[head])
            dk_acc[span, :] += dot_plain(queries_t[64 * head : 64 * head + 64], score_grad)
            dv_acc[span, :] += dot_plain(grad_t[64 * head : 64 * head + 64], probs.astype(BF))
        outs[0][rows, columns] = (dq * 0.125).astype(BF)
        return carry

    lax.fori_loop(0, q_ref.shape[0] // block, body, 0)
    outs[1][:, columns] = dk_acc[...].T.astype(BF)
    outs[2][:, columns] = dv_acc[...].T.astype(BF)


def backward_kernel(*refs):
    (
        q_ref, k_ref, v_ref, att_ref, grad_ref, lse_ref, miss_ref, own_ref, normed_ref,
        weight_ref, row_ref, branch_ref, gain_ref, vec_in_ref,
    ) = refs[:14]
    results, sums_in, last_in = refs[14:18], refs[18:22], refs[22:28]
    block_out, tokens_out, vec_out = refs[28:31]
    owns, others = refs[31:41], refs[41:51]
    (
        dq_s, dk_s, dv_s, dk_acc, dv_acc, qkv_s, own_result, grad_s, vec_s, vec_got,
        send_sems, recv_sems, local_sems, load_sems, side_send, side_recv, vec_send, vec_recv,
    ) = refs[51:69]
    held = refs[69:76]
    landing = refs[76:]
    step = pl.program_id(0)
    me, depth = lax.axis_index("seq"), lax.axis_index("dp")
    core = depth % 2
    peers = peer_ids()
    shard = results[0].shape[0]
    features = row_ref.shape[1]

    def job(n):
        sems = send_sems.at[n], recv_sems.at[n], local_sems.at[n]
        if n < 4:
            return Sum(
                ORDERS[n], 4 * held[n].shape[0], None, held[n], None, [None, None, landing[n]], owns[n], others[n], *sems
            )
        send = last_in[2 * (n - 4)] if n < 7 else qkv_s.at[2 * (n - 7)]
        keep = held[n] if n < 7 else qkv_s.at[2 * (n - 7) + 1]
        core_buf, *bufs = landing[4 * (n - 3) : 4 * (n - 2)]
        return Sum(ORDERS[n], keep.shape[0], send, keep, core_buf, bufs, owns[n], others[n], *sems)

    def load(n):
        if n == 7:
            return pltpu.make_async_copy(results[0], own_result, load_sems.at[7])
        src = sums_in[n] if n < 4 else last_in[2 * (n - 4) + 1]
        return pltpu.make_async_copy(src, held[n], load_sems.at[n])

    def store():
        return pltpu.make_async_copy(own_result, block_out.at[me, 0], load_sems.at[7])

    def token_store():
        return pltpu.make_async_copy(grad_s.at[0], tokens_out.at[me, 0], load_sems.at[8])

    kinds = [("low", 1), ("high", 1), ("both", 1)]

    def spread_row(number, k, piece, out):
        return pltpu.make_async_remote_copy(
            src_ref=piece, dst_ref=out.at[me, 0], send_sem=side_send.at[number, k - 1],
            recv_sem=side_recv.at[number, k - 1], device_id=peers[kinds[k - 1]], device_id_type=MESH,
        )

    def block_copy(k):
        return spread_row(0, k, results[k], block_out)

    def token_copy(k):
        return spread_row(1, k, grad_s.at[k], tokens_out)

    vec_names = [[("core", 1)], kinds, [("deep", 1), ("deep", 2), ("deep", 3)]]

    def vec_stage(stage):
        return [
            pltpu.make_async_remote_copy(
                src_ref=vec_s.at[stage], dst_ref=vec_got.at[stage, k],
                send_sem=vec_send.at[stage, k], recv_sem=vec_recv.at[stage, k],
                device_id=peers[name], device_id_type=MESH,
            )
            for k, name in enumerate(vec_names[stage])
        ]

    def vec_step(stage):
        for copy in vec_stage(stage):
            copy.wait_recv()
        total = vec_s[stage]
        for k in range(len(vec_names[stage])):
            total = total + vec_got[stage, k]
        if stage == 2:
            vec_out[...] = total
        else:
            vec_s[stage + 1] = total
            for copy in vec_stage(stage + 1):
                copy.start()

    def ticks(at, place):
        for n, tick in PLAN.get((at, place), []):
            resumed = n < 4 and tick == 3
            if resumed or (4 <= n < 7 and tick == 1):
                load(n).wait()
            job(n).tick(tick, resumed)

    @pl.when(step == 0)
    def _():
        barrier = pltpu.get_barrier_semaphore()
        for peer in peers.values():
            pl.semaphore_signal(barrier, inc=1, device_id=peer, device_id_type=MESH)
        for n in range(8):
            load(n).start()
        pl.semaphore_wait(barrier, len(peers))

    for at in range(7):

        @pl.when(step == at)
        def _():
            ticks(at, 0)
            if at == 2:
                load(7).wait()
                store().start()

    @pl.when(step < 6)
    def _():
        pair = 2 * (step // 2) + (core + 1 + step % 2) % 2
        pair_backward(
            (q_ref, k_ref, v_ref, att_ref, grad_ref, lse_ref, miss_ref, own_ref),
            (dq_s, dk_s, dv_s), dk_acc, dv_acc, pair, 256,
        )

    for at in range(6):

        @pl.when(step == at)
        def _():
            ticks(at, 1)
            if at == BLOCK_OUT_AT:
                for k in (1, 2, 3):
                    block_copy(k).start()

    @pl.when(step < 6)
    def _():
        pair = 2 * (step // 2) + (core + 1 + step % 2) % 2
        columns = pl.ds(pl.multiple_of(pair * 128, 128), 128)
        grads = jnp.concatenate([part[:, columns] for part in (dq_s, dk_s, dv_s)], axis=1)
        vec_out[2:3, columns] = total_rows(grads[:, :128].astype(F32))
        vec_out[3:4, columns] = total_rows(grads[:, 256:].astype(F32))

        def body(part, carry):
            left = normed_ref[:, pl.ds(pl.multiple_of(part * (features // 2), 128), features // 2)]
            scatter_part(qkv_s.at[step], dot_tokens(left, grads), ORDERS[7], part)
            return carry

        lax.fori_loop(0, 2, body, 0)

    @pl.when(step == 6)
    def _():
        def body(at, sums):
            k = 3 - at
            rows = pl.ds(pl.multiple_of(k * shard, shard), shard)
            back = dot_rows(dq_s[rows, :], weight_ref[:, :features])
            back = back + dot_rows(dk_s[rows, :], weight_ref[:, features : 2 * features])
            back = back + dot_rows(dv_s[rows, :], weight_ref[:, 2 * features :])
            unit, inverse = unit_norm(row_ref[rows, :].astype(F32))
            grad_s[k] = (branch_ref[rows, :].astype(F32) + norm_back(unit, inverse, back, row_of(gain_ref))).astype(BF)
            for piece in range(4):

                @pl.when(k == piece)
                def _():
                    if piece:
                        token_copy(piece).start()
                    else:
                        token_store().start()

            return tuple(old + total_rows(part) for old, part in zip(sums, (back * unit, back)))

        gain_sum, shift_sum = lax.fori_loop(0, 4, body, (jnp.zeros((1, features), F32),) * 2)
        vec_s[0] = vec_in_ref[...]
        vec_s[0, 0:1, :] = gain_sum
        vec_s[0, 1:2, :] = shift_sum
        vec_s[0, 2:4, :] = vec_out[2:4, :]
        vec_stage(0)[0].start()

    @pl.when(step == 7)
    def _():
        for index, (n, tick) in enumerate(PLAN["tail"]):
            if index in (3, 8, 13):
                vec_step((index - 3) // 5)
            job(n).tick(tick)
        for n in range(10):
            job(n).arrived(7)
        for n in range(10):
            job(n).left(3 if n < 4 else 0, 8)
        store().wait()
        token_store().wait()
        for k in (1, 2, 3):
            block_copy(k).wait()
            token_copy(k).wait()
        for stage in range(3):
            for copy in vec_stage(stage):
                copy.wait_send()


def backward(
    projected, attended, attended_grad, logs, miss, own, normed, qkv_weight, row, branch, gain, vec_in,
    results, sums_in, last_in,
):
    count, width = projected.shape
    features = width // 3
    pairs = width // 384
    half = features // 2
    shard = count // 4

    def pair(i):
        at = jnp.minimum(i, 5)
        return 2 * (at // 2) + (lax.axis_index("dp") % 2 + 1 + at % 2) % 2

    column = lambda base: pl.BlockSpec((count, 128), lambda i: (0, pair(i) + base))
    shape = jax.ShapeDtypeStruct
    wide = once((count, features))
    full = once((count, 128))
    vmem, dma = pltpu.VMEM, pltpu.SemaphoreType.DMA
    sizes = [last_in[0].shape, last_in[2].shape] * UNITS + [(features, half)] * 4
    held = [vmem(array.shape, BF) for array in (*sums_in, *last_in[1::2])]
    landing = []
    for n, (rows, columns) in enumerate(sizes):
        lands = landing_rows(ORDERS[n], rows)
        landing += [vmem((lands[2], columns), BF)] if n < 4 else [vmem((size, columns), BF) for size in [rows] + lands]
    return pl.pallas_call(
        backward_kernel,
        grid=(8,),
        in_specs=[
            column(0), column(pairs), column(2 * pairs), column(0), column(0),
            pl.BlockSpec((1, count, 128), lambda i: (pair(i), 0, 0)),
            full, full, wide, once(qkv_weight.shape), wide, wide, once((features,)), once((16, features)),
        ]
        + [ANY] * 14,
        out_specs=[ANY, ANY, once((16, features))] + [ANY] * 20,
        out_shape=[shape((4, 1, shard, features), BF)] * 2 + [shape((16, features), F32)]
        + [shape(size, BF) for size in sizes] * 2,
        scratch_shapes=[vmem((count, features), BF)] * 3
        + [vmem((128, count), F32)] * 2
        + [vmem((6, features, half), BF)]
        + [
            vmem((shard, features), BF), vmem((4, shard, features), BF),
            vmem((3, 16, features), F32), vmem((3, 3, 16, features), F32),
            dma((10, SEMS)), dma((10, SEMS)), dma((10,)), dma((9,)), dma((2, 3)), dma((2, 3)), dma((3, 3)), dma((3, 3)),
        ]
        + held + landing,
        compiler_params=pltpu.CompilerParams(collective_id=1, has_side_effects=True, vmem_limit_bytes=VMEM_GRANT),
        cost_estimate=pl.CostEstimate(flops=60 * 10**9, bytes_accessed=60 * 2**20, transcendentals=12 * 2**20),
        name="backward",
    )(
        projected, projected, projected, attended, attended_grad, logs, miss, own, normed, qkv_weight, row, branch,
        gain, vec_in, *results, *sums_in, *last_in,
    )


STEPS = 8


def own_group(order):
    total = 0
    for bit in own_bits(order):
        total = 2 * total + bit
    return total


def assemble_kernel(*refs):
    ins, vec_ref = refs[:20], refs[20]
    d1_ref, d2_ref, out_ref, qkv_ref = refs[21:25]
    vecs = refs[25:]
    core = lax.axis_index("dp") % 2
    features = out_ref.shape[1]
    size = ins[0].shape[1]
    half = features // 2

    def ordered(n):
        ref, last = ins[n], own_bits(ORDERS[n // 2])[3]
        rows = ref.shape[0] // 2
        return jnp.concatenate(
            [ref[pl.ds(pl.multiple_of((a + last - 2 * a * last) * rows, 16), rows), :] for a in range(2)], axis=0
        ).astype(F32)

    for side in range(2):
        home = core if side == 0 else 1 - core
        for unit in range(UNITS):
            columns = pl.ds(pl.multiple_of((2 * unit + home) * size, 128), size)
            d1_ref[:, columns] = ordered(4 * unit + side)
            d2_ref[unit, home] = ordered(4 * unit + 2 + side)
        out_ref[:, pl.ds(pl.multiple_of(home * half, 128), half)] = ordered(12 + side)
        for group in range(3):
            values = ordered(14 + 2 * group + side)
            for part in range(3):
                at = part * features + (2 * group + home) * 128
                qkv_ref[:, pl.ds(pl.multiple_of(at, 128), 128)] = values[:, part * 128 : (part + 1) * 128]

    @pl.when(pl.program_id(0) == 0)
    def _():
        for ref, row in zip(vecs, (0, 1, 12, 10, 11, 13)):
            ref[...] = vec_ref[row, :]
        qv_ref, fc1_ref = vecs[6:]
        for at in range(2):
            qv_ref[at * features : (at + 1) * features] = vec_ref[2 + at, :]
        for at in range(2 * UNITS):
            fc1_ref[at * size : (at + 1) * size] = vec_ref[4 + at, 0:size]


def assemble(parts, vector):
    features, size = parts[0].shape
    half = features // 2
    wide = 2 * UNITS * size
    shape = jax.ShapeDtypeStruct

    def spec(n):
        rows, columns = parts[n].shape
        return pl.BlockSpec((rows // STEPS, columns), lambda i: (i ^ (own_group(ORDERS[n // 2]) // 2), 0))

    lines = [features] * 6 + [2 * features, wide]
    d1, d2, out, qkv, *vecs = pl.pallas_call(
        assemble_kernel,
        grid=(STEPS,),
        in_specs=[spec(n) for n in range(20)] + [once(vector.shape)],
        out_specs=[
            pl.BlockSpec((features // STEPS, wide), lambda i: (i, 0)),
            pl.BlockSpec((UNITS, 2, size // STEPS, features), lambda i: (0, 0, i, 0)),
            pl.BlockSpec((features // STEPS, features), lambda i: (i, 0)),
            pl.BlockSpec((features // STEPS, 3 * features), lambda i: (i, 0)),
        ]
        + [once((line,)) for line in lines],
        out_shape=[
            shape((features, wide), F32), shape((UNITS, 2, size, features), F32), shape((features, features), F32),
            shape((features, 3 * features), F32),
        ]
        + [shape((line,), F32) for line in lines],
        compiler_params=pltpu.CompilerParams(vmem_limit_bytes=VMEM_GRANT),
        cost_estimate=pl.CostEstimate(flops=0, bytes_accessed=45 * 2**20, transcendentals=0),
        name="assemble",
    )(*parts, vector)
    return d1, d2.reshape(wide, features), out, qkv, vecs


def swap(array, axis, bit):
    count = lax.axis_size(axis)
    return lax.ppermute(array, axis, [(i, i ^ bit) for i in range(count)])


def fast_shards(
    tokens, image_lengths, cotangent, attn_gain, attn_shift, qkv_weight, qv_bias, out_weight,
    out_bias, mlp_gain, mlp_shift, fc1_weight, fc1_bias, fc2_weight, fc2_bias,
):
    shard_len = tokens.shape[2]
    parties = lax.axis_size("seq")
    row_len = shard_len * parties
    images = image_lengths.shape[2] - 1
    me = lax.axis_index("seq")

    row, normed, projected, *cots = enter(tokens, cotangent, attn_gain, attn_shift, qkv_weight, qv_bias)
    seg_row = segment_ids(lax.dynamic_index_in_dim(image_lengths, me, 0, keepdims=False), row_len, images)
    seg_row = seg_row.reshape(parties, shard_len)
    segment = jnp.concatenate([seg_row[me ^ k] for k in range(parties)], axis=0)
    miss, own = segment_features(segment)
    attended, logs = attention_forward(projected, miss, own)
    grads = [cots[0]] + [swap(cots[k], "seq", k) for k in (1, 2, 3)]
    fed = feed(
        row, attended, grads, out_weight, out_bias, mlp_gain, mlp_shift, fc1_weight, fc1_bias, fc2_weight, fc2_bias
    )
    results, (branch, attended_grad), sums, last, vec = fed[:4], fed[4:6], fed[6:10], fed[10:16], fed[16]
    block_out, tokens_grad, vector, *summed = backward(
        projected, attended, attended_grad, logs, miss, own, normed, qkv_weight, row, branch, attn_gain, vec,
        results, sums, last,
    )
    paired = [part for n in range(10) for part in (summed[n], summed[10 + n])]
    fc1_grad, fc2_grad, out_grad, qkv_grad, vecs = assemble(paired, vector)
    gain, shift, out_sum, mlp_gain_sum, mlp_shift_sum, fc2_sum, qv_sum, fc1_sum = vecs
    return (
        block_out, tokens_grad, gain, shift, qkv_grad, qv_sum, out_grad, out_sum, mlp_gain_sum, mlp_shift_sum,
        fc1_grad, fc1_sum, fc2_grad, fc2_sum,
    )


def shards(tokens, *rest):
    micro_count, row_count, shard_len, features = tokens.shape
    whole_rows = micro_count == 4 and row_count == 1 and shard_len % 128 == 0
    sizes = lax.axis_size("dp") == 8 and lax.axis_size("seq") == 4
    hidden = rest[10].shape[1]
    if sizes and whole_rows and features == 64 * HEADS == 768 and hidden == 4 * features:
        return fast_shards(tokens, *rest)
    return general_shards(tokens, *rest)


def solution(mesh):
    placed = (
        P(None, "dp", "seq", None),
        P(None, "dp", None),
        P(None, "dp", "seq", None),
        P(),
        P(),
        P(),
        P(),
        P(),
        P(),
        P(),
        P(),
        P(),
        P(),
        P(),
        P(),
    )
    return jax.shard_map(
        shards,
        mesh=mesh,
        in_specs=placed,
        out_specs=(
            P(None, "dp", "seq", None),
            P(None, "dp", "seq", None),
            P(),
            P(),
            P(),
            P(),
            P(),
            P(),
            P(),
            P(),
            P(),
            P(),
            P(),
            P(),
        ),
        check_vma=False,
    )
```

```python
import functools

import jax
import jax.numpy as jnp
from jax import lax
from jax.experimental import pallas as pl
from jax.experimental.pallas import tpu as pltpu
from jax.sharding import PartitionSpec as P

HEADS = 12


EPS = 1e-06
NEG = -1e30


def layer_norm(values, scale_row, shift_row):
    center = values - jnp.mean(values, axis=-1, keepdims=True)
    spread = jnp.mean(center * center, axis=-1, keepdims=True)
    return center * lax.rsqrt(spread + EPS) * scale_row + shift_row


def gelu_exact(values):
    return jax.nn.gelu(values, approximate=False)


def segment_ids(lengths, row_len, images):
    positions = jnp.arange(row_len, dtype=jnp.int32)
    ends = jnp.cumsum(lengths, axis=-1) + 2 * images
    patches = jnp.sum((positions[:, None] >= ends[..., None, :]).astype(jnp.int32), axis=-1)
    return jnp.where(positions < 2 * images, positions // 2, patches)


def matmul(first_op, second_op, pattern):
    return jnp.einsum(pattern, first_op, second_op, preferred_element_type=jnp.float32)


def general_shards(
    tokens,
    image_lengths,
    cotangent,
    attn_gain,
    attn_shift,
    qkv_weight,
    qv_bias,
    out_weight,
    out_bias,
    mlp_gain,
    mlp_shift,
    fc1_weight,
    fc1_bias,
    fc2_weight,
    fc2_bias,
):
    micro_count, row_count, shard_len, features = tokens.shape
    row_len = shard_len * lax.axis_size("seq")
    images = image_lengths.shape[2] - 1
    head_dim = features // HEADS
    score_scale = head_dim ** (-0.5)
    offset = lax.axis_index("seq") * shard_len
    tok_count = row_count * shard_len
    zero_keys = jnp.zeros((features,), jnp.float32)
    full_bias = jnp.concatenate([qv_bias[:features], zero_keys, qv_bias[features:]])
    totals = [
        jnp.zeros(weight.shape, jnp.float32)
        for weight in (
            attn_gain,
            attn_shift,
            qkv_weight,
            qv_bias,
            out_weight,
            out_bias,
            mlp_gain,
            mlp_shift,
            fc1_weight,
            fc1_bias,
            fc2_weight,
            fc2_bias,
        )
    ]
    outputs_list = []
    grads_list = []
    for micro_step in range(micro_count):
        inputs = tokens[micro_step].astype(jnp.float32)
        seg_all = segment_ids(image_lengths[micro_step], row_len, images)
        seg_here = lax.dynamic_slice_in_dim(seg_all, offset, shard_len, 1)
        allowed = seg_here[:, None, :, None] == seg_all[:, None, None, :]
        normed, first_pull = jax.vjp(layer_norm, inputs, attn_gain, attn_shift)
        normed_low = normed.astype(jnp.bfloat16).reshape(tok_count, features)
        projected = (matmul(normed_low, qkv_weight, "td,de->te") + full_bias).astype(jnp.bfloat16)
        projected = projected.reshape(row_count, shard_len, 3 * features)
        queries = projected[:, :, :features].reshape(row_count, shard_len, HEADS, head_dim)
        keys_all, values_all = (
            lax.all_gather(projected[:, :, features : 2 * features], "seq", axis=1, tiled=True),
            lax.all_gather(projected[:, :, 2 * features :], "seq", axis=1, tiled=True),
        )
        keys_all = keys_all.reshape(row_count, row_len, HEADS, head_dim)
        values_all = values_all.reshape(row_count, row_len, HEADS, head_dim)
        scores = jnp.where(allowed, matmul(queries, keys_all, "rqhd,rkhd->rhqk") * score_scale, NEG)
        largest = jnp.max(scores, axis=-1, keepdims=True)
        log_total = largest + jnp.log(jnp.sum(jnp.exp(scores - largest), axis=-1, keepdims=True))
        weights_low = jnp.exp(scores - log_total).astype(jnp.bfloat16)
        attended = (
            matmul(weights_low, values_all, "rhqk,rkhd->rqhd")
            .astype(jnp.bfloat16)
            .reshape(tok_count, features)
        )
        branch = matmul(attended, out_weight, "td,de->te") + out_bias
        middle = inputs + branch.reshape(inputs.shape)
        normed_two, second_pull = jax.vjp(layer_norm, middle, mlp_gain, mlp_shift)
        normed_two_low = normed_two.astype(jnp.bfloat16).reshape(tok_count, features)
        hidden_pre = matmul(normed_two_low, fc1_weight, "td,df->tf") + fc1_bias
        hidden, gelu_pull = jax.vjp(gelu_exact, hidden_pre)
        hidden_low = hidden.astype(jnp.bfloat16)
        result = middle + (matmul(hidden_low, fc2_weight, "tf,fd->td") + fc2_bias).reshape(
            inputs.shape
        )
        outputs_list.append(result.astype(jnp.bfloat16))
        incoming = cotangent[micro_step].reshape(tok_count, features)
        fc2_weight_part = matmul(hidden_low, incoming, "tf,td->fd")
        fc2_bias_part = jnp.sum(incoming.astype(jnp.float32), axis=0)
        hidden_grad = gelu_pull(matmul(incoming, fc2_weight, "td,fd->tf"))[0].astype(jnp.bfloat16)
        fc1_weight_part = matmul(normed_two_low, hidden_grad, "td,tf->df")
        fc1_bias_part = jnp.sum(hidden_grad.astype(jnp.float32), axis=0)
        back_two = matmul(hidden_grad, fc1_weight, "tf,df->td").reshape(inputs.shape)
        middle_norm, mlp_gain_part, mlp_shift_part = second_pull(back_two)
        middle_grad = incoming.astype(jnp.float32).reshape(inputs.shape) + middle_norm
        branch_grad = middle_grad.astype(jnp.bfloat16).reshape(tok_count, features)
        out_weight_part = matmul(attended, branch_grad, "td,te->de")
        out_bias_part = jnp.sum(branch_grad.astype(jnp.float32), axis=0)
        attended_grad = matmul(branch_grad, out_weight, "te,de->td").astype(jnp.bfloat16)
        attended_grad = attended_grad.reshape(row_count, shard_len, HEADS, head_dim)
        scores_again = jnp.where(
            allowed, matmul(queries, keys_all, "rqhd,rkhd->rhqk") * score_scale, NEG
        )
        chances = jnp.exp(scores_again - log_total)
        chances_low = chances.astype(jnp.bfloat16)
        chance_grad = matmul(attended_grad, values_all, "rqhd,rkhd->rhqk")
        row_delta = jnp.sum(chances * chance_grad, axis=-1, keepdims=True)
        score_grad = (chances * (chance_grad - row_delta)).astype(jnp.bfloat16)
        query_grad = matmul(score_grad, keys_all, "rhqk,rkhd->rqhd") * score_scale
        key_terms = matmul(score_grad, queries, "rhqk,rqhd->rkhd") * score_scale
        value_terms = matmul(chances_low, attended_grad, "rhqk,rqhd->rkhd")
        key_grad, value_grad = (
            lax.psum_scatter(
                key_terms.reshape(row_count, row_len, features).astype(jnp.bfloat16),
                "seq",
                scatter_dimension=1,
                tiled=True,
            ).astype(jnp.float32),
            lax.psum_scatter(
                value_terms.reshape(row_count, row_len, features).astype(jnp.bfloat16),
                "seq",
                scatter_dimension=1,
                tiled=True,
            ).astype(jnp.float32),
        )
        projected_grad = jnp.concatenate(
            [query_grad.reshape(row_count, shard_len, features), key_grad, value_grad], axis=-1
        )
        projected_grad = projected_grad.astype(jnp.bfloat16).reshape(tok_count, 3 * features)
        qkv_weight_part = matmul(normed_low, projected_grad, "td,te->de")
        bias_sums = jnp.sum(projected_grad.astype(jnp.float32), axis=0)
        qv_bias_part = jnp.concatenate([bias_sums[:features], bias_sums[2 * features :]])
        back_one = matmul(projected_grad, qkv_weight, "te,de->td").reshape(inputs.shape)
        inputs_norm, attn_gain_part, attn_shift_part = first_pull(back_one)
        grads_list.append((middle_grad + inputs_norm).astype(jnp.bfloat16))
        pieces = (
            attn_gain_part,
            attn_shift_part,
            qkv_weight_part,
            qv_bias_part,
            out_weight_part,
            out_bias_part,
            mlp_gain_part,
            mlp_shift_part,
            fc1_weight_part,
            fc1_bias_part,
            fc2_weight_part,
            fc2_bias_part,
        )
        totals = [running + member for running, member in zip(totals, pieces)]
    (
        attn_gain_sum,
        attn_shift_sum,
        qkv_weight_sum,
        qv_bias_sum,
        out_weight_sum,
        out_bias_sum,
        mlp_gain_sum,
        mlp_shift_sum,
        fc1_weight_sum,
        fc1_bias_sum,
        fc2_weight_sum,
        fc2_bias_sum,
    ) = totals
    summed = lax.psum(
        (
            attn_gain_sum,
            attn_shift_sum,
            qkv_weight_sum,
            qv_bias_sum,
            out_weight_sum,
            out_bias_sum,
            mlp_gain_sum,
            mlp_shift_sum,
            fc1_weight_sum,
            fc1_bias_sum,
            fc2_weight_sum,
            fc2_bias_sum,
        ),
        ("dp", "seq"),
    )
    return (jnp.stack(outputs_list), jnp.stack(grads_list)) + tuple(summed)

F32 = jnp.float32
BF = jnp.bfloat16
BIG = 1e30
MESH = pl.DeviceIdType.MESH
VMEM_GRANT = 60 * 2**20
ANY = pl.BlockSpec(memory_space=pl.ANY)


def dot_rows(first_op, second_op):
    return lax.dot_general(first_op, second_op, (((1,), (1,)), ((), ())), preferred_element_type=F32)


def dot_plain(first_op, second_op):
    return lax.dot_general(first_op, second_op, (((1,), (0,)), ((), ())), preferred_element_type=F32)


def dot_tokens(first_op, second_op):
    return lax.dot_general(first_op, second_op, (((0,), (0,)), ((), ())), preferred_element_type=F32)


def once(shape, index=None):
    place = index if index is not None else (lambda *_: (0,) * len(shape))
    return pl.BlockSpec(shape, place, pipeline_mode=pl.Buffered(1))


def total_rows(array):
    return jnp.sum(array, axis=0, keepdims=True)


def unit_norm(values):
    center = values - jnp.mean(values, axis=-1, keepdims=True)
    inverse = lax.rsqrt(jnp.mean(center * center, axis=-1, keepdims=True) + EPS)
    return center * inverse, inverse


def norm_back(unit, inverse, incoming, gain):
    scaled = incoming * gain
    return inverse * (
        scaled
        - jnp.mean(scaled, axis=-1, keepdims=True)
        - unit * jnp.mean(scaled * unit, axis=-1, keepdims=True)
    )


def row_of(ref):
    return ref[...].reshape(1, -1)


def enter_kernel(
    tokens_ref, cot_ref, gain_ref, shift_ref, weight_ref, bias_ref,
    row_out, normed_out, projected_out, cot0, cot1, cot2, cot3,
    landed, weight_s, normed_s, projected_s, cot_s, send_sem, recv_sem, load_sem, cot_sem, out_sem,
):
    me, depth = lax.axis_index("seq"), lax.axis_index("dp")
    high, low = me // 2, me % 2
    peers = [me, 2 * high + 1 - low, 2 * (1 - high) + low, 3 - me]
    shard, features = landed.shape[1:]
    barrier = pltpu.get_barrier_semaphore()
    for peer in peers[1:]:
        pl.semaphore_signal(barrier, inc=1, device_id=(depth, peer), device_id_type=MESH)
    own = pltpu.make_async_copy(tokens_ref.at[me, 0], landed.at[0], load_sem.at[0])
    weight = pltpu.make_async_copy(weight_ref, weight_s, load_sem.at[1])
    own.start()
    weight.start()
    pl.semaphore_wait(barrier, 3)

    def remote(at, k, start, size):
        rows = pl.ds(start, size)
        return pltpu.make_async_remote_copy(
            src_ref=tokens_ref.at[peers[k], 0, rows], dst_ref=landed.at[k, rows],
            send_sem=send_sem.at[at], recv_sem=recv_sem.at[at], device_id=(depth, peers[k]), device_id_type=MESH,
        )

    copies = [remote(k - 1, k, 0, shard) for k in (1, 2, 3)]
    for copy in copies[:2]:
        copy.start()
    loads = [pltpu.make_async_copy(cot_ref.at[peers[k], 0], cot_s.at[k], cot_sem.at[k]) for k in range(4)]
    stores = [
        pltpu.make_async_copy(cot_s.at[k], out, cot_sem.at[k]) for k, out in enumerate((cot0, cot1, cot2, cot3))
    ]
    for copy in loads:
        copy.start()
    bias = row_of(bias_ref)
    bias = jnp.concatenate([bias[:, :features], jnp.zeros((1, features), F32), bias[:, features:]], axis=1)

    def outs(k):
        rows = pl.ds(pl.multiple_of(k * shard, shard), shard)
        pairs = (
            (landed.at[k], row_out), (normed_s.at[rows], normed_out), (projected_s.at[rows], projected_out),
        )
        return [
            pltpu.make_async_copy(src, dst.at[rows], out_sem.at[3 * k + n]) for n, (src, dst) in enumerate(pairs)
        ]

    def body(k, carry):
        @pl.when(k == 0)
        def _():
            own.wait()
            weight.wait()

        @pl.when(k == 1)
        def _():
            for load, store in zip(loads, stores):
                load.wait()
                store.start()
            for copy in copies[:2]:
                copy.wait_send()
            copies[2].start()

        for piece in (1, 2, 3):

            @pl.when(k == piece)
            def _():
                copies[piece - 1].wait_recv()

        unit, _ = unit_norm(landed[k].astype(F32))
        normed = (unit * row_of(gain_ref) + row_of(shift_ref)).astype(BF)
        rows = pl.ds(pl.multiple_of(k * shard, shard), shard)
        normed_s[rows, :] = normed
        projected_s[rows, :] = (dot_plain(normed, weight_s[...]) + bias).astype(BF)
        for copy in outs(k):
            copy.start()
        return carry

    lax.fori_loop(0, 4, body, 0)
    for copy in stores:
        copy.wait()
    for k in range(4):
        for copy in outs(k):
            copy.wait()
    copies[2].wait_send()


def enter(tokens, cotangent, gain, shift, weight, bias):
    _, _, shard, features = tokens.shape
    count, wide = 4 * shard, weight.shape[1]
    shape = jax.ShapeDtypeStruct
    vmem = pl.BlockSpec(memory_space=pltpu.VMEM)
    dma = pltpu.SemaphoreType.DMA
    return pl.pallas_call(
        enter_kernel,
        in_specs=[ANY, ANY, vmem, vmem, ANY, vmem],
        out_specs=[ANY] * 7,
        out_shape=[shape((count, features), BF), shape((count, features), BF), shape((count, wide), BF)]
        + [shape((shard, features), BF)] * 4,
        scratch_shapes=[
            pltpu.VMEM((4, shard, features), BF), pltpu.VMEM(weight.shape, BF), pltpu.VMEM((count, features), BF),
            pltpu.VMEM((count, wide), BF), pltpu.VMEM((4, shard, features), BF),
            dma((3,)), dma((3,)), dma((2,)), dma((4,)), dma((12,)),
        ],
        compiler_params=pltpu.CompilerParams(collective_id=0, has_side_effects=True, vmem_limit_bytes=VMEM_GRANT),
        cost_estimate=pl.CostEstimate(flops=4 * 10**9, bytes_accessed=20 * 2**20, transcendentals=0),
        name="enter",
    )(tokens, cotangent, gain, shift, weight, bias)


def attention_forward_kernel(
    block, q_ref, k_ref, v_ref, miss_ref, own_ref, out_ref, lse_ref, scores_s, weights_s, mixed_s, largest_s
):
    lane = lax.broadcasted_iota(jnp.int32, (1, 128), 1)
    first = lane < 64
    keys, values, own = k_ref[...], v_ref[...], own_ref[...]
    ones = jnp.ones_like(values)
    keys_aug = [jnp.where(first, keys, own), jnp.where(first, own, keys)]
    values_aug = [jnp.where(first, values, ones), jnp.where(first, ones, values)]
    units = [(pl.ds(i * block, block), head) for i in range(q_ref.shape[0] // block) for head in range(2)]

    def score(n):
        rows, head = units[n]
        queries, miss = q_ref[rows, :] * BF(0.125), miss_ref[rows, :]
        queries_aug = jnp.where(first, queries, miss) if head == 0 else jnp.where(first, miss, queries)
        scores_s[n % 2] = dot_rows(queries_aug, keys_aug[head])

    def weigh(n):
        scores = scores_s[n % 2]
        largest = jnp.max(scores, axis=1, keepdims=True)
        weights_s[n % 2] = jnp.exp(scores - largest).astype(BF)
        largest_s[n % 2] = jnp.broadcast_to(largest, largest_s.shape[1:])

    def mix(n):
        rows, head = units[n]
        mixed = dot_plain(weights_s[n % 2], values_aug[head])
        total = mixed[:, 64:65] if head == 0 else mixed[:, 0:1]
        out, log = mixed / total, largest_s[n % 2] + jnp.log(total)
        if head == 0:
            mixed_s[0] = out
            mixed_s[1] = log
        else:
            out_ref[rows, :] = jnp.where(first, mixed_s[0], out).astype(BF)
            lse_ref[0, rows, :] = jnp.where(first, mixed_s[1], log)

    for turn in range(len(units) + 2):
        if turn < len(units):
            score(turn)
        if turn >= 2:
            mix(turn - 2)
        if 1 <= turn <= len(units):
            weigh(turn - 1)


def attention_forward(projected, miss, own, block=256):
    count, width = projected.shape
    pairs = width // 384
    column = lambda base: pl.BlockSpec((count, 128), lambda i: (0, i + base))
    full = pl.BlockSpec((count, 128), lambda i: (0, 0))
    return pl.pallas_call(
        functools.partial(attention_forward_kernel, block),
        grid=(pairs,),
        in_specs=[column(0), column(pairs), column(2 * pairs), full, full],
        out_specs=[column(0), pl.BlockSpec((1, count, 128), lambda i: (i, 0, 0))],
        out_shape=[
            jax.ShapeDtypeStruct((count, width // 3), BF),
            jax.ShapeDtypeStruct((pairs, count, 128), F32),
        ],
        scratch_shapes=[
            pltpu.VMEM((2, block, count), F32), pltpu.VMEM((2, block, count), BF), pltpu.VMEM((2, block, 128), F32),
            pltpu.VMEM((2, block, 128), F32),
        ],
        compiler_params=pltpu.CompilerParams(vmem_limit_bytes=VMEM_GRANT),
        cost_estimate=pl.CostEstimate(flops=24 * 10**9, bytes_accessed=8 * 2**20, transcendentals=12 * 2**20),
        name="attention_forward",
    )(projected, projected, projected, miss, own)


def three_parts(column):
    high = column.astype(BF)
    rest = column - high.astype(F32)
    middle = rest.astype(BF)
    return high, middle, (rest - middle.astype(F32)).astype(BF)


def segment_features(segment):
    lane = jnp.arange(128) % 64
    same = lane[None, :] == segment[:, None]
    live = (lane < 8)[None, :]
    return jnp.where(live & ~same, -BIG, 0.0).astype(BF), jnp.where(live & same, 1.0, 0.0).astype(BF)


def flipped(static, bits):
    total = 0
    for at, bit in enumerate(bits):
        weight = 1 << (len(bits) - 1 - at)
        total = total + weight * ((1 - bit) if static & weight else bit)
    return total


def own_bits(order):
    me, deep = lax.axis_index("seq"), lax.axis_index("dp") // 2
    parts = {"low": [me % 2], "high": [me // 2], "deep": [deep // 2, deep % 2]}
    return [bit for name in order for bit in parts[name]]


def blended(orders, which):
    if len(set(orders)) == 1:
        return own_bits(orders[0])
    last = len(orders) - 1
    total = [0] * 4
    for at, order in enumerate(orders):
        if last == 1:
            here = which if at else 1 - which
        else:
            here = ((2 - which) * (1 - which) // 2, which * (2 - which), which * (which - 1) // 2)[at]
        total = [old + here * bit for old, bit in zip(total, own_bits(order))]
    return total


def scatter_part(out_ref, values, order, part, base=0):
    size = values.shape[0] // 8
    top, *bits = order if isinstance(order, list) else own_bits(order)
    first = 8 * (part + top - 2 * part * top)
    for a in range(8):
        rows = pl.ds(pl.multiple_of((first + flipped(a, bits)) * size, 16), size)
        out_ref[rows, base : base + values.shape[1]] = values[a * size : (a + 1) * size].astype(out_ref.dtype)


def peer_ids():
    me, depth = lax.axis_index("seq"), lax.axis_index("dp")
    high, low = me // 2, me % 2
    core, deep = depth % 2, depth // 2
    upper, lower = deep // 2, deep % 2
    return {
        ("core", 1): (2 * deep + 1 - core, me),
        ("low", 1): (depth, 2 * high + 1 - low),
        ("high", 1): (depth, 2 * (1 - high) + low),
        ("both", 1): (depth, 3 - me),
        ("deep", 1): (2 * (2 * upper + 1 - lower) + core, me),
        ("deep", 2): (2 * (2 * (1 - upper) + lower) + core, me),
        ("deep", 3): (2 * (3 - deep) + core, me),
    }


LOW_FIRST = ("low", "high", "deep")
HIGH_FIRST = ("high", "low", "deep")
DEEP_FIRST = ("deep", "high", "low")
FAN = {"low": 2, "high": 2, "deep": 4}
SEMS = 12


def landing_rows(order, rows):
    sizes = []
    for name in order:
        rows //= FAN[name]
        sizes.append((FAN[name] - 1) * rows)
    return sizes


class Sum:
    def __init__(self, order, rows, send, keep, core_buf, bufs, own, other, send_sems, recv_sems, local_sem):
        self.order, self.rows, self.send, self.keep = order, rows, send, keep
        self.core_buf, self.bufs, self.own, self.other = core_buf, bufs, own, other
        self.send_sems, self.recv_sems, self.local_sem = send_sems, recv_sems, local_sem
        self.sizes = []
        for name in order:
            rows //= FAN[name]
            self.sizes.append(rows)
        self.peers = peer_ids()

    def stage(self, at):
        if at == 0:
            moves = [(self.send, self.core_buf, ("core", 1))]
        elif at <= 3:
            name, size, buf = self.order[at - 1], self.sizes[at - 1], self.bufs[at - 1]
            moves = [
                (self.keep.at[pl.ds(k * size, size)], buf.at[pl.ds((k - 1) * size, size)], (name, k))
                for k in range(1, FAN[name])
            ]
        elif at <= 6:
            name, size = self.order[6 - at], self.sizes[6 - at]
            src = self.keep if at == 4 else self.own
            moves = [
                (src.at[pl.ds(0, size)], self.own.at[pl.ds(k * size, size)], (name, k)) for k in range(1, FAN[name])
            ]
        else:
            moves = [(self.own, self.other, ("core", 1))]
        counts = [1] + [FAN[name] - 1 for name in self.order]
        base = sum((counts + counts[:0:-1])[:at])
        return [
            pltpu.make_async_remote_copy(
                src_ref=src, dst_ref=dst, send_sem=self.send_sems.at[base + k], recv_sem=self.recv_sems.at[base + k],
                device_id=self.peers[peer], device_id_type=MESH,
            )
            for k, (src, dst, peer) in enumerate(moves)
        ]

    def local(self):
        rows = pl.ds(0, self.sizes[2])
        return pltpu.make_async_copy(self.keep.at[rows], self.own.at[rows], self.local_sem)

    def start(self, stage):
        for copy in self.stage(stage):
            copy.start()

    def arrived(self, stage):
        for copy in self.stage(stage):
            copy.wait_recv()

    def left(self, first, last):
        for stage in range(first, last):
            for copy in self.stage(stage):
                copy.wait_send()

    def add(self, start, size, sources):
        chunk = next(rows for rows in (64, 48, 32) if size % rows == 0)

        def body(at, carry):
            rows = lambda base: pl.ds(pl.multiple_of(base + at * chunk, 16), chunk)
            total = self.keep[rows(start), :].astype(F32)
            for buf, offset in sources:
                total = total + buf[rows(offset + start), :].astype(F32)
            self.keep[rows(start), :] = total.astype(self.keep.dtype)
            return carry

        lax.fori_loop(0, size // chunk, body, 0)

    def sources(self, stage):
        if stage == 0:
            return [(self.core_buf, 0)]
        size = self.sizes[stage - 1]
        return [(self.bufs[stage - 1], k * size) for k in range(FAN[self.order[stage - 1]] - 1)]

    def settle(self, stage):
        self.arrived(stage)
        self.add(0, self.rows if stage == 0 else self.sizes[stage - 1], self.sources(stage))

    def tick(self, at, resumed=False):
        if at == 0 or resumed:
            self.start(at)
        elif at <= 3:
            self.arrived(at - 1)
            sources, size = self.sources(at - 1), self.sizes[at - 1]
            self.add(size, (self.rows if at == 1 else self.sizes[at - 2]) - size, sources)
            self.start(at)
            self.add(0, size, sources)
        elif at == 4:
            self.settle(3)
            self.local().start()
            self.start(4)
        elif at <= 7:
            self.arrived(at - 1)
            if at == 5:
                self.local().wait()
            self.start(at)
        else:
            self.arrived(7)


UNITS = 3


def gelu_parts(values):
    size = jnp.abs(values)
    bell = jnp.exp(-0.5 * values * values)
    part = 1.0 / (1.0 + 0.3275911 * 0.7071067811865476 * size)
    series = part * (
        0.127414796
        + part * (-0.142248368 + part * (0.7107068705 + part * (-0.7265760135 + part * 0.5307027145)))
    )
    tail = series * bell
    below = jnp.where(values >= 0, 1.0 - tail, tail)
    return values * below, below + values * (bell * 0.3989422804014327)


FEED_PLAN = {
    (3, 0): [(0, 0)],
    (3, 1): [(0, 1)],
    (5, 0): [(1, 0)],
    (5, 1): [(1, 1), (0, 2)],
    (6, 1): [(1, 2)],
}


def feed_kernel(
    row_ref, att_ref, g0, g1, g2, g3, out_weight_ref, out_bias_ref, gain_ref, shift_ref, fc2_bias_ref,
    w1_ref, bias_ref, w2_ref, *refs
):
    outs, refs = refs[:17], refs[17:]
    results, (branch_out, att_grad_out), sums_out = outs[:4], outs[4:6], outs[6:10]
    last_out, vec_ref = outs[10:16], outs[16]
    (
        n2_s, mid_s, acc_s, back_s, grad_s, hidden_s, hidden_grad_s, result_s, branch_s, att_grad_s,
        d1_s, d2_s, do_s, pre_s, down_s, bias_s, core1, core2, near1, near2, next1, next2, send_sems, recv_sems, load_sems, out_sems,
    ) = refs
    step = pl.program_id(0)
    core = lax.axis_index("dp") % 2
    count = row_ref.shape[0]
    size = w1_ref.shape[1]
    shard = count // 4
    half = do_s.shape[2]
    blocks = [pl.ds(i * shard, shard) for i in range(4)]
    peers = peer_ids()

    def job(unit, which):
        slot = 2 * unit + which
        d, bufs = (d1_s, (core1, near1, next1)) if which == 0 else (d2_s, (core2, near2, next2))
        return Sum(
            (LOW_FIRST, HIGH_FIRST)[which], d.shape[1], d.at[2 * unit], d.at[2 * unit + 1], bufs[0].at[unit],
            [bufs[1].at[unit], bufs[2].at[unit], None], None, None, send_sems.at[slot], recv_sems.at[slot], None,
        )

    def ticks(at, place):
        for unit, tick in FEED_PLAN.get((at, place), []):
            for which in range(2):
                job(unit, which).tick(tick)

    def load(k):
        return pltpu.make_async_copy((g0, g1, g2, g3)[k], grad_s.at[blocks[k]], load_sems.at[k])

    def stores(first, last_store):
        pairs = [(result_s.at[rows], out) for rows, out in zip(blocks, results)]
        pairs += [(branch_s, branch_out), (att_grad_s, att_grad_out)]
        last = 2 * (UNITS - 1)
        pairs += [(d1_s.at[last], last_out[0]), (d1_s.at[last + 1], last_out[1])]
        pairs += [(d2_s.at[last], last_out[2]), (d2_s.at[last + 1], last_out[3])]
        pairs += [(do_s.at[0], last_out[4]), (do_s.at[1], last_out[5])]
        for unit in range(2):
            for which, d in enumerate((d1_s, d2_s)):
                rows = pl.ds(0, d.shape[1] // 4)
                pairs.append((d.at[2 * unit + 1, rows], sums_out[2 * unit + which]))
        return [pltpu.make_async_copy(src, dst, out_sems.at[n]) for n, (src, dst) in enumerate(pairs) if first <= n < last_store]

    @pl.when(step == 0)
    def _():
        barrier = pltpu.get_barrier_semaphore()
        for name in ("core", "low", "high"):
            pl.semaphore_signal(barrier, inc=1, device_id=peers[name, 1], device_id_type=MESH)
        for k in range(4):
            load(k).start()
        vec_ref[...] = jnp.zeros_like(vec_ref)
        for at in range(2 * UNITS):
            bias_s[at : at + 1, :] = bias_ref[at * size : (at + 1) * size].reshape(1, -1)

        def project(i, carry):
            rows = pl.ds(pl.multiple_of(i * shard, shard), shard)
            mid = row_ref[rows, :].astype(F32) + (dot_plain(att_ref[rows, :], out_weight_ref[...]) + row_of(out_bias_ref))
            mid_s[rows, :] = mid
            acc_s[rows, :] = mid + row_of(fc2_bias_ref)
            unit, _ = unit_norm(mid)
            n2_s[rows, :] = (unit * row_of(gain_ref) + row_of(shift_ref)).astype(BF)
            return carry

        lax.fori_loop(0, 4, project, 0)
        back_s[...] = jnp.zeros_like(back_s)
        for k in range(4):
            load(k).wait()

    @pl.when(step == 2)
    def _():
        pl.semaphore_wait(pltpu.get_barrier_semaphore(), 3)

    for at in range(1, 2 * UNITS + 1):
        unit, keeping = (at - 1) // 2, (at - 1) % 2

        @pl.when(step == at)
        def _():
            ticks(at, 0)

    last_step = step == 2 * UNITS

    at_chunk = jnp.maximum(step - 1, 0)
    chunk_row = 2 * (at_chunk // 2) + (core + 1 + at_chunk % 2) % 2

    @pl.when(step > 0)
    def _():
        bias = bias_s[pl.ds(chunk_row, 1), :]

        pre_s[...] = dot_plain(n2_s[...], w1_ref[...]) + bias
        down_s[...] = dot_rows(grad_s[...], w2_ref[...])
        total = jnp.zeros((1, size), F32)
        for rows in blocks:
            hidden, slope = gelu_parts(pre_s[rows, :])
            hidden_grad = (down_s[rows, :] * slope).astype(BF)
            hidden_s[rows, :] = hidden.astype(BF)
            hidden_grad_s[rows, :] = hidden_grad
            total = total + total_rows(hidden_grad.astype(F32))
        acc_s[...] += dot_plain(hidden_s[...], w2_ref[...])
        back_s[...] += dot_rows(hidden_grad_s[...], w1_ref[...])
        vec_ref[pl.ds(4 + chunk_row, 1), 0:size] = total

    @pl.when(last_step)
    def _():
        def body(i, sums):
            rows = pl.ds(pl.multiple_of(i * shard, shard), shard)
            result_s[rows, :] = acc_s[rows, :].astype(BF)
            back = back_s[rows, :]
            unit, inverse = unit_norm(mid_s[rows, :])
            wide = grad_s[rows, :].astype(F32)
            branch = (wide + norm_back(unit, inverse, back, row_of(gain_ref))).astype(BF)
            branch_s[rows, :] = branch
            parts = (back * unit, back, branch.astype(F32), wide)
            return tuple(old + total_rows(part) for old, part in zip(sums, parts))

        sums = lax.fori_loop(0, 4, body, (jnp.zeros((1, n2_s.shape[1]), F32),) * 4)
        for at, part in enumerate(sums):
            vec_ref[at + 10 : at + 11, :] = part
        att_grad_s[...] = dot_rows(branch_s[...], out_weight_ref[...]).astype(BF)
        for copy in stores(0, 6):
            copy.start()

    for at in range(1, 2 * UNITS + 1):

        @pl.when(step == at)
        def _():
            ticks(at, 1)

    @pl.when(step > 0)
    def _():
        wide, narrow = n2_s.shape[1] // 2, size // 2
        order = blended(ORDERS[1:6:2], (step - 1) // 2)
        for part in range(2):
            left = n2_s[:, part * wide : (part + 1) * wide]
            scatter_part(d1_s.at[step - 1], dot_tokens(left, hidden_grad_s[...]), LOW_FIRST, part)
        for part in range(2):
            left = hidden_s[:, part * narrow : (part + 1) * narrow]
            scatter_part(d2_s.at[step - 1], dot_tokens(left, grad_s[...]), order, part)

    @pl.when(last_step)
    def _():
        def body(at, carry):
            slot, part = at // 2, at % 2
            wide = att_ref.shape[1] // 2
            columns = pl.ds(pl.multiple_of(((core + 1 + slot) % 2) * half, 128), half)
            left = att_ref[:, pl.ds(pl.multiple_of(part * wide, 128), wide)]
            scatter_part(do_s.at[slot], dot_tokens(left, branch_s[:, columns]), ORDERS[6], part)
            return carry

        lax.fori_loop(0, 4, body, 0)
        for copy in stores(6, 12):
            copy.start()
        for unit in range(2):
            for which in range(2):
                job(unit, which).settle(2)
        for copy in stores(12, 16):
            copy.start()
        for copy in stores(0, 16):
            copy.wait()
        for unit in range(2):
            for which in range(2):
                job(unit, which).left(0, 3)


def feed(row, attended, grads, out_weight, out_bias, gain, shift, fc1_weight, fc1_bias, fc2_weight, fc2_bias):
    count, features = row.shape
    size = fc1_weight.shape[1] // (2 * UNITS)
    half = features // 2
    shape = jax.ShapeDtypeStruct
    wide, line = once((count, features)), once((features,))
    vmem, dma = pltpu.VMEM, pltpu.SemaphoreType.DMA

    def chunk(i):
        at = jnp.maximum(i - 1, 0)
        return 2 * (at // 2) + (lax.axis_index("dp") % 2 + 1 + at % 2) % 2

    return pl.pallas_call(
        feed_kernel,
        grid=(2 * UNITS + 1,),
        in_specs=[wide, wide] + [ANY] * 4 + [once(out_weight.shape), line, line, line, line]
        + [
            pl.BlockSpec((features, size), lambda i: (0, chunk(i))),
            once(fc1_bias.shape),
            pl.BlockSpec((size, features), lambda i: (chunk(i), 0)),
        ],
        out_specs=[ANY] * 16 + [once((16, features))],
        out_shape=[shape(grads[0].shape, BF)] * 4 + [shape((count, features), BF)] * 2
        + [shape((features // 4, size), BF), shape((size // 4, features), BF)] * 2
        + [shape((features, size), BF)] * 2 + [shape((size, features), BF)] * 2
        + [shape((features, half), BF)] * 2 + [shape((16, features), F32)],
        scratch_shapes=[vmem((count, features), BF)] + [vmem((count, features), F32)] * 3
        + [vmem((count, features), BF), vmem((count, size), BF), vmem((count, size), BF)]
        + [vmem((count, features), BF)] * 3
        + [
            vmem((2 * UNITS, features, size), BF), vmem((2 * UNITS, size, features), BF), vmem((2, features, half), BF),
            vmem((count, size), F32), vmem((count, size), F32), vmem((8, size), F32),
            vmem((2, features, size), BF), vmem((2, size, features), BF),
            vmem((2, features // 2, size), BF), vmem((2, size // 2, features), BF),
            vmem((2, features // 4, size), BF), vmem((2, size // 4, features), BF),
            dma((4, SEMS)), dma((4, SEMS)), dma((4,)), dma((16,)),
        ],
        compiler_params=pltpu.CompilerParams(collective_id=2, has_side_effects=True, vmem_limit_bytes=VMEM_GRANT),
        cost_estimate=pl.CostEstimate(flops=35 * 10**9, bytes_accessed=40 * 2**20, transcendentals=0),
        name="feed",
    )(
        row, attended, *grads, out_weight, out_bias, gain, shift, fc2_bias, fc1_weight, fc1_bias, fc2_weight,
    )


ORDERS = (
    LOW_FIRST, HIGH_FIRST, LOW_FIRST, HIGH_FIRST, LOW_FIRST, HIGH_FIRST, HIGH_FIRST, LOW_FIRST, DEEP_FIRST, HIGH_FIRST,
)
PLAN = {
    (0, 0): [(0, 3)],
    (1, 0): [(4, 0), (1, 3), (5, 0), (6, 0)],
    (1, 1): [(0, 4)],
    (2, 0): [(2, 3), (4, 1), (5, 1), (1, 4), (6, 1)],
    (3, 1): [(3, 3)],
    (4, 0): [(0, 5), (7, 0)],
    (5, 0): [(7, 1), (2, 4), (1, 5)],
    (5, 1): [(4, 2), (3, 4)],
    (7, 0): [(2, 5)],
    (7, 1): [(3, 5), (6, 2), (7, 2), (1, 6)],
    (8, 0): [(8, 0), (0, 6)],
    (9, 0): [(8, 1), (5, 2)],
    (9, 1): [(6, 3), (4, 3), (3, 6)],
    (11, 0): [(7, 3), (2, 6)],
    (11, 1): [(5, 3)],
    (12, 0): [(9, 0)],
    "tail": [
        (9, 1), (0, 7), (6, 4), (1, 7), (4, 4), (7, 4), (3, 7), (2, 7), (5, 4), (9, 2), (8, 2), (6, 5),
        (7, 5), (4, 5), (8, 3), (5, 5), (9, 3), (6, 6), (8, 4), (9, 4), (8, 5), (5, 6), (7, 6), (9, 5),
        (4, 6), (8, 6), (7, 7), (9, 6), (6, 7), (4, 7), (5, 7), (8, 7), (9, 7),
    ],
}
BLOCK_OUT_AT = (0, 0)


def three_parts(column):
    high = column.astype(BF)
    rest = column - high.astype(F32)
    middle = rest.astype(BF)
    return high, middle, (rest - middle.astype(F32)).astype(BF)


def pair_backward(refs, outs, dk_acc, dv_acc, pair, part, block):
    q_ref, k_ref, v_ref, att_ref, grad_ref, lse_ref, miss_ref, own_ref = refs
    lane = lax.broadcasted_iota(jnp.int32, (1, 128), 1)
    first = lane < 64
    half = lane % 64
    keys, values, own = k_ref[...], v_ref[...], own_ref[...]
    unit = jnp.where((half >= 8) & (half < 11), 1.0, 0.0).astype(BF)
    own = own + unit
    unit_rows = jnp.broadcast_to(unit, values.shape)
    keys_aug = [jnp.where(first, keys, own), jnp.where(first, own, keys)]
    values_aug = [jnp.where(first, values, unit_rows), jnp.where(first, unit_rows, values)]
    keys_only = [jnp.where(first, keys, BF(0)), jnp.where(first, BF(0), keys)]

    @pl.when(part == 0)
    def _():
        dk_acc[...] = jnp.zeros_like(dk_acc)
        dv_acc[...] = jnp.zeros_like(dv_acc)

    columns = pl.ds(pl.multiple_of(pair * 128, 128), 128)

    def spread(column):
        high, middle, low = [part.astype(F32) for part in three_parts(-column)]
        wide = jnp.where(half == 8, high, jnp.where(half == 9, middle, jnp.where(half == 10, low, 0.0)))
        return wide.astype(BF)

    def body(step, carry):
        rows = pl.ds(pl.multiple_of(step * block, block), block)
        queries, miss, grad = q_ref[rows, :] * BF(0.125), miss_ref[rows, :], grad_ref[rows, :]
        both = att_ref[rows, :].astype(F32) * grad.astype(F32)
        logs = lse_ref[0, rows, :]
        queries_t, grad_t = queries.T, grad.T
        dq = jnp.zeros((block, 128), F32)
        for head in range(2):
            mine = first if head == 0 else jnp.logical_not(first)
            span = pl.ds(64 * head, 64)
            delta = jnp.sum(jnp.where(mine, both, 0.0), axis=1, keepdims=True)
            total = logs[:, 0:1] if head == 0 else logs[:, 64:65]
            queries_aug = jnp.where(mine, queries, spread(total) + miss)
            grad_aug = jnp.where(mine, grad, spread(delta))
            probs = jnp.exp(dot_rows(queries_aug, keys_aug[head]))
            score_grad = (probs * dot_rows(grad_aug, values_aug[head])).astype(BF)
            dq = dq + dot_plain(score_grad, keys_only[head])
            dk_acc[span, :] += dot_plain(queries_t[64 * head : 64 * head + 64], score_grad)
            dv_acc[span, :] += dot_plain(grad_t[64 * head : 64 * head + 64], probs.astype(BF))
        outs[0][rows, columns] = (dq * 0.125).astype(BF)
        return carry

    steps = q_ref.shape[0] // block // 2
    lax.fori_loop(part * steps, (part + 1) * steps, body, 0)

    @pl.when(part == 1)
    def _():
        outs[1][:, columns] = dk_acc[...].T.astype(BF)
        outs[2][:, columns] = dv_acc[...].T.astype(BF)


def backward_kernel(*refs):
    (
        q_ref, k_ref, v_ref, att_ref, grad_ref, lse_ref, miss_ref, own_ref, normed_ref,
        weight_ref, row_ref, branch_ref, gain_ref, vec_in_ref,
    ) = refs[:14]
    results, sums_in, last_in = refs[14:18], refs[18:22], refs[22:28]
    block_out, tokens_out, vec_out = refs[28:31]
    owns, others = refs[31:41], refs[41:51]
    (
        dq_s, dk_s, dv_s, dk_acc, dv_acc, qkv_s, own_result, grad_s, vec_s, vec_got,
        send_sems, recv_sems, local_sems, load_sems, side_send, side_recv, vec_send, vec_recv,
    ) = refs[51:69]
    held = refs[69:76]
    landing = refs[76:]
    step = pl.program_id(0)
    me, depth = lax.axis_index("seq"), lax.axis_index("dp")
    core = depth % 2
    peers = peer_ids()
    shard = results[0].shape[0]
    features = row_ref.shape[1]

    def job(n):
        sems = send_sems.at[n], recv_sems.at[n], local_sems.at[n]
        if n < 4:
            return Sum(
                ORDERS[n], 4 * held[n].shape[0], None, held[n], None, [None, None, landing[n]], owns[n], others[n], *sems
            )
        send = last_in[2 * (n - 4)] if n < 7 else qkv_s.at[2 * (n - 7)]
        keep = held[n] if n < 7 else qkv_s.at[2 * (n - 7) + 1]
        core_buf, *bufs = landing[4 * (n - 3) : 4 * (n - 2)]
        return Sum(ORDERS[n], keep.shape[0], send, keep, core_buf, bufs, owns[n], others[n], *sems)

    def load(n):
        if n == 7:
            return pltpu.make_async_copy(results[0], own_result, load_sems.at[7])
        src = sums_in[n] if n < 4 else last_in[2 * (n - 4) + 1]
        return pltpu.make_async_copy(src, held[n], load_sems.at[n])

    def store():
        return pltpu.make_async_copy(own_result, block_out.at[me, 0], load_sems.at[7])

    def token_store():
        return pltpu.make_async_copy(grad_s.at[0], tokens_out.at[me, 0], load_sems.at[8])

    kinds = [("low", 1), ("high", 1), ("both", 1)]

    def spread_row(number, k, piece, out):
        return pltpu.make_async_remote_copy(
            src_ref=piece, dst_ref=out.at[me, 0], send_sem=side_send.at[number, k - 1],
            recv_sem=side_recv.at[number, k - 1], device_id=peers[kinds[k - 1]], device_id_type=MESH,
        )

    def block_copy(k):
        return spread_row(0, k, results[k], block_out)

    def token_copy(k):
        return spread_row(1, k, grad_s.at[k], tokens_out)

    vec_names = [[("core", 1)], kinds, [("deep", 1), ("deep", 2), ("deep", 3)]]

    def vec_stage(stage):
        return [
            pltpu.make_async_remote_copy(
                src_ref=vec_s.at[stage], dst_ref=vec_got.at[stage, k],
                send_sem=vec_send.at[stage, k], recv_sem=vec_recv.at[stage, k],
                device_id=peers[name], device_id_type=MESH,
            )
            for k, name in enumerate(vec_names[stage])
        ]

    def vec_step(stage):
        for copy in vec_stage(stage):
            copy.wait_recv()
        total = vec_s[stage]
        for k in range(len(vec_names[stage])):
            total = total + vec_got[stage, k]
        if stage == 2:
            vec_out[...] = total
        else:
            vec_s[stage + 1] = total
            for copy in vec_stage(stage + 1):
                copy.start()

    def ticks(at, place):
        for n, tick in PLAN.get((at, place), []):
            resumed = n < 4 and tick == 3
            if resumed or (4 <= n < 7 and tick == 1):
                load(n).wait()
            job(n).tick(tick, resumed)

    @pl.when(step == 0)
    def _():
        barrier = pltpu.get_barrier_semaphore()
        for peer in peers.values():
            pl.semaphore_signal(barrier, inc=1, device_id=peer, device_id_type=MESH)
        for n in range(8):
            load(n).start()
        pl.semaphore_wait(barrier, len(peers))

    for at in range(13):

        @pl.when(step == at)
        def _():
            if (at, 0) == BLOCK_OUT_AT:
                for k in (1, 2, 3):
                    block_copy(k).start()
            ticks(at, 0)
            if at == 2:
                load(7).wait()
                store().start()

    turn = step // 2
    pair = 2 * (turn // 2) + (core + 1 + turn % 2) % 2

    @pl.when(step < 12)
    def _():
        pair_backward(
            (q_ref, k_ref, v_ref, att_ref, grad_ref, lse_ref, miss_ref, own_ref),
            (dq_s, dk_s, dv_s), dk_acc, dv_acc, pair, step % 2, 256,
        )

    for at in range(1, 12, 2):

        @pl.when(step == at)
        def _():
            if (at, 1) == BLOCK_OUT_AT:
                for k in (1, 2, 3):
                    block_copy(k).start()
            ticks(at, 1)

    @pl.when((step < 12) & (step % 2 == 1))
    def _():
        columns = pl.ds(pl.multiple_of(pair * 128, 128), 128)
        grads = jnp.concatenate([part[:, columns] for part in (dq_s, dk_s, dv_s)], axis=1)
        vec_out[2:3, columns] = total_rows(grads[:, :128].astype(F32))
        vec_out[3:4, columns] = total_rows(grads[:, 256:].astype(F32))

        def body(part, carry):
            left = normed_ref[:, pl.ds(pl.multiple_of(part * (features // 2), 128), features // 2)]
            scatter_part(qkv_s.at[turn], dot_tokens(left, grads), blended(ORDERS[7:10], turn // 2), part)
            return carry

        lax.fori_loop(0, 2, body, 0)

    @pl.when(step == 12)
    def _():
        def body(at, sums):
            k = 3 - at
            rows = pl.ds(pl.multiple_of(k * shard, shard), shard)
            back = dot_rows(dq_s[rows, :], weight_ref[:, :features])
            back = back + dot_rows(dk_s[rows, :], weight_ref[:, features : 2 * features])
            back = back + dot_rows(dv_s[rows, :], weight_ref[:, 2 * features :])
            unit, inverse = unit_norm(row_ref[rows, :].astype(F32))
            grad_s[k] = (branch_ref[rows, :].astype(F32) + norm_back(unit, inverse, back, row_of(gain_ref))).astype(BF)
            for piece in range(4):

                @pl.when(k == piece)
                def _():
                    if piece:
                        token_copy(piece).start()
                    else:
                        token_store().start()

            return tuple(old + total_rows(part) for old, part in zip(sums, (back * unit, back)))

        gain_sum, shift_sum = lax.fori_loop(0, 4, body, (jnp.zeros((1, features), F32),) * 2)
        vec_s[0] = vec_in_ref[...]
        vec_s[0, 0:1, :] = gain_sum
        vec_s[0, 1:2, :] = shift_sum
        vec_s[0, 2:4, :] = vec_out[2:4, :]
        vec_stage(0)[0].start()

    @pl.when(step == 13)
    def _():
        for index, (n, tick) in enumerate(PLAN["tail"]):
            if index in (3, 8, 13):
                vec_step((index - 3) // 5)
            job(n).tick(tick)
        for n in range(10):
            job(n).arrived(7)
        for n in range(10):
            job(n).left(3 if n < 4 else 0, 8)
        store().wait()
        token_store().wait()
        for k in (1, 2, 3):
            block_copy(k).wait()
            token_copy(k).wait()
        for stage in range(3):
            for copy in vec_stage(stage):
                copy.wait_send()


def backward(
    projected, attended, attended_grad, logs, miss, own, normed, qkv_weight, row, branch, gain, vec_in,
    results, sums_in, last_in,
):
    count, width = projected.shape
    features = width // 3
    pairs = width // 384
    half = features // 2
    shard = count // 4

    def pair(i):
        at = jnp.minimum(i // 2, 5)
        return 2 * (at // 2) + (lax.axis_index("dp") % 2 + 1 + at % 2) % 2

    column = lambda base: pl.BlockSpec((count, 128), lambda i: (0, pair(i) + base))
    shape = jax.ShapeDtypeStruct
    wide = once((count, features))
    full = once((count, 128))
    vmem, dma = pltpu.VMEM, pltpu.SemaphoreType.DMA
    sizes = [last_in[0].shape, last_in[2].shape] * UNITS + [(features, half)] * 4
    held = [vmem(array.shape, BF) for array in (*sums_in, *last_in[1::2])]
    landing = []
    for n, (rows, columns) in enumerate(sizes):
        lands = landing_rows(ORDERS[n], rows)
        landing += [vmem((lands[2], columns), BF)] if n < 4 else [vmem((size, columns), BF) for size in [rows] + lands]
    return pl.pallas_call(
        backward_kernel,
        grid=(14,),
        in_specs=[
            column(0), column(pairs), column(2 * pairs), column(0), column(0),
            pl.BlockSpec((1, count, 128), lambda i: (pair(i), 0, 0)),
            full, full, wide, once(qkv_weight.shape), wide, wide, once((features,)), once((16, features)),
        ]
        + [ANY] * 14,
        out_specs=[ANY, ANY, once((16, features))] + [ANY] * 20,
        out_shape=[shape((4, 1, shard, features), BF)] * 2 + [shape((16, features), F32)]
        + [shape(size, BF) for size in sizes] * 2,
        scratch_shapes=[vmem((count, features), BF)] * 3
        + [vmem((128, count), F32)] * 2
        + [vmem((6, features, half), BF)]
        + [
            vmem((shard, features), BF), vmem((4, shard, features), BF),
            vmem((3, 16, features), F32), vmem((3, 3, 16, features), F32),
            dma((10, SEMS)), dma((10, SEMS)), dma((10,)), dma((9,)), dma((2, 3)), dma((2, 3)), dma((3, 3)), dma((3, 3)),
        ]
        + held + landing,
        compiler_params=pltpu.CompilerParams(collective_id=1, has_side_effects=True, vmem_limit_bytes=VMEM_GRANT),
        cost_estimate=pl.CostEstimate(flops=60 * 10**9, bytes_accessed=60 * 2**20, transcendentals=12 * 2**20),
        name="backward",
    )(
        projected, projected, projected, attended, attended_grad, logs, miss, own, normed, qkv_weight, row, branch,
        gain, vec_in, *results, *sums_in, *last_in,
    )


STEPS = 8


def own_group(order):
    total = 0
    for bit in own_bits(order):
        total = 2 * total + bit
    return total


def assemble_kernel(*refs):
    ins, vec_ref = refs[:20], refs[20]
    d1_ref, d2_ref, out_ref, qkv_ref = refs[21:25]
    vecs = refs[25:]
    core = lax.axis_index("dp") % 2
    features = out_ref.shape[1]
    size = ins[0].shape[1]
    half = features // 2

    def ordered(n):
        ref, last = ins[n], own_bits(ORDERS[n // 2])[3]
        rows = ref.shape[0] // 2
        return jnp.concatenate(
            [ref[pl.ds(pl.multiple_of((a + last - 2 * a * last) * rows, 16), rows), :] for a in range(2)], axis=0
        ).astype(F32)

    for side in range(2):
        home = core if side == 0 else 1 - core
        for unit in range(UNITS):
            columns = pl.ds(pl.multiple_of((2 * unit + home) * size, 128), size)
            d1_ref[:, columns] = ordered(4 * unit + side)
            d2_ref[unit, home] = ordered(4 * unit + 2 + side)
        out_ref[:, pl.ds(pl.multiple_of(home * half, 128), half)] = ordered(12 + side)
        for group in range(3):
            values = ordered(14 + 2 * group + side)
            for part in range(3):
                at = part * features + (2 * group + home) * 128
                qkv_ref[:, pl.ds(pl.multiple_of(at, 128), 128)] = values[:, part * 128 : (part + 1) * 128]

    @pl.when(pl.program_id(0) == 0)
    def _():
        for ref, row in zip(vecs, (0, 1, 12, 10, 11, 13)):
            ref[...] = vec_ref[row, :]
        qv_ref, fc1_ref = vecs[6:]
        for at in range(2):
            qv_ref[at * features : (at + 1) * features] = vec_ref[2 + at, :]
        for at in range(2 * UNITS):
            fc1_ref[at * size : (at + 1) * size] = vec_ref[4 + at, 0:size]


def assemble(parts, vector):
    features, size = parts[0].shape
    half = features // 2
    wide = 2 * UNITS * size
    shape = jax.ShapeDtypeStruct

    def spec(n):
        rows, columns = parts[n].shape
        return pl.BlockSpec((rows // STEPS, columns), lambda i: (i ^ (own_group(ORDERS[n // 2]) // 2), 0))

    lines = [features] * 6 + [2 * features, wide]
    d1, d2, out, qkv, *vecs = pl.pallas_call(
        assemble_kernel,
        grid=(STEPS,),
        in_specs=[spec(n) for n in range(20)] + [once(vector.shape)],
        out_specs=[
            pl.BlockSpec((features // STEPS, wide), lambda i: (i, 0)),
            pl.BlockSpec((UNITS, 2, size // STEPS, features), lambda i: (0, 0, i, 0)),
            pl.BlockSpec((features // STEPS, features), lambda i: (i, 0)),
            pl.BlockSpec((features // STEPS, 3 * features), lambda i: (i, 0)),
        ]
        + [once((line,)) for line in lines],
        out_shape=[
            shape((features, wide), F32), shape((UNITS, 2, size, features), F32), shape((features, features), F32),
            shape((features, 3 * features), F32),
        ]
        + [shape((line,), F32) for line in lines],
        compiler_params=pltpu.CompilerParams(vmem_limit_bytes=VMEM_GRANT),
        cost_estimate=pl.CostEstimate(flops=0, bytes_accessed=45 * 2**20, transcendentals=0),
        name="assemble",
    )(*parts, vector)
    return d1, d2.reshape(wide, features), out, qkv, vecs


def swap(array, axis, bit):
    count = lax.axis_size(axis)
    return lax.ppermute(array, axis, [(i, i ^ bit) for i in range(count)])


def fast_shards(
    tokens, image_lengths, cotangent, attn_gain, attn_shift, qkv_weight, qv_bias, out_weight,
    out_bias, mlp_gain, mlp_shift, fc1_weight, fc1_bias, fc2_weight, fc2_bias,
):
    shard_len = tokens.shape[2]
    parties = lax.axis_size("seq")
    row_len = shard_len * parties
    images = image_lengths.shape[2] - 1
    me = lax.axis_index("seq")

    row, normed, projected, *cots = enter(tokens, cotangent, attn_gain, attn_shift, qkv_weight, qv_bias)
    seg_row = segment_ids(lax.dynamic_index_in_dim(image_lengths, me, 0, keepdims=False), row_len, images)
    seg_row = seg_row.reshape(parties, shard_len)
    segment = jnp.concatenate([seg_row[me ^ k] for k in range(parties)], axis=0)
    miss, own = segment_features(segment)
    attended, logs = attention_forward(projected, miss, own)
    grads = [cots[0]] + [swap(cots[k], "seq", k) for k in (1, 2, 3)]
    fed = feed(
        row, attended, grads, out_weight, out_bias, mlp_gain, mlp_shift, fc1_weight, fc1_bias, fc2_weight, fc2_bias
    )
    results, (branch, attended_grad), sums, last, vec = fed[:4], fed[4:6], fed[6:10], fed[10:16], fed[16]
    block_out, tokens_grad, vector, *summed = backward(
        projected, attended, attended_grad, logs, miss, own, normed, qkv_weight, row, branch, attn_gain, vec,
        results, sums, last,
    )
    paired = [part for n in range(10) for part in (summed[n], summed[10 + n])]
    fc1_grad, fc2_grad, out_grad, qkv_grad, vecs = assemble(paired, vector)
    gain, shift, out_sum, mlp_gain_sum, mlp_shift_sum, fc2_sum, qv_sum, fc1_sum = vecs
    return (
        block_out, tokens_grad, gain, shift, qkv_grad, qv_sum, out_grad, out_sum, mlp_gain_sum, mlp_shift_sum,
        fc1_grad, fc1_sum, fc2_grad, fc2_sum,
    )


def shards(tokens, *rest):
    micro_count, row_count, shard_len, features = tokens.shape
    whole_rows = micro_count == 4 and row_count == 1 and shard_len % 128 == 0
    sizes = lax.axis_size("dp") == 8 and lax.axis_size("seq") == 4
    hidden = rest[10].shape[1]
    if sizes and whole_rows and features == 64 * HEADS == 768 and hidden == 4 * features:
        return fast_shards(tokens, *rest)
    return general_shards(tokens, *rest)


def solution(mesh):
    placed = (
        P(None, "dp", "seq", None),
        P(None, "dp", None),
        P(None, "dp", "seq", None),
        P(),
        P(),
        P(),
        P(),
        P(),
        P(),
        P(),
        P(),
        P(),
        P(),
        P(),
        P(),
    )
    return jax.shard_map(
        shards,
        mesh=mesh,
        in_specs=placed,
        out_specs=(
            P(None, "dp", "seq", None),
            P(None, "dp", "seq", None),
            P(),
            P(),
            P(),
            P(),
            P(),
            P(),
            P(),
            P(),
            P(),
            P(),
            P(),
            P(),
        ),
        check_vma=False,
    )
```

```python
import functools

import jax
import jax.numpy as jnp
from jax import lax
from jax.experimental import pallas as pl
from jax.experimental.pallas import tpu as pltpu
from jax.sharding import PartitionSpec as P

HEADS = 12


EPS = 1e-06
NEG = -1e30


def layer_norm(values, scale_row, shift_row):
    center = values - jnp.mean(values, axis=-1, keepdims=True)
    spread = jnp.mean(center * center, axis=-1, keepdims=True)
    return center * lax.rsqrt(spread + EPS) * scale_row + shift_row


def gelu_exact(values):
    return jax.nn.gelu(values, approximate=False)


def segment_ids(lengths, row_len, images):
    positions = jnp.arange(row_len, dtype=jnp.int32)
    ends = jnp.cumsum(lengths, axis=-1) + 2 * images
    patches = jnp.sum((positions[:, None] >= ends[..., None, :]).astype(jnp.int32), axis=-1)
    return jnp.where(positions < 2 * images, positions // 2, patches)


def matmul(first_op, second_op, pattern):
    return jnp.einsum(pattern, first_op, second_op, preferred_element_type=jnp.float32)


def general_shards(
    tokens,
    image_lengths,
    cotangent,
    attn_gain,
    attn_shift,
    qkv_weight,
    qv_bias,
    out_weight,
    out_bias,
    mlp_gain,
    mlp_shift,
    fc1_weight,
    fc1_bias,
    fc2_weight,
    fc2_bias,
):
    micro_count, row_count, shard_len, features = tokens.shape
    row_len = shard_len * lax.axis_size("seq")
    images = image_lengths.shape[2] - 1
    head_dim = features // HEADS
    score_scale = head_dim ** (-0.5)
    offset = lax.axis_index("seq") * shard_len
    tok_count = row_count * shard_len
    zero_keys = jnp.zeros((features,), jnp.float32)
    full_bias = jnp.concatenate([qv_bias[:features], zero_keys, qv_bias[features:]])
    totals = [
        jnp.zeros(weight.shape, jnp.float32)
        for weight in (
            attn_gain,
            attn_shift,
            qkv_weight,
            qv_bias,
            out_weight,
            out_bias,
            mlp_gain,
            mlp_shift,
            fc1_weight,
            fc1_bias,
            fc2_weight,
            fc2_bias,
        )
    ]
    outputs_list = []
    grads_list = []
    for micro_step in range(micro_count):
        inputs = tokens[micro_step].astype(jnp.float32)
        seg_all = segment_ids(image_lengths[micro_step], row_len, images)
        seg_here = lax.dynamic_slice_in_dim(seg_all, offset, shard_len, 1)
        allowed = seg_here[:, None, :, None] == seg_all[:, None, None, :]
        normed, first_pull = jax.vjp(layer_norm, inputs, attn_gain, attn_shift)
        normed_low = normed.astype(jnp.bfloat16).reshape(tok_count, features)
        projected = (matmul(normed_low, qkv_weight, "td,de->te") + full_bias).astype(jnp.bfloat16)
        projected = projected.reshape(row_count, shard_len, 3 * features)
        queries = projected[:, :, :features].reshape(row_count, shard_len, HEADS, head_dim)
        keys_all, values_all = (
            lax.all_gather(projected[:, :, features : 2 * features], "seq", axis=1, tiled=True),
            lax.all_gather(projected[:, :, 2 * features :], "seq", axis=1, tiled=True),
        )
        keys_all = keys_all.reshape(row_count, row_len, HEADS, head_dim)
        values_all = values_all.reshape(row_count, row_len, HEADS, head_dim)
        scores = jnp.where(allowed, matmul(queries, keys_all, "rqhd,rkhd->rhqk") * score_scale, NEG)
        largest = jnp.max(scores, axis=-1, keepdims=True)
        log_total = largest + jnp.log(jnp.sum(jnp.exp(scores - largest), axis=-1, keepdims=True))
        weights_low = jnp.exp(scores - log_total).astype(jnp.bfloat16)
        attended = (
            matmul(weights_low, values_all, "rhqk,rkhd->rqhd")
            .astype(jnp.bfloat16)
            .reshape(tok_count, features)
        )
        branch = matmul(attended, out_weight, "td,de->te") + out_bias
        middle = inputs + branch.reshape(inputs.shape)
        normed_two, second_pull = jax.vjp(layer_norm, middle, mlp_gain, mlp_shift)
        normed_two_low = normed_two.astype(jnp.bfloat16).reshape(tok_count, features)
        hidden_pre = matmul(normed_two_low, fc1_weight, "td,df->tf") + fc1_bias
        hidden, gelu_pull = jax.vjp(gelu_exact, hidden_pre)
        hidden_low = hidden.astype(jnp.bfloat16)
        result = middle + (matmul(hidden_low, fc2_weight, "tf,fd->td") + fc2_bias).reshape(
            inputs.shape
        )
        outputs_list.append(result.astype(jnp.bfloat16))
        incoming = cotangent[micro_step].reshape(tok_count, features)
        fc2_weight_part = matmul(hidden_low, incoming, "tf,td->fd")
        fc2_bias_part = jnp.sum(incoming.astype(jnp.float32), axis=0)
        hidden_grad = gelu_pull(matmul(incoming, fc2_weight, "td,fd->tf"))[0].astype(jnp.bfloat16)
        fc1_weight_part = matmul(normed_two_low, hidden_grad, "td,tf->df")
        fc1_bias_part = jnp.sum(hidden_grad.astype(jnp.float32), axis=0)
        back_two = matmul(hidden_grad, fc1_weight, "tf,df->td").reshape(inputs.shape)
        middle_norm, mlp_gain_part, mlp_shift_part = second_pull(back_two)
        middle_grad = incoming.astype(jnp.float32).reshape(inputs.shape) + middle_norm
        branch_grad = middle_grad.astype(jnp.bfloat16).reshape(tok_count, features)
        out_weight_part = matmul(attended, branch_grad, "td,te->de")
        out_bias_part = jnp.sum(branch_grad.astype(jnp.float32), axis=0)
        attended_grad = matmul(branch_grad, out_weight, "te,de->td").astype(jnp.bfloat16)
        attended_grad = attended_grad.reshape(row_count, shard_len, HEADS, head_dim)
        scores_again = jnp.where(
            allowed, matmul(queries, keys_all, "rqhd,rkhd->rhqk") * score_scale, NEG
        )
        chances = jnp.exp(scores_again - log_total)
        chances_low = chances.astype(jnp.bfloat16)
        chance_grad = matmul(attended_grad, values_all, "rqhd,rkhd->rhqk")
        row_delta = jnp.sum(chances * chance_grad, axis=-1, keepdims=True)
        score_grad = (chances * (chance_grad - row_delta)).astype(jnp.bfloat16)
        query_grad = matmul(score_grad, keys_all, "rhqk,rkhd->rqhd") * score_scale
        key_terms = matmul(score_grad, queries, "rhqk,rqhd->rkhd") * score_scale
        value_terms = matmul(chances_low, attended_grad, "rhqk,rqhd->rkhd")
        key_grad, value_grad = (
            lax.psum_scatter(
                key_terms.reshape(row_count, row_len, features).astype(jnp.bfloat16),
                "seq",
                scatter_dimension=1,
                tiled=True,
            ).astype(jnp.float32),
            lax.psum_scatter(
                value_terms.reshape(row_count, row_len, features).astype(jnp.bfloat16),
                "seq",
                scatter_dimension=1,
                tiled=True,
            ).astype(jnp.float32),
        )
        projected_grad = jnp.concatenate(
            [query_grad.reshape(row_count, shard_len, features), key_grad, value_grad], axis=-1
        )
        projected_grad = projected_grad.astype(jnp.bfloat16).reshape(tok_count, 3 * features)
        qkv_weight_part = matmul(normed_low, projected_grad, "td,te->de")
        bias_sums = jnp.sum(projected_grad.astype(jnp.float32), axis=0)
        qv_bias_part = jnp.concatenate([bias_sums[:features], bias_sums[2 * features :]])
        back_one = matmul(projected_grad, qkv_weight, "te,de->td").reshape(inputs.shape)
        inputs_norm, attn_gain_part, attn_shift_part = first_pull(back_one)
        grads_list.append((middle_grad + inputs_norm).astype(jnp.bfloat16))
        pieces = (
            attn_gain_part,
            attn_shift_part,
            qkv_weight_part,
            qv_bias_part,
            out_weight_part,
            out_bias_part,
            mlp_gain_part,
            mlp_shift_part,
            fc1_weight_part,
            fc1_bias_part,
            fc2_weight_part,
            fc2_bias_part,
        )
        totals = [running + member for running, member in zip(totals, pieces)]
    (
        attn_gain_sum,
        attn_shift_sum,
        qkv_weight_sum,
        qv_bias_sum,
        out_weight_sum,
        out_bias_sum,
        mlp_gain_sum,
        mlp_shift_sum,
        fc1_weight_sum,
        fc1_bias_sum,
        fc2_weight_sum,
        fc2_bias_sum,
    ) = totals
    summed = lax.psum(
        (
            attn_gain_sum,
            attn_shift_sum,
            qkv_weight_sum,
            qv_bias_sum,
            out_weight_sum,
            out_bias_sum,
            mlp_gain_sum,
            mlp_shift_sum,
            fc1_weight_sum,
            fc1_bias_sum,
            fc2_weight_sum,
            fc2_bias_sum,
        ),
        ("dp", "seq"),
    )
    return (jnp.stack(outputs_list), jnp.stack(grads_list)) + tuple(summed)

F32 = jnp.float32
BF = jnp.bfloat16
BIG = 1e30
MESH = pl.DeviceIdType.MESH
VMEM_GRANT = 60 * 2**20
ANY = pl.BlockSpec(memory_space=pl.ANY)


def dot_rows(first_op, second_op):
    return lax.dot_general(first_op, second_op, (((1,), (1,)), ((), ())), preferred_element_type=F32)


def dot_plain(first_op, second_op):
    return lax.dot_general(first_op, second_op, (((1,), (0,)), ((), ())), preferred_element_type=F32)


def dot_tokens(first_op, second_op):
    return lax.dot_general(first_op, second_op, (((0,), (0,)), ((), ())), preferred_element_type=F32)


def once(shape, index=None):
    place = index if index is not None else (lambda *_: (0,) * len(shape))
    return pl.BlockSpec(shape, place, pipeline_mode=pl.Buffered(1))


def total_rows(array):
    return jnp.sum(array, axis=0, keepdims=True)


def unit_norm(values):
    center = values - jnp.mean(values, axis=-1, keepdims=True)
    inverse = lax.rsqrt(jnp.mean(center * center, axis=-1, keepdims=True) + EPS)
    return center * inverse, inverse


def norm_back(unit, inverse, incoming, gain):
    scaled = incoming * gain
    return inverse * (
        scaled
        - jnp.mean(scaled, axis=-1, keepdims=True)
        - unit * jnp.mean(scaled * unit, axis=-1, keepdims=True)
    )


def row_of(ref):
    return ref[...].reshape(1, -1)


def enter_kernel(
    tokens_ref, gain_ref, shift_ref, weight_ref, bias_ref,
    row_out, normed_out, projected_out,
    landed, weight_s, normed_s, projected_s, send_sem, recv_sem, load_sem, out_sem,
):
    me, depth = lax.axis_index("seq"), lax.axis_index("dp")
    high, low = me // 2, me % 2
    peers = [me, 2 * high + 1 - low, 2 * (1 - high) + low, 3 - me]
    shard, features = landed.shape[1:]
    barrier = pltpu.get_barrier_semaphore()
    for peer in peers[1:]:
        pl.semaphore_signal(barrier, inc=1, device_id=(depth, peer), device_id_type=MESH)
    own = pltpu.make_async_copy(tokens_ref.at[me, 0], landed.at[0], load_sem.at[0])
    weight = pltpu.make_async_copy(weight_ref, weight_s, load_sem.at[1])
    own.start()
    weight.start()
    pl.semaphore_wait(barrier, 3)

    def remote(at, k, start, size):
        rows = pl.ds(start, size)
        return pltpu.make_async_remote_copy(
            src_ref=tokens_ref.at[peers[k], 0, rows], dst_ref=landed.at[k, rows],
            send_sem=send_sem.at[at], recv_sem=recv_sem.at[at], device_id=(depth, peers[k]), device_id_type=MESH,
        )

    copies = [remote(k - 1, k, 0, shard) for k in (1, 2, 3)]
    for copy in copies[:2]:
        copy.start()
    bias = row_of(bias_ref)
    bias = jnp.concatenate([bias[:, :features], jnp.zeros((1, features), F32), bias[:, features:]], axis=1)

    def outs(k):
        rows = pl.ds(pl.multiple_of(k * shard, shard), shard)
        pairs = (
            (landed.at[k], row_out), (normed_s.at[rows], normed_out), (projected_s.at[rows], projected_out),
        )
        return [
            pltpu.make_async_copy(src, dst.at[rows], out_sem.at[3 * k + n]) for n, (src, dst) in enumerate(pairs)
        ]

    def body(k, carry):
        @pl.when(k == 0)
        def _():
            own.wait()
            weight.wait()

        @pl.when(k == 1)
        def _():
            for copy in copies[:2]:
                copy.wait_send()
            copies[2].start()

        for piece in (1, 2, 3):

            @pl.when(k == piece)
            def _():
                copies[piece - 1].wait_recv()

        unit, _ = unit_norm(landed[k].astype(F32))
        normed = (unit * row_of(gain_ref) + row_of(shift_ref)).astype(BF)
        rows = pl.ds(pl.multiple_of(k * shard, shard), shard)
        normed_s[rows, :] = normed
        projected_s[rows, :] = (dot_plain(normed, weight_s[...]) + bias).astype(BF)
        for copy in outs(k):
            copy.start()
        return carry

    lax.fori_loop(0, 4, body, 0)
    for k in range(4):
        for copy in outs(k):
            copy.wait()
    copies[2].wait_send()


def enter(tokens, gain, shift, weight, bias):
    _, _, shard, features = tokens.shape
    count, wide = 4 * shard, weight.shape[1]
    shape = jax.ShapeDtypeStruct
    vmem = pl.BlockSpec(memory_space=pltpu.VMEM)
    dma = pltpu.SemaphoreType.DMA
    return pl.pallas_call(
        enter_kernel,
        in_specs=[ANY, vmem, vmem, ANY, vmem],
        out_specs=[ANY] * 3,
        out_shape=[shape((count, features), BF), shape((count, features), BF), shape((count, wide), BF)],
        scratch_shapes=[
            pltpu.VMEM((4, shard, features), BF), pltpu.VMEM(weight.shape, BF), pltpu.VMEM((count, features), BF),
            pltpu.VMEM((count, wide), BF),
            dma((3,)), dma((3,)), dma((2,)), dma((12,)),
        ],
        compiler_params=pltpu.CompilerParams(collective_id=0, has_side_effects=True, vmem_limit_bytes=VMEM_GRANT),
        cost_estimate=pl.CostEstimate(flops=4 * 10**9, bytes_accessed=20 * 2**20, transcendentals=0),
        name="enter",
    )(tokens, gain, shift, weight, bias)


def attention_forward_kernel(
    block, q_ref, k_ref, v_ref, miss_ref, own_ref, cot_ref, out_ref, lse_ref, grad_out,
    scores_s, weights_s, mixed_s, largest_s, piece_s, send_sem, recv_sem, own_sem,
):
    step = pl.program_id(0)
    me = lax.axis_index("seq")
    peers = peer_ids()
    kinds = [("low", 1), ("high", 1), ("both", 1)]
    shard = piece_s.shape[0]

    def exchange():
        return [
            pltpu.make_async_remote_copy(
                src_ref=cot_ref.at[peers[name][1], 0], dst_ref=grad_out.at[pl.ds((k + 1) * shard, shard)],
                send_sem=send_sem.at[k], recv_sem=recv_sem.at[k], device_id=peers[name], device_id_type=MESH,
            )
            for k, name in enumerate(kinds)
        ]

    def load():
        return pltpu.make_async_copy(cot_ref.at[me, 0], piece_s, own_sem)

    def store():
        return pltpu.make_async_copy(piece_s, grad_out.at[pl.ds(0, shard)], own_sem)

    @pl.when(step == 0)
    def _():
        barrier = pltpu.get_barrier_semaphore()
        for name in kinds:
            pl.semaphore_signal(barrier, inc=1, device_id=peers[name], device_id_type=MESH)
        load().start()
        pl.semaphore_wait(barrier, 3)
        for copy in exchange():
            copy.start()

    @pl.when(step == 1)
    def _():
        load().wait()
        store().start()

    lane = lax.broadcasted_iota(jnp.int32, (1, 128), 1)
    first = lane < 64
    keys, values, own = k_ref[...], v_ref[...], own_ref[...]
    ones = jnp.ones_like(values)
    keys_aug = [jnp.where(first, keys, own), jnp.where(first, own, keys)]
    values_aug = [jnp.where(first, values, ones), jnp.where(first, ones, values)]
    units = [(pl.ds(i * block, block), head) for i in range(q_ref.shape[0] // block) for head in range(2)]

    def score(n):
        rows, head = units[n]
        queries, miss = q_ref[rows, :] * BF(0.125), miss_ref[rows, :]
        queries_aug = jnp.where(first, queries, miss) if head == 0 else jnp.where(first, miss, queries)
        scores_s[n % 2] = dot_rows(queries_aug, keys_aug[head])

    def weigh(n):
        scores = scores_s[n % 2]
        largest = jnp.max(scores, axis=1, keepdims=True)
        weights_s[n % 2] = jnp.exp(scores - largest).astype(BF)
        largest_s[n % 2] = jnp.broadcast_to(largest, largest_s.shape[1:])

    def mix(n):
        rows, head = units[n]
        mixed = dot_plain(weights_s[n % 2], values_aug[head])
        total = mixed[:, 64:65] if head == 0 else mixed[:, 0:1]
        out, log = mixed / total, largest_s[n % 2] + jnp.log(total)
        if head == 0:
            mixed_s[0] = out
            mixed_s[1] = log
        else:
            out_ref[rows, :] = jnp.where(first, mixed_s[0], out).astype(BF)
            lse_ref[0, rows, :] = jnp.where(first, mixed_s[1], log)

    for turn in range(len(units) + 2):
        if turn < len(units):
            score(turn)
        if turn >= 2:
            mix(turn - 2)
        if 1 <= turn <= len(units):
            weigh(turn - 1)

    @pl.when(step == pl.num_programs(0) - 1)
    def _():
        store().wait()
        for copy in exchange():
            copy.wait()


def attention_forward(projected, miss, own, cotangent, block=256):
    count, width = projected.shape
    pairs = width // 384
    column = lambda base: pl.BlockSpec((count, 128), lambda i: (0, i + base))
    full = pl.BlockSpec((count, 128), lambda i: (0, 0))
    return pl.pallas_call(
        functools.partial(attention_forward_kernel, block),
        grid=(pairs,),
        in_specs=[column(0), column(pairs), column(2 * pairs), full, full, ANY],
        out_specs=[column(0), pl.BlockSpec((1, count, 128), lambda i: (i, 0, 0)), ANY],
        out_shape=[
            jax.ShapeDtypeStruct((count, width // 3), BF),
            jax.ShapeDtypeStruct((pairs, count, 128), F32),
            jax.ShapeDtypeStruct((count, width // 3), BF),
        ],
        scratch_shapes=[
            pltpu.VMEM((2, block, count), F32), pltpu.VMEM((2, block, count), BF), pltpu.VMEM((2, block, 128), F32),
            pltpu.VMEM((2, block, 128), F32), pltpu.VMEM((count // 4, width // 3), BF), pltpu.SemaphoreType.DMA((3,)),
            pltpu.SemaphoreType.DMA((3,)), pltpu.SemaphoreType.DMA,
        ],
        compiler_params=pltpu.CompilerParams(collective_id=3, has_side_effects=True, vmem_limit_bytes=VMEM_GRANT),
        cost_estimate=pl.CostEstimate(flops=24 * 10**9, bytes_accessed=8 * 2**20, transcendentals=12 * 2**20),
        name="attention_forward",
    )(projected, projected, projected, miss, own, cotangent)


def three_parts(column):
    high = column.astype(BF)
    rest = column - high.astype(F32)
    middle = rest.astype(BF)
    return high, middle, (rest - middle.astype(F32)).astype(BF)


def segment_features(segment):
    lane = jnp.arange(128) % 64
    same = lane[None, :] == segment[:, None]
    live = (lane < 8)[None, :]
    return jnp.where(live & ~same, -BIG, 0.0).astype(BF), jnp.where(live & same, 1.0, 0.0).astype(BF)


def flipped(static, bits):
    total = 0
    for at, bit in enumerate(bits):
        weight = 1 << (len(bits) - 1 - at)
        total = total + weight * ((1 - bit) if static & weight else bit)
    return total


def own_bits(order):
    me, deep = lax.axis_index("seq"), lax.axis_index("dp") // 2
    parts = {"low": [me % 2], "high": [me // 2], "deep": [deep // 2, deep % 2]}
    return [bit for name in order for bit in parts[name]]


def blended(orders, which):
    if len(set(orders)) == 1:
        return own_bits(orders[0])
    last = len(orders) - 1
    total = [0] * 4
    for at, order in enumerate(orders):
        if last == 1:
            here = which if at else 1 - which
        else:
            here = ((2 - which) * (1 - which) // 2, which * (2 - which), which * (which - 1) // 2)[at]
        total = [old + here * bit for old, bit in zip(total, own_bits(order))]
    return total


def scatter_part(out_ref, values, order, part, base=0):
    size = values.shape[0] // 8
    top, *bits = order if isinstance(order, list) else own_bits(order)
    first = 8 * (part + top - 2 * part * top)
    for a in range(8):
        rows = pl.ds(pl.multiple_of((first + flipped(a, bits)) * size, 16), size)
        out_ref[rows, base : base + values.shape[1]] = values[a * size : (a + 1) * size].astype(out_ref.dtype)


def peer_ids():
    me, depth = lax.axis_index("seq"), lax.axis_index("dp")
    high, low = me // 2, me % 2
    core, deep = depth % 2, depth // 2
    upper, lower = deep // 2, deep % 2
    return {
        ("core", 1): (2 * deep + 1 - core, me),
        ("low", 1): (depth, 2 * high + 1 - low),
        ("high", 1): (depth, 2 * (1 - high) + low),
        ("both", 1): (depth, 3 - me),
        ("deep", 1): (2 * (2 * upper + 1 - lower) + core, me),
        ("deep", 2): (2 * (2 * (1 - upper) + lower) + core, me),
        ("deep", 3): (2 * (3 - deep) + core, me),
    }


LOW_FIRST = ("low", "high", "deep")
HIGH_FIRST = ("high", "low", "deep")
DEEP_FIRST = ("deep", "high", "low")
FAN = {"low": 2, "high": 2, "deep": 4}
SEMS = 12


def landing_rows(order, rows):
    sizes = []
    for name in order:
        rows //= FAN[name]
        sizes.append((FAN[name] - 1) * rows)
    return sizes


class Sum:
    def __init__(self, order, rows, send, keep, core_buf, bufs, own, other, send_sems, recv_sems, local_sem):
        self.order, self.rows, self.send, self.keep = order, rows, send, keep
        self.core_buf, self.bufs, self.own, self.other = core_buf, bufs, own, other
        self.send_sems, self.recv_sems, self.local_sem = send_sems, recv_sems, local_sem
        self.sizes = []
        for name in order:
            rows //= FAN[name]
            self.sizes.append(rows)
        self.peers = peer_ids()

    def stage(self, at):
        if at == 0:
            moves = [(self.send, self.core_buf, ("core", 1))]
        elif at <= 3:
            name, size, buf = self.order[at - 1], self.sizes[at - 1], self.bufs[at - 1]
            moves = [
                (self.keep.at[pl.ds(k * size, size)], buf.at[pl.ds((k - 1) * size, size)], (name, k))
                for k in range(1, FAN[name])
            ]
        elif at <= 6:
            name, size = self.order[6 - at], self.sizes[6 - at]
            src = self.keep if at == 4 else self.own
            moves = [
                (src.at[pl.ds(0, size)], self.own.at[pl.ds(k * size, size)], (name, k)) for k in range(1, FAN[name])
            ]
        else:
            moves = [(self.own, self.other, ("core", 1))]
        counts = [1] + [FAN[name] - 1 for name in self.order]
        base = sum((counts + counts[:0:-1])[:at])
        return [
            pltpu.make_async_remote_copy(
                src_ref=src, dst_ref=dst, send_sem=self.send_sems.at[base + k], recv_sem=self.recv_sems.at[base + k],
                device_id=self.peers[peer], device_id_type=MESH,
            )
            for k, (src, dst, peer) in enumerate(moves)
        ]

    def local(self):
        rows = pl.ds(0, self.sizes[2])
        return pltpu.make_async_copy(self.keep.at[rows], self.own.at[rows], self.local_sem)

    def start(self, stage):
        for copy in self.stage(stage):
            copy.start()

    def arrived(self, stage):
        for copy in self.stage(stage):
            copy.wait_recv()

    def left(self, first, last):
        for stage in range(first, last):
            for copy in self.stage(stage):
                copy.wait_send()

    def add(self, start, size, sources):
        chunk = next(rows for rows in (64, 48, 32) if size % rows == 0)

        def body(at, carry):
            rows = lambda base: pl.ds(pl.multiple_of(base + at * chunk, 16), chunk)
            total = self.keep[rows(start), :].astype(F32)
            for buf, offset in sources:
                total = total + buf[rows(offset + start), :].astype(F32)
            self.keep[rows(start), :] = total.astype(self.keep.dtype)
            return carry

        lax.fori_loop(0, size // chunk, body, 0)

    def sources(self, stage):
        if stage == 0:
            return [(self.core_buf, 0)]
        size = self.sizes[stage - 1]
        return [(self.bufs[stage - 1], k * size) for k in range(FAN[self.order[stage - 1]] - 1)]

    def settle(self, stage):
        self.arrived(stage)
        self.add(0, self.rows if stage == 0 else self.sizes[stage - 1], self.sources(stage))

    def tick(self, at, resumed=False):
        if at == 0 or resumed:
            if at == 4:
                self.local().start()
            self.start(at)
        elif at <= 3:
            self.arrived(at - 1)
            sources, size = self.sources(at - 1), self.sizes[at - 1]
            self.add(size, (self.rows if at == 1 else self.sizes[at - 2]) - size, sources)
            self.start(at)
            self.add(0, size, sources)
        elif at == 4:
            self.settle(3)
            self.local().start()
            self.start(4)
        elif at <= 7:
            self.arrived(at - 1)
            if at == 5:
                self.local().wait()
            self.start(at)
        else:
            self.arrived(7)


UNITS = 3


def gelu_parts(values):
    size = jnp.abs(values)
    bell = jnp.exp(-0.5 * values * values)
    part = 1.0 / (1.0 + 0.3275911 * 0.7071067811865476 * size)
    series = part * (
        0.127414796
        + part * (-0.142248368 + part * (0.7107068705 + part * (-0.7265760135 + part * 0.5307027145)))
    )
    tail = series * bell
    below = jnp.where(values >= 0, 1.0 - tail, tail)
    return values * below, below + values * (bell * 0.3989422804014327)


FEED_PLAN = {
    (3, 0): [(0, 0)],
    (3, 1): [(0, 1)],
    (5, 0): [(1, 0), (0, 2)],
    (5, 1): [(1, 1)],
    (6, 0): [(0, 3)],
    (6, 2): [(1, 2)],
}


def feed_kernel(
    row_ref, att_ref, cot_ref, out_weight_ref, out_bias_ref, gain_ref, shift_ref, fc2_bias_ref,
    w1_ref, bias_ref, w2_ref, *refs
):
    outs, refs = refs[:17], refs[17:]
    results, (branch_out, att_grad_out), sums_out = outs[:4], outs[4:6], outs[6:10]
    last_out, vec_ref = outs[10:16], outs[16]
    (
        n2_s, mid_s, acc_s, back_s, grad_s, hidden_s, hidden_grad_s, result_s, branch_s, att_grad_s,
        d1_s, d2_s, do_s, pre_s, down_s, bias_s, core1, core2, near1, near2, next1, next2, last1, last2, send_sems, recv_sems, load_sem, out_sems,
    ) = refs
    step = pl.program_id(0)
    core = lax.axis_index("dp") % 2
    count = row_ref.shape[0]
    size = w1_ref.shape[1]
    shard = count // 4
    half = do_s.shape[2]
    blocks = [pl.ds(i * shard, shard) for i in range(4)]
    peers = peer_ids()

    def job(unit, which):
        slot = 2 * unit + which
        d, bufs = (d1_s, (core1, near1, next1)) if which == 0 else (d2_s, (core2, near2, next2))
        return Sum(
            (LOW_FIRST, HIGH_FIRST)[which], d.shape[1], d.at[2 * unit], d.at[2 * unit + 1], bufs[0].at[unit],
            [bufs[1].at[unit], bufs[2].at[unit], (last1, last2)[which]], None, None, send_sems.at[slot], recv_sems.at[slot], None,
        )

    def ticks(at, place):
        for unit, tick in FEED_PLAN.get((at, place), []):
            for which in range(2):
                job(unit, which).tick(tick)

    def load():
        return pltpu.make_async_copy(cot_ref, grad_s, load_sem)

    def stores(first, last_store):
        pairs = [(result_s.at[rows], out) for rows, out in zip(blocks, results)]
        pairs += [(branch_s, branch_out), (att_grad_s, att_grad_out)]
        last = 2 * (UNITS - 1)
        pairs += [(d1_s.at[last], last_out[0]), (d1_s.at[last + 1], last_out[1])]
        pairs += [(d2_s.at[last], last_out[2]), (d2_s.at[last + 1], last_out[3])]
        pairs += [(do_s.at[0], last_out[4]), (do_s.at[1], last_out[5])]
        for unit in range(2):
            for which, d in enumerate((d1_s, d2_s)):
                rows = pl.ds(0, d.shape[1] // (4 if unit else 16))
                pairs.append((d.at[2 * unit + 1, rows], sums_out[2 * unit + which]))
        return [pltpu.make_async_copy(src, dst, out_sems.at[n]) for n, (src, dst) in enumerate(pairs) if first <= n < last_store]

    @pl.when(step == 0)
    def _():
        barrier = pltpu.get_barrier_semaphore()
        for name, peer in peers.items():
            if name != ("both", 1):
                pl.semaphore_signal(barrier, inc=1, device_id=peer, device_id_type=MESH)
        load().start()
        vec_ref[...] = jnp.zeros_like(vec_ref)
        for at in range(2 * UNITS):
            bias_s[at : at + 1, :] = bias_ref[at * size : (at + 1) * size].reshape(1, -1)

        def project(i, carry):
            rows = pl.ds(pl.multiple_of(i * shard, shard), shard)
            mid = row_ref[rows, :].astype(F32) + (dot_plain(att_ref[rows, :], out_weight_ref[...]) + row_of(out_bias_ref))
            mid_s[rows, :] = mid
            acc_s[rows, :] = mid + row_of(fc2_bias_ref)
            unit, _ = unit_norm(mid)
            n2_s[rows, :] = (unit * row_of(gain_ref) + row_of(shift_ref)).astype(BF)
            return carry

        lax.fori_loop(0, 4, project, 0)
        back_s[...] = jnp.zeros_like(back_s)
        load().wait()

    @pl.when(step == 2)
    def _():
        pl.semaphore_wait(pltpu.get_barrier_semaphore(), 6)

    for at in range(1, 2 * UNITS + 1):
        unit, keeping = (at - 1) // 2, (at - 1) % 2

        @pl.when(step == at)
        def _():
            ticks(at, 0)

    last_step = step == 2 * UNITS

    at_chunk = jnp.maximum(step - 1, 0)
    chunk_row = 2 * (at_chunk // 2) + (core + 1 + at_chunk % 2) % 2

    @pl.when(step > 0)
    def _():
        bias = bias_s[pl.ds(chunk_row, 1), :]

        pre_s[...] = dot_plain(n2_s[...], w1_ref[...]) + bias
        down_s[...] = dot_rows(grad_s[...], w2_ref[...])
        total = jnp.zeros((1, size), F32)
        for rows in blocks:
            hidden, slope = gelu_parts(pre_s[rows, :])
            hidden_grad = (down_s[rows, :] * slope).astype(BF)
            hidden_s[rows, :] = hidden.astype(BF)
            hidden_grad_s[rows, :] = hidden_grad
            total = total + total_rows(hidden_grad.astype(F32))
        acc_s[...] += dot_plain(hidden_s[...], w2_ref[...])
        back_s[...] += dot_rows(hidden_grad_s[...], w1_ref[...])
        vec_ref[pl.ds(4 + chunk_row, 1), 0:size] = total

    @pl.when(last_step)
    def _():
        def body(i, sums):
            rows = pl.ds(pl.multiple_of(i * shard, shard), shard)
            result_s[rows, :] = acc_s[rows, :].astype(BF)
            back = back_s[rows, :]
            unit, inverse = unit_norm(mid_s[rows, :])
            wide = grad_s[rows, :].astype(F32)
            branch = (wide + norm_back(unit, inverse, back, row_of(gain_ref))).astype(BF)
            branch_s[rows, :] = branch
            parts = (back * unit, back, branch.astype(F32), wide)
            return tuple(old + total_rows(part) for old, part in zip(sums, parts))

        sums = lax.fori_loop(0, 4, body, (jnp.zeros((1, n2_s.shape[1]), F32),) * 4)
        for at, part in enumerate(sums):
            vec_ref[at + 10 : at + 11, :] = part
        att_grad_s[...] = dot_rows(branch_s[...], out_weight_ref[...]).astype(BF)
        for copy in stores(0, 6):
            copy.start()

    for at in range(1, 2 * UNITS + 1):

        @pl.when(step == at)
        def _():
            ticks(at, 1)

    @pl.when(step > 0)
    def _():
        wide, narrow = n2_s.shape[1] // 2, size // 2
        order = blended(ORDERS[1:6:2], (step - 1) // 2)
        for part in range(2):
            left = n2_s[:, part * wide : (part + 1) * wide]
            scatter_part(d1_s.at[step - 1], dot_tokens(left, hidden_grad_s[...]), LOW_FIRST, part)
        for part in range(2):
            left = hidden_s[:, part * narrow : (part + 1) * narrow]
            scatter_part(d2_s.at[step - 1], dot_tokens(left, grad_s[...]), order, part)

    @pl.when(last_step)
    def _():
        ticks(2 * UNITS, 2)

        def body(at, carry):
            slot, part = at // 2, at % 2
            wide = att_ref.shape[1] // 2
            columns = pl.ds(pl.multiple_of(((core + 1 + slot) % 2) * half, 128), half)
            left = att_ref[:, pl.ds(pl.multiple_of(part * wide, 128), wide)]
            scatter_part(do_s.at[slot], dot_tokens(left, branch_s[:, columns]), ORDERS[6], part)
            return carry

        lax.fori_loop(0, 4, body, 0)
        for copy in stores(6, 12):
            copy.start()
        for unit in range(2):
            for which in range(2):
                job(unit, which).settle(2 if unit else 3)
        for copy in stores(12, 16):
            copy.start()
        for copy in stores(0, 16):
            copy.wait()
        for unit in range(2):
            for which in range(2):
                job(unit, which).left(0, 3 if unit else 4)


def feed(row, attended, cotangent, out_weight, out_bias, gain, shift, fc1_weight, fc1_bias, fc2_weight, fc2_bias):
    count, features = row.shape
    size = fc1_weight.shape[1] // (2 * UNITS)
    half = features // 2
    shape = jax.ShapeDtypeStruct
    wide, line = once((count, features)), once((features,))
    vmem, dma = pltpu.VMEM, pltpu.SemaphoreType.DMA

    def chunk(i):
        at = jnp.maximum(i - 1, 0)
        return 2 * (at // 2) + (lax.axis_index("dp") % 2 + 1 + at % 2) % 2

    return pl.pallas_call(
        feed_kernel,
        grid=(2 * UNITS + 1,),
        in_specs=[wide, wide, ANY] + [once(out_weight.shape), line, line, line, line]
        + [
            pl.BlockSpec((features, size), lambda i: (0, chunk(i))),
            once(fc1_bias.shape),
            pl.BlockSpec((size, features), lambda i: (chunk(i), 0)),
        ],
        out_specs=[ANY] * 16 + [once((16, features))],
        out_shape=[shape((count // 4, features), BF)] * 4 + [shape((count, features), BF)] * 2
        + [shape((rows // part, columns), BF) for part in (16, 4) for rows, columns in ((features, size), (size, features))]
        + [shape((features, size), BF)] * 2 + [shape((size, features), BF)] * 2
        + [shape((features, half), BF)] * 2 + [shape((16, features), F32)],
        scratch_shapes=[vmem((count, features), BF)] + [vmem((count, features), F32)] * 3
        + [vmem((count, features), BF), vmem((count, size), BF), vmem((count, size), BF)]
        + [vmem((count, features), BF)] * 3
        + [
            vmem((2 * UNITS, features, size), BF), vmem((2 * UNITS, size, features), BF), vmem((2, features, half), BF),
            vmem((count, size), F32), vmem((count, size), F32), vmem((8, size), F32),
            vmem((2, features, size), BF), vmem((2, size, features), BF),
            vmem((2, features // 2, size), BF), vmem((2, size // 2, features), BF),
            vmem((2, features // 4, size), BF), vmem((2, size // 4, features), BF),
            vmem((3 * features // 16, size), BF), vmem((3 * size // 16, features), BF),
            dma((4, SEMS)), dma((4, SEMS)), dma, dma((16,)),
        ],
        compiler_params=pltpu.CompilerParams(collective_id=2, has_side_effects=True, vmem_limit_bytes=VMEM_GRANT),
        cost_estimate=pl.CostEstimate(flops=35 * 10**9, bytes_accessed=40 * 2**20, transcendentals=0),
        name="feed",
    )(
        row, attended, cotangent, out_weight, out_bias, gain, shift, fc2_bias, fc1_weight, fc1_bias, fc2_weight,
    )


ORDERS = (
    LOW_FIRST, HIGH_FIRST, LOW_FIRST, HIGH_FIRST, LOW_FIRST, HIGH_FIRST, HIGH_FIRST, LOW_FIRST, HIGH_FIRST, LOW_FIRST,
)
FIRST_TICK = (4, 4, 3, 3, 0, 0, 0, 0, 0, 0)
PLAN = {
    (0, 0): [(4, 0), (0, 4)],
    (1, 0): [(4, 1)],
    (1, 1): [(5, 0), (3, 3), (0, 5)],
    (2, 0): [(1, 4), (6, 0)],
    (3, 0): [(5, 1), (6, 1)],
    (3, 1): [(1, 5), (2, 3), (3, 4)],
    (4, 0): [(7, 0)],
    (5, 0): [(7, 1), (4, 2), (0, 6)],
    (5, 1): [(2, 4), (3, 5)],
    (7, 1): [(1, 6), (2, 5)],
    (8, 0): [(8, 0)],
    (9, 0): [(6, 2), (8, 1), (4, 3)],
    (9, 1): [(5, 2), (3, 6)],
    (11, 0): [(7, 2), (4, 4)],
    (11, 1): [(6, 3), (2, 6), (0, 7)],
    (12, 0): [(5, 3), (9, 0)],
    "tail": [
        (6, 4), (9, 1), (4, 5), (5, 4), (2, 7), (7, 3), (8, 2), (1, 7), (6, 5), (9, 2), (7, 4), (5, 5),
        (4, 6), (3, 7), (8, 3), (9, 3), (6, 6), (7, 5), (8, 4), (5, 6), (9, 4), (7, 6), (4, 7), (8, 5),
        (9, 5), (6, 7), (8, 6), (7, 7), (9, 6), (5, 7), (8, 7), (9, 7),
    ],
}
BLOCK_OUT_AT = (0, 0)


def three_parts(column):
    high = column.astype(BF)
    rest = column - high.astype(F32)
    middle = rest.astype(BF)
    return high, middle, (rest - middle.astype(F32)).astype(BF)


def pair_backward(refs, outs, dk_acc, dv_acc, pair, part, block):
    q_ref, k_ref, v_ref, att_ref, grad_ref, lse_ref, miss_ref, own_ref = refs
    lane = lax.broadcasted_iota(jnp.int32, (1, 128), 1)
    first = lane < 64
    half = lane % 64
    keys, values, own = k_ref[...], v_ref[...], own_ref[...]
    unit = jnp.where((half >= 8) & (half < 11), 1.0, 0.0).astype(BF)
    own = own + unit
    unit_rows = jnp.broadcast_to(unit, values.shape)
    keys_aug = [jnp.where(first, keys, own), jnp.where(first, own, keys)]
    values_aug = [jnp.where(first, values, unit_rows), jnp.where(first, unit_rows, values)]
    keys_only = [jnp.where(first, keys, BF(0)), jnp.where(first, BF(0), keys)]

    @pl.when(part == 0)
    def _():
        dk_acc[...] = jnp.zeros_like(dk_acc)
        dv_acc[...] = jnp.zeros_like(dv_acc)

    columns = pl.ds(pl.multiple_of(pair * 128, 128), 128)

    def spread(column):
        high, middle, low = [part.astype(F32) for part in three_parts(-column)]
        wide = jnp.where(half == 8, high, jnp.where(half == 9, middle, jnp.where(half == 10, low, 0.0)))
        return wide.astype(BF)

    def body(step, carry):
        rows = pl.ds(pl.multiple_of(step * block, block), block)
        queries, miss, grad = q_ref[rows, :] * BF(0.125), miss_ref[rows, :], grad_ref[rows, :]
        both = att_ref[rows, :].astype(F32) * grad.astype(F32)
        logs = lse_ref[0, rows, :]
        queries_t, grad_t = queries.T, grad.T
        dq = jnp.zeros((block, 128), F32)
        for head in range(2):
            mine = first if head == 0 else jnp.logical_not(first)
            span = pl.ds(64 * head, 64)
            delta = jnp.sum(jnp.where(mine, both, 0.0), axis=1, keepdims=True)
            total = logs[:, 0:1] if head == 0 else logs[:, 64:65]
            queries_aug = jnp.where(mine, queries, spread(total) + miss)
            grad_aug = jnp.where(mine, grad, spread(delta))
            probs = jnp.exp(dot_rows(queries_aug, keys_aug[head]))
            score_grad = (probs * dot_rows(grad_aug, values_aug[head])).astype(BF)
            dq = dq + dot_plain(score_grad, keys_only[head])
            dk_acc[span, :] += dot_plain(queries_t[64 * head : 64 * head + 64], score_grad)
            dv_acc[span, :] += dot_plain(grad_t[64 * head : 64 * head + 64], probs.astype(BF))
        outs[0][rows, columns] = (dq * 0.125).astype(BF)
        return carry

    steps = q_ref.shape[0] // block // 2
    lax.fori_loop(part * steps, (part + 1) * steps, body, 0)

    @pl.when(part == 1)
    def _():
        outs[1][:, columns] = dk_acc[...].T.astype(BF)
        outs[2][:, columns] = dv_acc[...].T.astype(BF)


def backward_kernel(*refs):
    (
        q_ref, k_ref, v_ref, att_ref, grad_ref, lse_ref, miss_ref, own_ref, normed_ref,
        weight_ref, row_ref, branch_ref, gain_ref, vec_in_ref,
    ) = refs[:14]
    results, sums_in, last_in = refs[14:18], refs[18:22], refs[22:28]
    block_out, vec_out = refs[28:30]
    token_outs = refs[30:34]
    owns, others = refs[34:44], refs[44:54]
    (
        dq_s, dk_s, dv_s, dk_acc, dv_acc, qkv_s, own_result, grad_s, vec_s, vec_got,
        send_sems, recv_sems, local_sems, load_sems, side_send, side_recv, vec_send, vec_recv,
    ) = refs[54:72]
    held = refs[72:79]
    landing = refs[79:]
    step = pl.program_id(0)
    me, depth = lax.axis_index("seq"), lax.axis_index("dp")
    core = depth % 2
    peers = peer_ids()
    shard = results[0].shape[0]
    features = row_ref.shape[1]

    def job(n):
        sems = send_sems.at[n], recv_sems.at[n], local_sems.at[n]
        if n < 4:
            bufs = [None, None, landing[n - 2] if n > 1 else None]
            return Sum(ORDERS[n], owns[n].shape[0], None, held[n], None, bufs, owns[n], others[n], *sems)
        send = last_in[2 * (n - 4)] if n < 7 else qkv_s.at[2 * (n - 7)]
        keep = held[n] if n < 7 else qkv_s.at[2 * (n - 7) + 1]
        core_buf, *bufs = landing[4 * n - 14 : 4 * n - 10]
        return Sum(ORDERS[n], keep.shape[0], send, keep, core_buf, bufs, owns[n], others[n], *sems)

    def load(n):
        if n == 7:
            return pltpu.make_async_copy(results[0], own_result, load_sems.at[7])
        src = sums_in[n] if n < 4 else last_in[2 * (n - 4) + 1]
        return pltpu.make_async_copy(src, held[n], load_sems.at[n])

    def store():
        return pltpu.make_async_copy(own_result, block_out.at[me, 0], load_sems.at[7])

    def token_store(k):
        return pltpu.make_async_copy(grad_s.at[k], token_outs[k], load_sems.at[8 + k])

    kinds = [("low", 1), ("high", 1), ("both", 1)]

    def block_copy(k):
        return pltpu.make_async_remote_copy(
            src_ref=results[k], dst_ref=block_out.at[me, 0], send_sem=side_send.at[k - 1],
            recv_sem=side_recv.at[k - 1], device_id=peers[kinds[k - 1]], device_id_type=MESH,
        )

    vec_names = [[("core", 1)], kinds, [("deep", 1), ("deep", 2), ("deep", 3)]]

    def vec_stage(stage):
        return [
            pltpu.make_async_remote_copy(
                src_ref=vec_s.at[stage], dst_ref=vec_got.at[stage, k],
                send_sem=vec_send.at[stage, k], recv_sem=vec_recv.at[stage, k],
                device_id=peers[name], device_id_type=MESH,
            )
            for k, name in enumerate(vec_names[stage])
        ]

    def vec_step(stage):
        for copy in vec_stage(stage):
            copy.wait_recv()
        total = vec_s[stage]
        for k in range(len(vec_names[stage])):
            total = total + vec_got[stage, k]
        if stage == 2:
            vec_out[...] = total
        else:
            vec_s[stage + 1] = total
            for copy in vec_stage(stage + 1):
                copy.start()

    def ticks(at, place):
        for n, tick in PLAN.get((at, place), []):
            resumed = tick == FIRST_TICK[n] > 0
            if resumed or (4 <= n < 7 and tick == 1):
                load(n).wait()
            job(n).tick(tick, resumed)

    @pl.when(step == 0)
    def _():
        barrier = pltpu.get_barrier_semaphore()
        for peer in peers.values():
            pl.semaphore_signal(barrier, inc=1, device_id=peer, device_id_type=MESH)
        for n in range(8):
            load(n).start()
        pl.semaphore_wait(barrier, len(peers))

    for at in range(13):

        @pl.when(step == at)
        def _():
            if (at, 0) == BLOCK_OUT_AT:
                for k in (1, 2, 3):
                    block_copy(k).start()
            ticks(at, 0)
            if at == 2:
                load(7).wait()
                store().start()

    turn = step // 2
    pair = 2 * (turn // 2) + (core + 1 + turn % 2) % 2

    @pl.when(step < 12)
    def _():
        pair_backward(
            (q_ref, k_ref, v_ref, att_ref, grad_ref, lse_ref, miss_ref, own_ref),
            (dq_s, dk_s, dv_s), dk_acc, dv_acc, pair, step % 2, 256,
        )

    for at in range(1, 12, 2):

        @pl.when(step == at)
        def _():
            if (at, 1) == BLOCK_OUT_AT:
                for k in (1, 2, 3):
                    block_copy(k).start()
            ticks(at, 1)

    @pl.when((step < 12) & (step % 2 == 1))
    def _():
        columns = pl.ds(pl.multiple_of(pair * 128, 128), 128)
        grads = jnp.concatenate([part[:, columns] for part in (dq_s, dk_s, dv_s)], axis=1)
        vec_out[2:3, columns] = total_rows(grads[:, :128].astype(F32))
        vec_out[3:4, columns] = total_rows(grads[:, 256:].astype(F32))

        def body(part, carry):
            left = normed_ref[:, pl.ds(pl.multiple_of(part * (features // 2), 128), features // 2)]
            scatter_part(qkv_s.at[turn], dot_tokens(left, grads), blended(ORDERS[7:10], turn // 2), part)
            return carry

        lax.fori_loop(0, 2, body, 0)

    @pl.when(step == 12)
    def _():
        def body(at, sums):
            k = 3 - at
            rows = pl.ds(pl.multiple_of(k * shard, shard), shard)
            back = dot_rows(dq_s[rows, :], weight_ref[:, :features])
            back = back + dot_rows(dk_s[rows, :], weight_ref[:, features : 2 * features])
            back = back + dot_rows(dv_s[rows, :], weight_ref[:, 2 * features :])
            unit, inverse = unit_norm(row_ref[rows, :].astype(F32))
            grad_s[k] = (branch_ref[rows, :].astype(F32) + norm_back(unit, inverse, back, row_of(gain_ref))).astype(BF)
            for piece in range(4):

                @pl.when(k == piece)
                def _():
                    token_store(piece).start()

            return tuple(old + total_rows(part) for old, part in zip(sums, (back * unit, back)))

        gain_sum, shift_sum = lax.fori_loop(0, 4, body, (jnp.zeros((1, features), F32),) * 2)
        vec_s[0] = vec_in_ref[...]
        vec_s[0, 0:1, :] = gain_sum
        vec_s[0, 1:2, :] = shift_sum
        vec_s[0, 2:4, :] = vec_out[2:4, :]
        vec_stage(0)[0].start()

    @pl.when(step == 13)
    def _():
        for index, (n, tick) in enumerate(PLAN["tail"]):
            if index in (3, 8, 13):
                vec_step((index - 3) // 5)
            job(n).tick(tick)
        for n in range(10):
            job(n).arrived(7)
        for n in range(10):
            job(n).left(FIRST_TICK[n], 8)
        store().wait()
        for k in range(4):
            token_store(k).wait()
        for k in (1, 2, 3):
            block_copy(k).wait()
        for stage in range(3):
            for copy in vec_stage(stage):
                copy.wait_send()


def backward(
    projected, attended, attended_grad, logs, miss, own, normed, qkv_weight, row, branch, gain, vec_in,
    results, sums_in, last_in,
):
    count, width = projected.shape
    features = width // 3
    pairs = width // 384
    half = features // 2
    shard = count // 4

    def pair(i):
        at = jnp.minimum(i // 2, 5)
        return 2 * (at // 2) + (lax.axis_index("dp") % 2 + 1 + at % 2) % 2

    column = lambda base: pl.BlockSpec((count, 128), lambda i: (0, pair(i) + base))
    shape = jax.ShapeDtypeStruct
    wide = once((count, features))
    full = once((count, 128))
    vmem, dma = pltpu.VMEM, pltpu.SemaphoreType.DMA
    sizes = [last_in[0].shape, last_in[2].shape] * UNITS + [(features, half)] * 4
    held = [vmem(array.shape, BF) for array in (*sums_in, *last_in[1::2])]
    landing = []
    for n, (rows, columns) in enumerate(sizes):
        lands = landing_rows(ORDERS[n], rows)
        landing += [vmem((size, columns), BF) for size in ([rows] + lands)[FIRST_TICK[n] :]]
    return pl.pallas_call(
        backward_kernel,
        grid=(14,),
        in_specs=[
            column(0), column(pairs), column(2 * pairs), column(0), column(0),
            pl.BlockSpec((1, count, 128), lambda i: (pair(i), 0, 0)),
            full, full, wide, once(qkv_weight.shape), wide, wide, once((features,)), once((16, features)),
        ]
        + [ANY] * 14,
        out_specs=[ANY, once((16, features))] + [ANY] * 24,
        out_shape=[shape((4, 1, shard, features), BF), shape((16, features), F32)] + [shape((shard, features), BF)] * 4
        + [shape(size, BF) for size in sizes] * 2,
        scratch_shapes=[vmem((count, features), BF)] * 3
        + [vmem((128, count), F32)] * 2
        + [vmem((6, features, half), BF)]
        + [
            vmem((shard, features), BF), vmem((4, shard, features), BF),
            vmem((3, 16, features), F32), vmem((3, 3, 16, features), F32),
            dma((10, SEMS)), dma((10, SEMS)), dma((10,)), dma((12,)), dma((3,)), dma((3,)), dma((3, 3)), dma((3, 3)),
        ]
        + held + landing,
        compiler_params=pltpu.CompilerParams(collective_id=1, has_side_effects=True, vmem_limit_bytes=VMEM_GRANT),
        cost_estimate=pl.CostEstimate(flops=60 * 10**9, bytes_accessed=60 * 2**20, transcendentals=12 * 2**20),
        name="backward",
    )(
        projected, projected, projected, attended, attended_grad, logs, miss, own, normed, qkv_weight, row, branch,
        gain, vec_in, *results, *sums_in, *last_in,
    )


STEPS = 8


def own_group(order):
    total = 0
    for bit in own_bits(order):
        total = 2 * total + bit
    return total


def assemble_kernel(*refs):
    ins, vec_ref = refs[:20], refs[20]
    d1_ref, d2_ref, out_ref, qkv_ref = refs[21:25]
    vecs = refs[25:]
    core = lax.axis_index("dp") % 2
    features = out_ref.shape[1]
    size = ins[0].shape[1]
    half = features // 2

    def ordered(n):
        ref, last = ins[n], own_bits(ORDERS[n // 2])[3]
        rows = ref.shape[0] // 2
        return jnp.concatenate(
            [ref[pl.ds(pl.multiple_of((a + last - 2 * a * last) * rows, 16), rows), :] for a in range(2)], axis=0
        ).astype(F32)

    for side in range(2):
        home = core if side == 0 else 1 - core
        for unit in range(UNITS):
            columns = pl.ds(pl.multiple_of((2 * unit + home) * size, 128), size)
            d1_ref[:, columns] = ordered(4 * unit + side)
            d2_ref[unit, home] = ordered(4 * unit + 2 + side)
        out_ref[:, pl.ds(pl.multiple_of(home * half, 128), half)] = ordered(12 + side)
        for group in range(3):
            values = ordered(14 + 2 * group + side)
            for part in range(3):
                at = part * features + (2 * group + home) * 128
                qkv_ref[:, pl.ds(pl.multiple_of(at, 128), 128)] = values[:, part * 128 : (part + 1) * 128]

    @pl.when(pl.program_id(0) == 0)
    def _():
        for ref, row in zip(vecs, (0, 1, 12, 10, 11, 13)):
            ref[...] = vec_ref[row, :]
        qv_ref, fc1_ref = vecs[6:]
        for at in range(2):
            qv_ref[at * features : (at + 1) * features] = vec_ref[2 + at, :]
        for at in range(2 * UNITS):
            fc1_ref[at * size : (at + 1) * size] = vec_ref[4 + at, 0:size]


def assemble(parts, vector):
    features, size = parts[0].shape
    half = features // 2
    wide = 2 * UNITS * size
    shape = jax.ShapeDtypeStruct

    def spec(n):
        rows, columns = parts[n].shape
        return pl.BlockSpec((rows // STEPS, columns), lambda i: (i ^ (own_group(ORDERS[n // 2]) // 2), 0))

    lines = [features] * 6 + [2 * features, wide]
    d1, d2, out, qkv, *vecs = pl.pallas_call(
        assemble_kernel,
        grid=(STEPS,),
        in_specs=[spec(n) for n in range(20)] + [once(vector.shape)],
        out_specs=[
            pl.BlockSpec((features // STEPS, wide), lambda i: (i, 0)),
            pl.BlockSpec((UNITS, 2, size // STEPS, features), lambda i: (0, 0, i, 0)),
            pl.BlockSpec((features // STEPS, features), lambda i: (i, 0)),
            pl.BlockSpec((features // STEPS, 3 * features), lambda i: (i, 0)),
        ]
        + [once((line,)) for line in lines],
        out_shape=[
            shape((features, wide), F32), shape((UNITS, 2, size, features), F32), shape((features, features), F32),
            shape((features, 3 * features), F32),
        ]
        + [shape((line,), F32) for line in lines],
        compiler_params=pltpu.CompilerParams(vmem_limit_bytes=VMEM_GRANT),
        cost_estimate=pl.CostEstimate(flops=0, bytes_accessed=45 * 2**20, transcendentals=0),
        name="assemble",
    )(*parts, vector)
    return d1, d2.reshape(wide, features), out, qkv, vecs


def place_row_kernel(p0, p1, p2, p3, out_ref):
    which = pl.program_id(0) ^ lax.axis_index("seq")
    for k, piece in enumerate((p0, p1, p2, p3)):

        @pl.when(which == k)
        def _():
            out_ref[0, 0] = piece[...]


def place_row(pieces):
    shard, features = pieces[0].shape
    return pl.pallas_call(
        place_row_kernel,
        grid=(4,),
        in_specs=[once((shard, features))] * 4,
        out_specs=pl.BlockSpec((1, 1, shard, features), lambda i: (i, 0, 0, 0)),
        out_shape=jax.ShapeDtypeStruct((4, 1, shard, features), BF),
        compiler_params=pltpu.CompilerParams(vmem_limit_bytes=VMEM_GRANT),
        cost_estimate=pl.CostEstimate(flops=0, bytes_accessed=3 * 2**20, transcendentals=0),
        name="place_row",
    )(*pieces)


def swap(array, axis, bit):
    count = lax.axis_size(axis)
    return lax.ppermute(array, axis, [(i, i ^ bit) for i in range(count)])


def fast_shards(
    tokens, image_lengths, cotangent, attn_gain, attn_shift, qkv_weight, qv_bias, out_weight,
    out_bias, mlp_gain, mlp_shift, fc1_weight, fc1_bias, fc2_weight, fc2_bias,
):
    shard_len = tokens.shape[2]
    parties = lax.axis_size("seq")
    row_len = shard_len * parties
    images = image_lengths.shape[2] - 1
    me = lax.axis_index("seq")

    row, normed, projected = enter(tokens, attn_gain, attn_shift, qkv_weight, qv_bias)
    seg_row = segment_ids(lax.dynamic_index_in_dim(image_lengths, me, 0, keepdims=False), row_len, images)
    seg_row = seg_row.reshape(parties, shard_len)
    segment = jnp.concatenate([seg_row[me ^ k] for k in range(parties)], axis=0)
    miss, own = segment_features(segment)
    attended, logs, grads = attention_forward(projected, miss, own, cotangent)
    fed = feed(
        row, attended, grads, out_weight, out_bias, mlp_gain, mlp_shift, fc1_weight, fc1_bias, fc2_weight, fc2_bias
    )
    results, (branch, attended_grad), sums, last, vec = fed[:4], fed[4:6], fed[6:10], fed[10:16], fed[16]
    block_out, vector, *rest = backward(
        projected, attended, attended_grad, logs, miss, own, normed, qkv_weight, row, branch, attn_gain, vec,
        results, sums, last,
    )
    pieces, summed = rest[:4], rest[4:]
    paired = [part for n in range(10) for part in (summed[n], summed[10 + n])]
    tokens_grad = place_row([pieces[0]] + [swap(pieces[k], "seq", k) for k in (1, 2, 3)])
    fc1_grad, fc2_grad, out_grad, qkv_grad, vecs = assemble(paired, vector)
    gain, shift, out_sum, mlp_gain_sum, mlp_shift_sum, fc2_sum, qv_sum, fc1_sum = vecs
    return (
        block_out, tokens_grad, gain, shift, qkv_grad, qv_sum, out_grad, out_sum, mlp_gain_sum, mlp_shift_sum,
        fc1_grad, fc1_sum, fc2_grad, fc2_sum,
    )


def shards(tokens, *rest):
    micro_count, row_count, shard_len, features = tokens.shape
    whole_rows = micro_count == 4 and row_count == 1 and shard_len % 128 == 0
    sizes = lax.axis_size("dp") == 8 and lax.axis_size("seq") == 4
    hidden = rest[10].shape[1]
    if sizes and whole_rows and features == 64 * HEADS == 768 and hidden == 4 * features:
        return fast_shards(tokens, *rest)
    return general_shards(tokens, *rest)


def solution(mesh):
    placed = (
        P(None, "dp", "seq", None),
        P(None, "dp", None),
        P(None, "dp", "seq", None),
        P(),
        P(),
        P(),
        P(),
        P(),
        P(),
        P(),
        P(),
        P(),
        P(),
        P(),
        P(),
    )
    return jax.shard_map(
        shards,
        mesh=mesh,
        in_specs=placed,
        out_specs=(
            P(None, "dp", "seq", None),
            P(None, "dp", "seq", None),
            P(),
            P(),
            P(),
            P(),
            P(),
            P(),
            P(),
            P(),
            P(),
            P(),
            P(),
            P(),
        ),
        check_vma=False,
    )
```

```python
import functools

import jax
import jax.numpy as jnp
from jax import lax
from jax.experimental import pallas as pl
from jax.experimental.pallas import tpu as pltpu
from jax.sharding import PartitionSpec as P

HEADS = 12


EPS = 1e-06
NEG = -1e30


def layer_norm(values, scale_row, shift_row):
    center = values - jnp.mean(values, axis=-1, keepdims=True)
    spread = jnp.mean(center * center, axis=-1, keepdims=True)
    return center * lax.rsqrt(spread + EPS) * scale_row + shift_row


def gelu_exact(values):
    return jax.nn.gelu(values, approximate=False)


def segment_ids(lengths, row_len, images):
    positions = jnp.arange(row_len, dtype=jnp.int32)
    ends = jnp.cumsum(lengths, axis=-1) + 2 * images
    patches = jnp.sum((positions[:, None] >= ends[..., None, :]).astype(jnp.int32), axis=-1)
    return jnp.where(positions < 2 * images, positions // 2, patches)


def matmul(first_op, second_op, pattern):
    return jnp.einsum(pattern, first_op, second_op, preferred_element_type=jnp.float32)


def general_shards(
    tokens,
    image_lengths,
    cotangent,
    attn_gain,
    attn_shift,
    qkv_weight,
    qv_bias,
    out_weight,
    out_bias,
    mlp_gain,
    mlp_shift,
    fc1_weight,
    fc1_bias,
    fc2_weight,
    fc2_bias,
):
    micro_count, row_count, shard_len, features = tokens.shape
    row_len = shard_len * lax.axis_size("seq")
    images = image_lengths.shape[2] - 1
    head_dim = features // HEADS
    score_scale = head_dim ** (-0.5)
    offset = lax.axis_index("seq") * shard_len
    tok_count = row_count * shard_len
    zero_keys = jnp.zeros((features,), jnp.float32)
    full_bias = jnp.concatenate([qv_bias[:features], zero_keys, qv_bias[features:]])
    totals = [
        jnp.zeros(weight.shape, jnp.float32)
        for weight in (
            attn_gain,
            attn_shift,
            qkv_weight,
            qv_bias,
            out_weight,
            out_bias,
            mlp_gain,
            mlp_shift,
            fc1_weight,
            fc1_bias,
            fc2_weight,
            fc2_bias,
        )
    ]
    outputs_list = []
    grads_list = []
    for micro_step in range(micro_count):
        inputs = tokens[micro_step].astype(jnp.float32)
        seg_all = segment_ids(image_lengths[micro_step], row_len, images)
        seg_here = lax.dynamic_slice_in_dim(seg_all, offset, shard_len, 1)
        allowed = seg_here[:, None, :, None] == seg_all[:, None, None, :]
        normed, first_pull = jax.vjp(layer_norm, inputs, attn_gain, attn_shift)
        normed_low = normed.astype(jnp.bfloat16).reshape(tok_count, features)
        projected = (matmul(normed_low, qkv_weight, "td,de->te") + full_bias).astype(jnp.bfloat16)
        projected = projected.reshape(row_count, shard_len, 3 * features)
        queries = projected[:, :, :features].reshape(row_count, shard_len, HEADS, head_dim)
        keys_all, values_all = (
            lax.all_gather(projected[:, :, features : 2 * features], "seq", axis=1, tiled=True),
            lax.all_gather(projected[:, :, 2 * features :], "seq", axis=1, tiled=True),
        )
        keys_all = keys_all.reshape(row_count, row_len, HEADS, head_dim)
        values_all = values_all.reshape(row_count, row_len, HEADS, head_dim)
        scores = jnp.where(allowed, matmul(queries, keys_all, "rqhd,rkhd->rhqk") * score_scale, NEG)
        largest = jnp.max(scores, axis=-1, keepdims=True)
        log_total = largest + jnp.log(jnp.sum(jnp.exp(scores - largest), axis=-1, keepdims=True))
        weights_low = jnp.exp(scores - log_total).astype(jnp.bfloat16)
        attended = (
            matmul(weights_low, values_all, "rhqk,rkhd->rqhd")
            .astype(jnp.bfloat16)
            .reshape(tok_count, features)
        )
        branch = matmul(attended, out_weight, "td,de->te") + out_bias
        middle = inputs + branch.reshape(inputs.shape)
        normed_two, second_pull = jax.vjp(layer_norm, middle, mlp_gain, mlp_shift)
        normed_two_low = normed_two.astype(jnp.bfloat16).reshape(tok_count, features)
        hidden_pre = matmul(normed_two_low, fc1_weight, "td,df->tf") + fc1_bias
        hidden, gelu_pull = jax.vjp(gelu_exact, hidden_pre)
        hidden_low = hidden.astype(jnp.bfloat16)
        result = middle + (matmul(hidden_low, fc2_weight, "tf,fd->td") + fc2_bias).reshape(
            inputs.shape
        )
        outputs_list.append(result.astype(jnp.bfloat16))
        incoming = cotangent[micro_step].reshape(tok_count, features)
        fc2_weight_part = matmul(hidden_low, incoming, "tf,td->fd")
        fc2_bias_part = jnp.sum(incoming.astype(jnp.float32), axis=0)
        hidden_grad = gelu_pull(matmul(incoming, fc2_weight, "td,fd->tf"))[0].astype(jnp.bfloat16)
        fc1_weight_part = matmul(normed_two_low, hidden_grad, "td,tf->df")
        fc1_bias_part = jnp.sum(hidden_grad.astype(jnp.float32), axis=0)
        back_two = matmul(hidden_grad, fc1_weight, "tf,df->td").reshape(inputs.shape)
        middle_norm, mlp_gain_part, mlp_shift_part = second_pull(back_two)
        middle_grad = incoming.astype(jnp.float32).reshape(inputs.shape) + middle_norm
        branch_grad = middle_grad.astype(jnp.bfloat16).reshape(tok_count, features)
        out_weight_part = matmul(attended, branch_grad, "td,te->de")
        out_bias_part = jnp.sum(branch_grad.astype(jnp.float32), axis=0)
        attended_grad = matmul(branch_grad, out_weight, "te,de->td").astype(jnp.bfloat16)
        attended_grad = attended_grad.reshape(row_count, shard_len, HEADS, head_dim)
        scores_again = jnp.where(
            allowed, matmul(queries, keys_all, "rqhd,rkhd->rhqk") * score_scale, NEG
        )
        chances = jnp.exp(scores_again - log_total)
        chances_low = chances.astype(jnp.bfloat16)
        chance_grad = matmul(attended_grad, values_all, "rqhd,rkhd->rhqk")
        row_delta = jnp.sum(chances * chance_grad, axis=-1, keepdims=True)
        score_grad = (chances * (chance_grad - row_delta)).astype(jnp.bfloat16)
        query_grad = matmul(score_grad, keys_all, "rhqk,rkhd->rqhd") * score_scale
        key_terms = matmul(score_grad, queries, "rhqk,rqhd->rkhd") * score_scale
        value_terms = matmul(chances_low, attended_grad, "rhqk,rqhd->rkhd")
        key_grad, value_grad = (
            lax.psum_scatter(
                key_terms.reshape(row_count, row_len, features).astype(jnp.bfloat16),
                "seq",
                scatter_dimension=1,
                tiled=True,
            ).astype(jnp.float32),
            lax.psum_scatter(
                value_terms.reshape(row_count, row_len, features).astype(jnp.bfloat16),
                "seq",
                scatter_dimension=1,
                tiled=True,
            ).astype(jnp.float32),
        )
        projected_grad = jnp.concatenate(
            [query_grad.reshape(row_count, shard_len, features), key_grad, value_grad], axis=-1
        )
        projected_grad = projected_grad.astype(jnp.bfloat16).reshape(tok_count, 3 * features)
        qkv_weight_part = matmul(normed_low, projected_grad, "td,te->de")
        bias_sums = jnp.sum(projected_grad.astype(jnp.float32), axis=0)
        qv_bias_part = jnp.concatenate([bias_sums[:features], bias_sums[2 * features :]])
        back_one = matmul(projected_grad, qkv_weight, "te,de->td").reshape(inputs.shape)
        inputs_norm, attn_gain_part, attn_shift_part = first_pull(back_one)
        grads_list.append((middle_grad + inputs_norm).astype(jnp.bfloat16))
        pieces = (
            attn_gain_part,
            attn_shift_part,
            qkv_weight_part,
            qv_bias_part,
            out_weight_part,
            out_bias_part,
            mlp_gain_part,
            mlp_shift_part,
            fc1_weight_part,
            fc1_bias_part,
            fc2_weight_part,
            fc2_bias_part,
        )
        totals = [running + member for running, member in zip(totals, pieces)]
    (
        attn_gain_sum,
        attn_shift_sum,
        qkv_weight_sum,
        qv_bias_sum,
        out_weight_sum,
        out_bias_sum,
        mlp_gain_sum,
        mlp_shift_sum,
        fc1_weight_sum,
        fc1_bias_sum,
        fc2_weight_sum,
        fc2_bias_sum,
    ) = totals
    summed = lax.psum(
        (
            attn_gain_sum,
            attn_shift_sum,
            qkv_weight_sum,
            qv_bias_sum,
            out_weight_sum,
            out_bias_sum,
            mlp_gain_sum,
            mlp_shift_sum,
            fc1_weight_sum,
            fc1_bias_sum,
            fc2_weight_sum,
            fc2_bias_sum,
        ),
        ("dp", "seq"),
    )
    return (jnp.stack(outputs_list), jnp.stack(grads_list)) + tuple(summed)

F32 = jnp.float32
BF = jnp.bfloat16
BIG = 1e30
MESH = pl.DeviceIdType.MESH
VMEM_GRANT = 60 * 2**20
ANY = pl.BlockSpec(memory_space=pl.ANY)


def dot_rows(first_op, second_op):
    return lax.dot_general(first_op, second_op, (((1,), (1,)), ((), ())), preferred_element_type=F32)


def dot_plain(first_op, second_op):
    return lax.dot_general(first_op, second_op, (((1,), (0,)), ((), ())), preferred_element_type=F32)


def dot_tokens(first_op, second_op):
    return lax.dot_general(first_op, second_op, (((0,), (0,)), ((), ())), preferred_element_type=F32)


def once(shape, index=None):
    place = index if index is not None else (lambda *_: (0,) * len(shape))
    return pl.BlockSpec(shape, place, pipeline_mode=pl.Buffered(1))


def total_rows(array):
    return jnp.sum(array, axis=0, keepdims=True)


def unit_norm(values):
    center = values - jnp.mean(values, axis=-1, keepdims=True)
    inverse = lax.rsqrt(jnp.mean(center * center, axis=-1, keepdims=True) + EPS)
    return center * inverse, inverse


def norm_back(unit, inverse, incoming, gain):
    scaled = incoming * gain
    return inverse * (
        scaled
        - jnp.mean(scaled, axis=-1, keepdims=True)
        - unit * jnp.mean(scaled * unit, axis=-1, keepdims=True)
    )


def row_of(ref):
    return ref[...].reshape(1, -1)


def enter_kernel(
    tokens_ref, gain_ref, shift_ref, weight_ref, bias_ref,
    row_out, normed_out, projected_out,
    landed, weight_s, normed_s, projected_s, send_sem, recv_sem, load_sem, out_sem,
):
    me, depth = lax.axis_index("seq"), lax.axis_index("dp")
    high, low = me // 2, me % 2
    peers = [me, 2 * high + 1 - low, 2 * (1 - high) + low, 3 - me]
    shard, features = landed.shape[1:]
    barrier = pltpu.get_barrier_semaphore()
    for peer in peers[1:]:
        pl.semaphore_signal(barrier, inc=1, device_id=(depth, peer), device_id_type=MESH)
    own = pltpu.make_async_copy(tokens_ref.at[me, 0], landed.at[0], load_sem.at[0])
    weight = pltpu.make_async_copy(weight_ref, weight_s, load_sem.at[1])
    own.start()
    weight.start()
    pl.semaphore_wait(barrier, 3)

    def remote(at, k, start, size):
        rows = pl.ds(start, size)
        return pltpu.make_async_remote_copy(
            src_ref=tokens_ref.at[peers[k], 0, rows], dst_ref=landed.at[k, rows],
            send_sem=send_sem.at[at], recv_sem=recv_sem.at[at], device_id=(depth, peers[k]), device_id_type=MESH,
        )

    copies = [remote(k - 1, k, 0, shard) for k in (1, 2, 3)]
    for copy in copies[:2]:
        copy.start()
    bias = row_of(bias_ref)
    bias = jnp.concatenate([bias[:, :features], jnp.zeros((1, features), F32), bias[:, features:]], axis=1)

    def outs(k):
        rows = pl.ds(pl.multiple_of(k * shard, shard), shard)
        pairs = (
            (landed.at[k], row_out), (normed_s.at[rows], normed_out), (projected_s.at[rows], projected_out),
        )
        return [
            pltpu.make_async_copy(src, dst.at[rows], out_sem.at[3 * k + n]) for n, (src, dst) in enumerate(pairs)
        ]

    def body(k, carry):
        @pl.when(k == 0)
        def _():
            own.wait()
            weight.wait()

        @pl.when(k == 1)
        def _():
            for copy in copies[:2]:
                copy.wait_send()
            copies[2].start()

        for piece in (1, 2, 3):

            @pl.when(k == piece)
            def _():
                copies[piece - 1].wait_recv()

        unit, _ = unit_norm(landed[k].astype(F32))
        normed = (unit * row_of(gain_ref) + row_of(shift_ref)).astype(BF)
        rows = pl.ds(pl.multiple_of(k * shard, shard), shard)
        normed_s[rows, :] = normed
        projected_s[rows, :] = (dot_plain(normed, weight_s[...]) + bias).astype(BF)
        for copy in outs(k):
            copy.start()
        return carry

    lax.fori_loop(0, 4, body, 0)
    for k in range(4):
        for copy in outs(k):
            copy.wait()
    copies[2].wait_send()


def enter(tokens, gain, shift, weight, bias):
    _, _, shard, features = tokens.shape
    count, wide = 4 * shard, weight.shape[1]
    shape = jax.ShapeDtypeStruct
    vmem = pl.BlockSpec(memory_space=pltpu.VMEM)
    dma = pltpu.SemaphoreType.DMA
    return pl.pallas_call(
        enter_kernel,
        in_specs=[ANY, vmem, vmem, ANY, vmem],
        out_specs=[ANY] * 3,
        out_shape=[shape((count, features), BF), shape((count, features), BF), shape((count, wide), BF)],
        scratch_shapes=[
            pltpu.VMEM((4, shard, features), BF), pltpu.VMEM(weight.shape, BF), pltpu.VMEM((count, features), BF),
            pltpu.VMEM((count, wide), BF),
            dma((3,)), dma((3,)), dma((2,)), dma((12,)),
        ],
        compiler_params=pltpu.CompilerParams(collective_id=0, has_side_effects=True, vmem_limit_bytes=VMEM_GRANT),
        cost_estimate=pl.CostEstimate(flops=4 * 10**9, bytes_accessed=20 * 2**20, transcendentals=0),
        name="enter",
    )(tokens, gain, shift, weight, bias)


def attention_forward_kernel(
    block, q_ref, k_ref, v_ref, miss_ref, own_ref, cot_ref, out_ref, lse_ref, grad_out,
    scores_s, weights_s, mixed_s, largest_s, piece_s, send_sem, recv_sem, own_sem,
):
    step = pl.program_id(0)
    me = lax.axis_index("seq")
    peers = peer_ids()
    kinds = [("low", 1), ("high", 1), ("both", 1)]
    shard = piece_s.shape[0]

    def exchange():
        return [
            pltpu.make_async_remote_copy(
                src_ref=cot_ref.at[peers[name][1], 0], dst_ref=grad_out.at[pl.ds((k + 1) * shard, shard)],
                send_sem=send_sem.at[k], recv_sem=recv_sem.at[k], device_id=peers[name], device_id_type=MESH,
            )
            for k, name in enumerate(kinds)
        ]

    def load():
        return pltpu.make_async_copy(cot_ref.at[me, 0], piece_s, own_sem)

    def store():
        return pltpu.make_async_copy(piece_s, grad_out.at[pl.ds(0, shard)], own_sem)

    @pl.when(step == 0)
    def _():
        barrier = pltpu.get_barrier_semaphore()
        for name in kinds:
            pl.semaphore_signal(barrier, inc=1, device_id=peers[name], device_id_type=MESH)
        load().start()
        pl.semaphore_wait(barrier, 3)
        for copy in exchange():
            copy.start()

    @pl.when(step == 1)
    def _():
        load().wait()
        store().start()

    lane = lax.broadcasted_iota(jnp.int32, (1, 128), 1)
    first = lane < 64
    keys, values, own = k_ref[...], v_ref[...], own_ref[...]
    ones = jnp.ones_like(values)
    keys_aug = [jnp.where(first, keys, own), jnp.where(first, own, keys)]
    values_aug = [jnp.where(first, values, ones), jnp.where(first, ones, values)]
    units = [(pl.ds(i * block, block), head) for i in range(q_ref.shape[0] // block) for head in range(2)]

    def score(n):
        rows, head = units[n]
        queries, miss = q_ref[rows, :] * BF(0.125), miss_ref[rows, :]
        queries_aug = jnp.where(first, queries, miss) if head == 0 else jnp.where(first, miss, queries)
        scores_s[n % 2] = dot_rows(queries_aug, keys_aug[head])

    def weigh(n):
        scores = scores_s[n % 2]
        largest = jnp.max(scores, axis=1, keepdims=True)
        weights_s[n % 2] = jnp.exp(scores - largest).astype(BF)
        largest_s[n % 2] = jnp.broadcast_to(largest, largest_s.shape[1:])

    def mix(n):
        rows, head = units[n]
        mixed = dot_plain(weights_s[n % 2], values_aug[head])
        total = mixed[:, 64:65] if head == 0 else mixed[:, 0:1]
        out, log = mixed / total, largest_s[n % 2] + jnp.log(total)
        if head == 0:
            mixed_s[0] = out
            mixed_s[1] = log
        else:
            out_ref[rows, :] = jnp.where(first, mixed_s[0], out).astype(BF)
            lse_ref[0, rows, :] = jnp.where(first, mixed_s[1], log)

    for turn in range(len(units) + 2):
        if turn < len(units):
            score(turn)
        if turn >= 2:
            mix(turn - 2)
        if 1 <= turn <= len(units):
            weigh(turn - 1)

    @pl.when(step == pl.num_programs(0) - 1)
    def _():
        store().wait()
        for copy in exchange():
            copy.wait()


def attention_forward(projected, miss, own, cotangent, block=256):
    count, width = projected.shape
    pairs = width // 384
    column = lambda base: pl.BlockSpec((count, 128), lambda i: (0, i + base))
    full = pl.BlockSpec((count, 128), lambda i: (0, 0))
    return pl.pallas_call(
        functools.partial(attention_forward_kernel, block),
        grid=(pairs,),
        in_specs=[column(0), column(pairs), column(2 * pairs), full, full, ANY],
        out_specs=[column(0), pl.BlockSpec((1, count, 128), lambda i: (i, 0, 0)), ANY],
        out_shape=[
            jax.ShapeDtypeStruct((count, width // 3), BF),
            jax.ShapeDtypeStruct((pairs, count, 128), F32),
            jax.ShapeDtypeStruct((count, width // 3), BF),
        ],
        scratch_shapes=[
            pltpu.VMEM((2, block, count), F32), pltpu.VMEM((2, block, count), BF), pltpu.VMEM((2, block, 128), F32),
            pltpu.VMEM((2, block, 128), F32), pltpu.VMEM((count // 4, width // 3), BF), pltpu.SemaphoreType.DMA((3,)),
            pltpu.SemaphoreType.DMA((3,)), pltpu.SemaphoreType.DMA,
        ],
        compiler_params=pltpu.CompilerParams(collective_id=3, has_side_effects=True, vmem_limit_bytes=VMEM_GRANT),
        cost_estimate=pl.CostEstimate(flops=24 * 10**9, bytes_accessed=8 * 2**20, transcendentals=12 * 2**20),
        name="attention_forward",
    )(projected, projected, projected, miss, own, cotangent)


def three_parts(column):
    high = column.astype(BF)
    rest = column - high.astype(F32)
    middle = rest.astype(BF)
    return high, middle, (rest - middle.astype(F32)).astype(BF)


def segment_features(segment):
    lane = jnp.arange(128) % 64
    same = lane[None, :] == segment[:, None]
    live = (lane < 8)[None, :]
    return jnp.where(live & ~same, -BIG, 0.0).astype(BF), jnp.where(live & same, 1.0, 0.0).astype(BF)


def flipped(static, bits):
    total = 0
    for at, bit in enumerate(bits):
        weight = 1 << (len(bits) - 1 - at)
        total = total + weight * ((1 - bit) if static & weight else bit)
    return total


def own_bits(order):
    me, deep = lax.axis_index("seq"), lax.axis_index("dp") // 2
    parts = {"low": [me % 2], "high": [me // 2], "deep": [deep // 2, deep % 2]}
    return [bit for name in order for bit in parts[name]]


def blended(orders, which):
    if len(set(orders)) == 1:
        return own_bits(orders[0])
    last = len(orders) - 1
    total = [0] * 4
    for at, order in enumerate(orders):
        if last == 1:
            here = which if at else 1 - which
        else:
            here = ((2 - which) * (1 - which) // 2, which * (2 - which), which * (which - 1) // 2)[at]
        total = [old + here * bit for old, bit in zip(total, own_bits(order))]
    return total


def scatter_groups(out_ref, values, order, part=None, base=0):
    bits = order if isinstance(order, list) else own_bits(order)
    groups, first = 16, 0
    if part is not None:
        top, *bits = bits
        groups, first = 8, 8 * (part + top - 2 * part * top)
    size = values.shape[0] // groups
    for a in range(groups):
        rows = pl.ds(pl.multiple_of((first + flipped(a, bits)) * size, 16), size)
        out_ref[rows, base : base + values.shape[1]] = values[a * size : (a + 1) * size].astype(out_ref.dtype)


def peer_ids():
    me, depth = lax.axis_index("seq"), lax.axis_index("dp")
    high, low = me // 2, me % 2
    core, deep = depth % 2, depth // 2
    upper, lower = deep // 2, deep % 2
    return {
        ("core", 1): (2 * deep + 1 - core, me),
        ("low", 1): (depth, 2 * high + 1 - low),
        ("high", 1): (depth, 2 * (1 - high) + low),
        ("both", 1): (depth, 3 - me),
        ("deep", 1): (2 * (2 * upper + 1 - lower) + core, me),
        ("deep", 2): (2 * (2 * (1 - upper) + lower) + core, me),
        ("deep", 3): (2 * (3 - deep) + core, me),
    }


LOW_FIRST = ("low", "high", "deep")
HIGH_FIRST = ("high", "low", "deep")
DEEP_FIRST = ("deep", "high", "low")
FAN = {"low": 2, "high": 2, "deep": 4}
SEMS = 12


def landing_rows(order, rows):
    sizes = []
    for name in order:
        rows //= FAN[name]
        sizes.append((FAN[name] - 1) * rows)
    return sizes


class Sum:
    def __init__(self, order, rows, send, keep, core_buf, bufs, own, other, send_sems, recv_sems, local_sem):
        self.order, self.rows, self.send, self.keep = order, rows, send, keep
        self.core_buf, self.bufs, self.own, self.other = core_buf, bufs, own, other
        self.send_sems, self.recv_sems, self.local_sem = send_sems, recv_sems, local_sem
        self.sizes = []
        for name in order:
            rows //= FAN[name]
            self.sizes.append(rows)
        self.peers = peer_ids()

    def stage(self, at):
        if at == 0:
            moves = [(self.send, self.core_buf, ("core", 1))]
        elif at <= 3:
            name, size, buf = self.order[at - 1], self.sizes[at - 1], self.bufs[at - 1]
            moves = [
                (self.keep.at[pl.ds(k * size, size)], buf.at[pl.ds((k - 1) * size, size)], (name, k))
                for k in range(1, FAN[name])
            ]
        elif at <= 6:
            name, size = self.order[6 - at], self.sizes[6 - at]
            src = self.keep if at == 4 else self.own
            moves = [
                (src.at[pl.ds(0, size)], self.own.at[pl.ds(k * size, size)], (name, k)) for k in range(1, FAN[name])
            ]
        else:
            moves = [(self.own, self.other, ("core", 1))]
        counts = [1] + [FAN[name] - 1 for name in self.order]
        base = sum((counts + counts[:0:-1])[:at])
        return [
            pltpu.make_async_remote_copy(
                src_ref=src, dst_ref=dst, send_sem=self.send_sems.at[base + k], recv_sem=self.recv_sems.at[base + k],
                device_id=self.peers[peer], device_id_type=MESH,
            )
            for k, (src, dst, peer) in enumerate(moves)
        ]

    def local(self):
        rows = pl.ds(0, self.sizes[2])
        return pltpu.make_async_copy(self.keep.at[rows], self.own.at[rows], self.local_sem)

    def start(self, stage):
        for copy in self.stage(stage):
            copy.start()

    def arrived(self, stage):
        for copy in self.stage(stage):
            copy.wait_recv()

    def left(self, first, last):
        for stage in range(first, last):
            for copy in self.stage(stage):
                copy.wait_send()

    def add(self, start, size, sources):
        chunk = next(rows for rows in (64, 48, 32) if size % rows == 0)

        def body(at, carry):
            rows = lambda base: pl.ds(pl.multiple_of(base + at * chunk, 16), chunk)
            total = self.keep[rows(start), :].astype(F32)
            for buf, offset in sources:
                total = total + buf[rows(offset + start), :].astype(F32)
            self.keep[rows(start), :] = total.astype(self.keep.dtype)
            return carry

        lax.fori_loop(0, size // chunk, body, 0)

    def sources(self, stage):
        if stage == 0:
            return [(self.core_buf, 0)]
        size = self.sizes[stage - 1]
        return [(self.bufs[stage - 1], k * size) for k in range(FAN[self.order[stage - 1]] - 1)]

    def settle(self, stage):
        self.arrived(stage)
        self.add(0, self.rows if stage == 0 else self.sizes[stage - 1], self.sources(stage))

    def tick(self, at, resumed=False):
        if at == 0 or resumed:
            if at == 4:
                self.local().start()
            self.start(at)
        elif at <= 3:
            self.arrived(at - 1)
            sources, size = self.sources(at - 1), self.sizes[at - 1]
            self.add(size, (self.rows if at == 1 else self.sizes[at - 2]) - size, sources)
            self.start(at)
            self.add(0, size, sources)
        elif at == 4:
            self.settle(3)
            self.local().start()
            self.start(4)
        elif at <= 7:
            self.arrived(at - 1)
            if at == 5:
                self.local().wait()
            self.start(at)
        else:
            self.arrived(7)


UNITS = 3


def gelu_parts(values):
    size = jnp.abs(values)
    bell = jnp.exp(-0.5 * values * values)
    part = 1.0 / (1.0 + 0.3275911 * 0.7071067811865476 * size)
    series = part * (
        0.127414796
        + part * (-0.142248368 + part * (0.7107068705 + part * (-0.7265760135 + part * 0.5307027145)))
    )
    tail = series * bell
    below = jnp.where(values >= 0, 1.0 - tail, tail)
    return values * below, below + values * (bell * 0.3989422804014327)


FEED_PLAN = {
    (3, 0): [(0, 0)],
    (3, 1): [(0, 1)],
    (5, 0): [(1, 0), (0, 2)],
    (5, 1): [(1, 1)],
    (6, 0): [(0, 3)],
    (6, 2): [(1, 2)],
}


def feed_kernel(
    row_ref, att_ref, cot_ref, out_weight_ref, out_bias_ref, gain_ref, shift_ref, fc2_bias_ref,
    w1_ref, bias_ref, w2_ref, *refs
):
    outs, refs = refs[:17], refs[17:]
    results, (branch_out, att_grad_out), sums_out = outs[:4], outs[4:6], outs[6:10]
    last_out, vec_ref = outs[10:16], outs[16]
    (
        n2_s, mid_s, acc_s, back_s, grad_s, hidden_s, hidden_grad_s, result_s, branch_s, att_grad_s,
        d1_s, d2_s, do_s, pre_s, down_s, bias_s, core1, core2, near1, near2, next1, next2, last1, last2, send_sems, recv_sems, load_sem, out_sems,
    ) = refs
    step = pl.program_id(0)
    core = lax.axis_index("dp") % 2
    count = row_ref.shape[0]
    size = w1_ref.shape[1]
    shard = count // 4
    half = do_s.shape[2]
    blocks = [pl.ds(i * shard, shard) for i in range(4)]
    peers = peer_ids()

    def job(unit, which):
        slot = 2 * unit + which
        d, bufs = (d1_s, (core1, near1, next1)) if which == 0 else (d2_s, (core2, near2, next2))
        return Sum(
            (LOW_FIRST, HIGH_FIRST)[which], d.shape[1], d.at[2 * unit], d.at[2 * unit + 1], bufs[0].at[unit],
            [bufs[1].at[unit], bufs[2].at[unit], (last1, last2)[which]], None, None, send_sems.at[slot], recv_sems.at[slot], None,
        )

    def ticks(at, place):
        for unit, tick in FEED_PLAN.get((at, place), []):
            for which in range(2):
                job(unit, which).tick(tick)

    def load():
        return pltpu.make_async_copy(cot_ref, grad_s, load_sem)

    def stores(first, last_store):
        pairs = [(result_s.at[rows], out) for rows, out in zip(blocks, results)]
        pairs += [(branch_s, branch_out), (att_grad_s, att_grad_out)]
        last = 2 * (UNITS - 1)
        pairs += [(d1_s.at[last], last_out[0]), (d1_s.at[last + 1], last_out[1])]
        pairs += [(d2_s.at[last], last_out[2]), (d2_s.at[last + 1], last_out[3])]
        pairs += [(do_s.at[0], last_out[4]), (do_s.at[1], last_out[5])]
        for unit in range(2):
            for which, d in enumerate((d1_s, d2_s)):
                rows = pl.ds(0, d.shape[1] // (4 if unit else 16))
                pairs.append((d.at[2 * unit + 1, rows], sums_out[2 * unit + which]))
        return [pltpu.make_async_copy(src, dst, out_sems.at[n]) for n, (src, dst) in enumerate(pairs) if first <= n < last_store]

    @pl.when(step == 0)
    def _():
        barrier = pltpu.get_barrier_semaphore()
        for name, peer in peers.items():
            if name != ("both", 1):
                pl.semaphore_signal(barrier, inc=1, device_id=peer, device_id_type=MESH)
        load().start()
        vec_ref[...] = jnp.zeros_like(vec_ref)
        for at in range(2 * UNITS):
            bias_s[at : at + 1, :] = bias_ref[at * size : (at + 1) * size].reshape(1, -1)

        def project(i, carry):
            rows = pl.ds(pl.multiple_of(i * shard, shard), shard)
            mid = row_ref[rows, :].astype(F32) + (dot_plain(att_ref[rows, :], out_weight_ref[...]) + row_of(out_bias_ref))
            mid_s[rows, :] = mid
            acc_s[rows, :] = mid + row_of(fc2_bias_ref)
            unit, _ = unit_norm(mid)
            n2_s[rows, :] = (unit * row_of(gain_ref) + row_of(shift_ref)).astype(BF)
            return carry

        lax.fori_loop(0, 4, project, 0)
        back_s[...] = jnp.zeros_like(back_s)
        load().wait()

    @pl.when(step == 2)
    def _():
        pl.semaphore_wait(pltpu.get_barrier_semaphore(), 6)

    for at in range(1, 2 * UNITS + 1):
        unit, keeping = (at - 1) // 2, (at - 1) % 2

        @pl.when(step == at)
        def _():
            ticks(at, 0)

    last_step = step == 2 * UNITS

    at_chunk = jnp.maximum(step - 1, 0)
    chunk_row = 2 * (at_chunk // 2) + (core + 1 + at_chunk % 2) % 2

    @pl.when(step > 0)
    def _():
        bias = bias_s[pl.ds(chunk_row, 1), :]

        pre_s[...] = dot_plain(n2_s[...], w1_ref[...]) + bias
        down_s[...] = dot_rows(grad_s[...], w2_ref[...])
        total = jnp.zeros((1, size), F32)
        for rows in blocks:
            hidden, slope = gelu_parts(pre_s[rows, :])
            hidden_grad = (down_s[rows, :] * slope).astype(BF)
            hidden_s[rows, :] = hidden.astype(BF)
            hidden_grad_s[rows, :] = hidden_grad
            total = total + total_rows(hidden_grad.astype(F32))
        acc_s[...] += dot_plain(hidden_s[...], w2_ref[...])
        back_s[...] += dot_rows(hidden_grad_s[...], w1_ref[...])
        vec_ref[pl.ds(4 + chunk_row, 1), 0:size] = total

    @pl.when(last_step)
    def _():
        def body(i, sums):
            rows = pl.ds(pl.multiple_of(i * shard, shard), shard)
            result_s[rows, :] = acc_s[rows, :].astype(BF)
            back = back_s[rows, :]
            unit, inverse = unit_norm(mid_s[rows, :])
            wide = grad_s[rows, :].astype(F32)
            branch = (wide + norm_back(unit, inverse, back, row_of(gain_ref))).astype(BF)
            branch_s[rows, :] = branch
            parts = (back * unit, back, branch.astype(F32), wide)
            return tuple(old + total_rows(part) for old, part in zip(sums, parts))

        sums = lax.fori_loop(0, 4, body, (jnp.zeros((1, n2_s.shape[1]), F32),) * 4)
        for at, part in enumerate(sums):
            vec_ref[at + 10 : at + 11, :] = part
        att_grad_s[...] = dot_rows(branch_s[...], out_weight_ref[...]).astype(BF)
        for copy in stores(0, 6):
            copy.start()

    for at in range(1, 2 * UNITS + 1):

        @pl.when(step == at)
        def _():
            ticks(at, 1)

    @pl.when(step > 0)
    def _():
        order = blended(ORDERS[1:6:2], (step - 1) // 2)
        scatter_groups(d1_s.at[step - 1], dot_tokens(n2_s[...], hidden_grad_s[...]), LOW_FIRST)
        scatter_groups(d2_s.at[step - 1], dot_tokens(hidden_s[...], grad_s[...]), order)

    @pl.when(last_step)
    def _():
        ticks(2 * UNITS, 2)

        for slot in range(2):
            columns = pl.ds(pl.multiple_of(((core + 1 + slot) % 2) * half, 128), half)
            scatter_groups(do_s.at[slot], dot_tokens(att_ref[...], branch_s[:, columns]), ORDERS[6])
        for copy in stores(6, 12):
            copy.start()
        for unit in range(2):
            for which in range(2):
                job(unit, which).settle(2 if unit else 3)
        for copy in stores(12, 16):
            copy.start()
        for copy in stores(0, 16):
            copy.wait()
        for unit in range(2):
            for which in range(2):
                job(unit, which).left(0, 3 if unit else 4)


def feed(row, attended, cotangent, out_weight, out_bias, gain, shift, fc1_weight, fc1_bias, fc2_weight, fc2_bias):
    count, features = row.shape
    size = fc1_weight.shape[1] // (2 * UNITS)
    half = features // 2
    shape = jax.ShapeDtypeStruct
    wide, line = once((count, features)), once((features,))
    vmem, dma = pltpu.VMEM, pltpu.SemaphoreType.DMA

    def chunk(i):
        at = jnp.maximum(i - 1, 0)
        return 2 * (at // 2) + (lax.axis_index("dp") % 2 + 1 + at % 2) % 2

    return pl.pallas_call(
        feed_kernel,
        grid=(2 * UNITS + 1,),
        in_specs=[wide, wide, ANY] + [once(out_weight.shape), line, line, line, line]
        + [
            pl.BlockSpec((features, size), lambda i: (0, chunk(i))),
            once(fc1_bias.shape),
            pl.BlockSpec((size, features), lambda i: (chunk(i), 0)),
        ],
        out_specs=[ANY] * 16 + [once((16, features))],
        out_shape=[shape((count // 4, features), BF)] * 4 + [shape((count, features), BF)] * 2
        + [shape((rows // part, columns), BF) for part in (16, 4) for rows, columns in ((features, size), (size, features))]
        + [shape((features, size), BF)] * 2 + [shape((size, features), BF)] * 2
        + [shape((features, half), BF)] * 2 + [shape((16, features), F32)],
        scratch_shapes=[vmem((count, features), BF)] + [vmem((count, features), F32)] * 3
        + [vmem((count, features), BF), vmem((count, size), BF), vmem((count, size), BF)]
        + [vmem((count, features), BF)] * 3
        + [
            vmem((2 * UNITS, features, size), BF), vmem((2 * UNITS, size, features), BF), vmem((2, features, half), BF),
            vmem((count, size), F32), vmem((count, size), F32), vmem((8, size), F32),
            vmem((2, features, size), BF), vmem((2, size, features), BF),
            vmem((2, features // 2, size), BF), vmem((2, size // 2, features), BF),
            vmem((2, features // 4, size), BF), vmem((2, size // 4, features), BF),
            vmem((3 * features // 16, size), BF), vmem((3 * size // 16, features), BF),
            dma((4, SEMS)), dma((4, SEMS)), dma, dma((16,)),
        ],
        compiler_params=pltpu.CompilerParams(collective_id=2, has_side_effects=True, vmem_limit_bytes=VMEM_GRANT),
        cost_estimate=pl.CostEstimate(flops=35 * 10**9, bytes_accessed=40 * 2**20, transcendentals=0),
        name="feed",
    )(
        row, attended, cotangent, out_weight, out_bias, gain, shift, fc2_bias, fc1_weight, fc1_bias, fc2_weight,
    )


ORDERS = (
    LOW_FIRST, HIGH_FIRST, LOW_FIRST, HIGH_FIRST, LOW_FIRST, HIGH_FIRST, HIGH_FIRST, LOW_FIRST, HIGH_FIRST, LOW_FIRST,
)
FIRST_TICK = (4, 4, 3, 3, 0, 0, 0, 0, 0, 0)
PLAN = {
    (0, 0): [(4, 0), (0, 4)],
    (1, 0): [(4, 1)],
    (1, 1): [(5, 0), (3, 3), (0, 5)],
    (2, 0): [(1, 4), (6, 0)],
    (3, 0): [(5, 1), (6, 1)],
    (3, 1): [(1, 5), (2, 3), (3, 4)],
    (4, 0): [(7, 0)],
    (5, 0): [(7, 1), (4, 2), (0, 6)],
    (5, 1): [(2, 4), (3, 5)],
    (7, 1): [(1, 6), (2, 5)],
    (8, 0): [(8, 0)],
    (9, 0): [(6, 2), (8, 1), (4, 3)],
    (9, 1): [(5, 2), (3, 6)],
    (11, 0): [(7, 2), (4, 4)],
    (11, 1): [(6, 3), (2, 6), (0, 7)],
    (12, 0): [(5, 3), (9, 0)],
    "tail": [
        (6, 4), (9, 1), (4, 5), (5, 4), (2, 7), (7, 3), (8, 2), (1, 7), (6, 5), (9, 2), (7, 4), (5, 5),
        (4, 6), (3, 7), (8, 3), (9, 3), (6, 6), (7, 5), (8, 4), (5, 6), (9, 4), (7, 6), (4, 7), (8, 5),
        (9, 5), (6, 7), (8, 6), (7, 7), (9, 6), (5, 7), (8, 7), (9, 7),
    ],
}
BLOCK_OUT_AT = (0, 0)


def three_parts(column):
    high = column.astype(BF)
    rest = column - high.astype(F32)
    middle = rest.astype(BF)
    return high, middle, (rest - middle.astype(F32)).astype(BF)


def pair_backward(refs, outs, dk_acc, dv_acc, pair, part, block):
    q_ref, k_ref, v_ref, att_ref, grad_ref, lse_ref, miss_ref, own_ref = refs
    lane = lax.broadcasted_iota(jnp.int32, (1, 128), 1)
    first = lane < 64
    half = lane % 64
    keys, values, own = k_ref[...], v_ref[...], own_ref[...]
    unit = jnp.where((half >= 8) & (half < 11), 1.0, 0.0).astype(BF)
    own = own + unit
    unit_rows = jnp.broadcast_to(unit, values.shape)
    keys_aug = [jnp.where(first, keys, own), jnp.where(first, own, keys)]
    values_aug = [jnp.where(first, values, unit_rows), jnp.where(first, unit_rows, values)]
    keys_only = [jnp.where(first, keys, BF(0)), jnp.where(first, BF(0), keys)]

    @pl.when(part == 0)
    def _():
        dk_acc[...] = jnp.zeros_like(dk_acc)
        dv_acc[...] = jnp.zeros_like(dv_acc)

    columns = pl.ds(pl.multiple_of(pair * 128, 128), 128)

    def spread(column):
        high, middle, low = [part.astype(F32) for part in three_parts(-column)]
        wide = jnp.where(half == 8, high, jnp.where(half == 9, middle, jnp.where(half == 10, low, 0.0)))
        return wide.astype(BF)

    def body(step, carry):
        rows = pl.ds(pl.multiple_of(step * block, block), block)
        queries, miss, grad = q_ref[rows, :] * BF(0.125), miss_ref[rows, :], grad_ref[rows, :]
        both = att_ref[rows, :].astype(F32) * grad.astype(F32)
        logs = lse_ref[0, rows, :]
        queries_t, grad_t = queries.T, grad.T
        dq = jnp.zeros((block, 128), F32)
        for head in range(2):
            mine = first if head == 0 else jnp.logical_not(first)
            span = pl.ds(64 * head, 64)
            delta = jnp.sum(jnp.where(mine, both, 0.0), axis=1, keepdims=True)
            total = logs[:, 0:1] if head == 0 else logs[:, 64:65]
            queries_aug = jnp.where(mine, queries, spread(total) + miss)
            grad_aug = jnp.where(mine, grad, spread(delta))
            probs = jnp.exp(dot_rows(queries_aug, keys_aug[head]))
            score_grad = (probs * dot_rows(grad_aug, values_aug[head])).astype(BF)
            dq = dq + dot_plain(score_grad, keys_only[head])
            dk_acc[span, :] += dot_plain(queries_t[64 * head : 64 * head + 64], score_grad)
            dv_acc[span, :] += dot_plain(grad_t[64 * head : 64 * head + 64], probs.astype(BF))
        outs[0][rows, columns] = (dq * 0.125).astype(BF)
        return carry

    steps = q_ref.shape[0] // block // 2
    lax.fori_loop(part * steps, (part + 1) * steps, body, 0)

    @pl.when(part == 1)
    def _():
        outs[1][:, columns] = dk_acc[...].T.astype(BF)
        outs[2][:, columns] = dv_acc[...].T.astype(BF)


def backward_kernel(*refs):
    (
        q_ref, k_ref, v_ref, att_ref, grad_ref, lse_ref, miss_ref, own_ref, normed_ref,
        weight_ref, row_ref, branch_ref, gain_ref, vec_in_ref,
    ) = refs[:14]
    results, sums_in, last_in = refs[14:18], refs[18:22], refs[22:28]
    block_out, vec_out = refs[28:30]
    token_outs = refs[30:34]
    owns, others = refs[34:44], refs[44:54]
    (
        dq_s, dk_s, dv_s, dk_acc, dv_acc, qkv_s, own_result, grad_s, vec_s, vec_got,
        send_sems, recv_sems, local_sems, load_sems, side_send, side_recv, vec_send, vec_recv,
    ) = refs[54:72]
    held = refs[72:79]
    landing = refs[79:]
    step = pl.program_id(0)
    me, depth = lax.axis_index("seq"), lax.axis_index("dp")
    core = depth % 2
    peers = peer_ids()
    shard = results[0].shape[0]
    features = row_ref.shape[1]

    def job(n):
        sems = send_sems.at[n], recv_sems.at[n], local_sems.at[n]
        if n < 4:
            bufs = [None, None, landing[n - 2] if n > 1 else None]
            return Sum(ORDERS[n], owns[n].shape[0], None, held[n], None, bufs, owns[n], others[n], *sems)
        send = last_in[2 * (n - 4)] if n < 7 else qkv_s.at[2 * (n - 7)]
        keep = held[n] if n < 7 else qkv_s.at[2 * (n - 7) + 1]
        core_buf, *bufs = landing[4 * n - 14 : 4 * n - 10]
        return Sum(ORDERS[n], keep.shape[0], send, keep, core_buf, bufs, owns[n], others[n], *sems)

    def load(n):
        if n == 7:
            return pltpu.make_async_copy(results[0], own_result, load_sems.at[7])
        src = sums_in[n] if n < 4 else last_in[2 * (n - 4) + 1]
        return pltpu.make_async_copy(src, held[n], load_sems.at[n])

    def store():
        return pltpu.make_async_copy(own_result, block_out.at[me, 0], load_sems.at[7])

    def token_store(k):
        return pltpu.make_async_copy(grad_s.at[k], token_outs[k], load_sems.at[8 + k])

    kinds = [("low", 1), ("high", 1), ("both", 1)]

    def block_copy(k):
        return pltpu.make_async_remote_copy(
            src_ref=results[k], dst_ref=block_out.at[me, 0], send_sem=side_send.at[k - 1],
            recv_sem=side_recv.at[k - 1], device_id=peers[kinds[k - 1]], device_id_type=MESH,
        )

    vec_names = [[("core", 1)], kinds, [("deep", 1), ("deep", 2), ("deep", 3)]]

    def vec_stage(stage):
        return [
            pltpu.make_async_remote_copy(
                src_ref=vec_s.at[stage], dst_ref=vec_got.at[stage, k],
                send_sem=vec_send.at[stage, k], recv_sem=vec_recv.at[stage, k],
                device_id=peers[name], device_id_type=MESH,
            )
            for k, name in enumerate(vec_names[stage])
        ]

    def vec_step(stage):
        for copy in vec_stage(stage):
            copy.wait_recv()
        total = vec_s[stage]
        for k in range(len(vec_names[stage])):
            total = total + vec_got[stage, k]
        if stage == 2:
            vec_out[...] = total
        else:
            vec_s[stage + 1] = total
            for copy in vec_stage(stage + 1):
                copy.start()

    def ticks(at, place):
        for n, tick in PLAN.get((at, place), []):
            resumed = tick == FIRST_TICK[n] > 0
            if resumed or (4 <= n < 7 and tick == 1):
                load(n).wait()
            job(n).tick(tick, resumed)

    @pl.when(step == 0)
    def _():
        barrier = pltpu.get_barrier_semaphore()
        for peer in peers.values():
            pl.semaphore_signal(barrier, inc=1, device_id=peer, device_id_type=MESH)
        for n in range(8):
            load(n).start()
        pl.semaphore_wait(barrier, len(peers))

    for at in range(13):

        @pl.when(step == at)
        def _():
            if (at, 0) == BLOCK_OUT_AT:
                for k in (1, 2, 3):
                    block_copy(k).start()
            ticks(at, 0)
            if at == 2:
                load(7).wait()
                store().start()

    turn = step // 2
    pair = 2 * (turn // 2) + (core + 1 + turn % 2) % 2

    @pl.when(step < 12)
    def _():
        pair_backward(
            (q_ref, k_ref, v_ref, att_ref, grad_ref, lse_ref, miss_ref, own_ref),
            (dq_s, dk_s, dv_s), dk_acc, dv_acc, pair, step % 2, 256,
        )

    for at in range(1, 12, 2):

        @pl.when(step == at)
        def _():
            if (at, 1) == BLOCK_OUT_AT:
                for k in (1, 2, 3):
                    block_copy(k).start()
            ticks(at, 1)

    @pl.when((step < 12) & (step % 2 == 1))
    def _():
        columns = pl.ds(pl.multiple_of(pair * 128, 128), 128)
        grads = jnp.concatenate([part[:, columns] for part in (dq_s, dk_s, dv_s)], axis=1)
        vec_out[2:3, columns] = total_rows(grads[:, :128].astype(F32))
        vec_out[3:4, columns] = total_rows(grads[:, 256:].astype(F32))

        def body(part, carry):
            left = normed_ref[:, pl.ds(pl.multiple_of(part * (features // 2), 128), features // 2)]
            scatter_groups(qkv_s.at[turn], dot_tokens(left, grads), blended(ORDERS[7:10], turn // 2), part)
            return carry

        lax.fori_loop(0, 2, body, 0)

    @pl.when(step == 12)
    def _():
        def body(at, sums):
            k = 3 - at
            rows = pl.ds(pl.multiple_of(k * shard, shard), shard)
            back = dot_rows(dq_s[rows, :], weight_ref[:, :features])
            back = back + dot_rows(dk_s[rows, :], weight_ref[:, features : 2 * features])
            back = back + dot_rows(dv_s[rows, :], weight_ref[:, 2 * features :])
            unit, inverse = unit_norm(row_ref[rows, :].astype(F32))
            grad_s[k] = (branch_ref[rows, :].astype(F32) + norm_back(unit, inverse, back, row_of(gain_ref))).astype(BF)
            for piece in range(4):

                @pl.when(k == piece)
                def _():
                    token_store(piece).start()

            return tuple(old + total_rows(part) for old, part in zip(sums, (back * unit, back)))

        gain_sum, shift_sum = lax.fori_loop(0, 4, body, (jnp.zeros((1, features), F32),) * 2)
        vec_s[0] = vec_in_ref[...]
        vec_s[0, 0:1, :] = gain_sum
        vec_s[0, 1:2, :] = shift_sum
        vec_s[0, 2:4, :] = vec_out[2:4, :]
        vec_stage(0)[0].start()

    @pl.when(step == 13)
    def _():
        for index, (n, tick) in enumerate(PLAN["tail"]):
            if index in (3, 8, 13):
                vec_step((index - 3) // 5)
            job(n).tick(tick)
        for n in range(10):
            job(n).arrived(7)
        for n in range(10):
            job(n).left(FIRST_TICK[n], 8)
        store().wait()
        for k in range(4):
            token_store(k).wait()
        for k in (1, 2, 3):
            block_copy(k).wait()
        for stage in range(3):
            for copy in vec_stage(stage):
                copy.wait_send()


def backward(
    projected, attended, attended_grad, logs, miss, own, normed, qkv_weight, row, branch, gain, vec_in,
    results, sums_in, last_in,
):
    count, width = projected.shape
    features = width // 3
    pairs = width // 384
    half = features // 2
    shard = count // 4

    def pair(i):
        at = jnp.minimum(i // 2, 5)
        return 2 * (at // 2) + (lax.axis_index("dp") % 2 + 1 + at % 2) % 2

    column = lambda base: pl.BlockSpec((count, 128), lambda i: (0, pair(i) + base))
    shape = jax.ShapeDtypeStruct
    wide = once((count, features))
    full = once((count, 128))
    vmem, dma = pltpu.VMEM, pltpu.SemaphoreType.DMA
    sizes = [last_in[0].shape, last_in[2].shape] * UNITS + [(features, half)] * 4
    held = [vmem(array.shape, BF) for array in (*sums_in, *last_in[1::2])]
    landing = []
    for n, (rows, columns) in enumerate(sizes):
        lands = landing_rows(ORDERS[n], rows)
        landing += [vmem((size, columns), BF) for size in ([rows] + lands)[FIRST_TICK[n] :]]
    return pl.pallas_call(
        backward_kernel,
        grid=(14,),
        in_specs=[
            column(0), column(pairs), column(2 * pairs), column(0), column(0),
            pl.BlockSpec((1, count, 128), lambda i: (pair(i), 0, 0)),
            full, full, wide, once(qkv_weight.shape), wide, wide, once((features,)), once((16, features)),
        ]
        + [ANY] * 14,
        out_specs=[ANY, once((16, features))] + [ANY] * 24,
        out_shape=[shape((4, 1, shard, features), BF), shape((16, features), F32)] + [shape((shard, features), BF)] * 4
        + [shape(size, BF) for size in sizes] * 2,
        scratch_shapes=[vmem((count, features), BF)] * 3
        + [vmem((128, count), F32)] * 2
        + [vmem((6, features, half), BF)]
        + [
            vmem((shard, features), BF), vmem((4, shard, features), BF),
            vmem((3, 16, features), F32), vmem((3, 3, 16, features), F32),
            dma((10, SEMS)), dma((10, SEMS)), dma((10,)), dma((12,)), dma((3,)), dma((3,)), dma((3, 3)), dma((3, 3)),
        ]
        + held + landing,
        compiler_params=pltpu.CompilerParams(collective_id=1, has_side_effects=True, vmem_limit_bytes=VMEM_GRANT),
        cost_estimate=pl.CostEstimate(flops=60 * 10**9, bytes_accessed=60 * 2**20, transcendentals=12 * 2**20),
        name="backward",
    )(
        projected, projected, projected, attended, attended_grad, logs, miss, own, normed, qkv_weight, row, branch,
        gain, vec_in, *results, *sums_in, *last_in,
    )


STEPS = 8


def own_group(order):
    total = 0
    for bit in own_bits(order):
        total = 2 * total + bit
    return total


def assemble_kernel(*refs):
    ins, vec_ref = refs[:20], refs[20]
    d1_ref, d2_ref, out_ref, qkv_ref = refs[21:25]
    vecs = refs[25:]
    core = lax.axis_index("dp") % 2
    features = out_ref.shape[1]
    size = ins[0].shape[1]
    half = features // 2

    def ordered(n):
        ref, last = ins[n], own_bits(ORDERS[n // 2])[3]
        rows = ref.shape[0] // 2
        return jnp.concatenate(
            [ref[pl.ds(pl.multiple_of((a + last - 2 * a * last) * rows, 16), rows), :] for a in range(2)], axis=0
        ).astype(F32)

    for side in range(2):
        home = core if side == 0 else 1 - core
        for unit in range(UNITS):
            columns = pl.ds(pl.multiple_of((2 * unit + home) * size, 128), size)
            d1_ref[:, columns] = ordered(4 * unit + side)
            d2_ref[unit, home] = ordered(4 * unit + 2 + side)
        out_ref[:, pl.ds(pl.multiple_of(home * half, 128), half)] = ordered(12 + side)
        for group in range(3):
            values = ordered(14 + 2 * group + side)
            for part in range(3):
                at = part * features + (2 * group + home) * 128
                qkv_ref[:, pl.ds(pl.multiple_of(at, 128), 128)] = values[:, part * 128 : (part + 1) * 128]

    @pl.when(pl.program_id(0) == 0)
    def _():
        for ref, row in zip(vecs, (0, 1, 12, 10, 11, 13)):
            ref[...] = vec_ref[row, :]
        qv_ref, fc1_ref = vecs[6:]
        for at in range(2):
            qv_ref[at * features : (at + 1) * features] = vec_ref[2 + at, :]
        for at in range(2 * UNITS):
            fc1_ref[at * size : (at + 1) * size] = vec_ref[4 + at, 0:size]


def assemble(parts, vector):
    features, size = parts[0].shape
    half = features // 2
    wide = 2 * UNITS * size
    shape = jax.ShapeDtypeStruct

    def spec(n):
        rows, columns = parts[n].shape
        return pl.BlockSpec((rows // STEPS, columns), lambda i: (i ^ (own_group(ORDERS[n // 2]) // 2), 0))

    lines = [features] * 6 + [2 * features, wide]
    d1, d2, out, qkv, *vecs = pl.pallas_call(
        assemble_kernel,
        grid=(STEPS,),
        in_specs=[spec(n) for n in range(20)] + [once(vector.shape)],
        out_specs=[
            pl.BlockSpec((features // STEPS, wide), lambda i: (i, 0)),
            pl.BlockSpec((UNITS, 2, size // STEPS, features), lambda i: (0, 0, i, 0)),
            pl.BlockSpec((features // STEPS, features), lambda i: (i, 0)),
            pl.BlockSpec((features // STEPS, 3 * features), lambda i: (i, 0)),
        ]
        + [once((line,)) for line in lines],
        out_shape=[
            shape((features, wide), F32), shape((UNITS, 2, size, features), F32), shape((features, features), F32),
            shape((features, 3 * features), F32),
        ]
        + [shape((line,), F32) for line in lines],
        compiler_params=pltpu.CompilerParams(vmem_limit_bytes=VMEM_GRANT),
        cost_estimate=pl.CostEstimate(flops=0, bytes_accessed=45 * 2**20, transcendentals=0),
        name="assemble",
    )(*parts, vector)
    return d1, d2.reshape(wide, features), out, qkv, vecs


def place_row_kernel(p0, p1, p2, p3, out_ref, held, sems):
    me = lax.axis_index("seq")
    pieces = (p0, p1, p2, p3)
    loads = [pltpu.make_async_copy(piece, held.at[k], sems.at[k]) for k, piece in enumerate(pieces)]
    stores = [pltpu.make_async_copy(held.at[k], out_ref.at[me ^ k, 0], sems.at[k + 4]) for k in range(4)]
    for copy in loads:
        copy.start()
    for load, store in zip(loads, stores):
        load.wait()
        store.start()
    for copy in stores:
        copy.wait()


def place_row(pieces):
    shard, features = pieces[0].shape
    return pl.pallas_call(
        place_row_kernel,
        in_specs=[ANY] * 4,
        out_specs=ANY,
        scratch_shapes=[pltpu.VMEM((4, shard, features), BF), pltpu.SemaphoreType.DMA((8,))],
        out_shape=jax.ShapeDtypeStruct((4, 1, shard, features), BF),
        compiler_params=pltpu.CompilerParams(vmem_limit_bytes=VMEM_GRANT),
        cost_estimate=pl.CostEstimate(flops=0, bytes_accessed=3 * 2**20, transcendentals=0),
        name="place_row",
    )(*pieces)


def swap(array, axis, bit):
    count = lax.axis_size(axis)
    return lax.ppermute(array, axis, [(i, i ^ bit) for i in range(count)])


def fast_shards(
    tokens, image_lengths, cotangent, attn_gain, attn_shift, qkv_weight, qv_bias, out_weight,
    out_bias, mlp_gain, mlp_shift, fc1_weight, fc1_bias, fc2_weight, fc2_bias,
):
    shard_len = tokens.shape[2]
    parties = lax.axis_size("seq")
    row_len = shard_len * parties
    images = image_lengths.shape[2] - 1
    me = lax.axis_index("seq")

    row, normed, projected = enter(tokens, attn_gain, attn_shift, qkv_weight, qv_bias)
    seg_row = segment_ids(lax.dynamic_index_in_dim(image_lengths, me, 0, keepdims=False), row_len, images)
    seg_row = seg_row.reshape(parties, shard_len)
    segment = jnp.concatenate([seg_row[me ^ k] for k in range(parties)], axis=0)
    miss, own = segment_features(segment)
    attended, logs, grads = attention_forward(projected, miss, own, cotangent)
    fed = feed(
        row, attended, grads, out_weight, out_bias, mlp_gain, mlp_shift, fc1_weight, fc1_bias, fc2_weight, fc2_bias
    )
    results, (branch, attended_grad), sums, last, vec = fed[:4], fed[4:6], fed[6:10], fed[10:16], fed[16]
    block_out, vector, *rest = backward(
        projected, attended, attended_grad, logs, miss, own, normed, qkv_weight, row, branch, attn_gain, vec,
        results, sums, last,
    )
    pieces, summed = rest[:4], rest[4:]
    paired = [part for n in range(10) for part in (summed[n], summed[10 + n])]
    tokens_grad = place_row([pieces[0]] + [swap(pieces[k], "seq", k) for k in (1, 2, 3)])
    fc1_grad, fc2_grad, out_grad, qkv_grad, vecs = assemble(paired, vector)
    gain, shift, out_sum, mlp_gain_sum, mlp_shift_sum, fc2_sum, qv_sum, fc1_sum = vecs
    return (
        block_out, tokens_grad, gain, shift, qkv_grad, qv_sum, out_grad, out_sum, mlp_gain_sum, mlp_shift_sum,
        fc1_grad, fc1_sum, fc2_grad, fc2_sum,
    )


def shards(tokens, *rest):
    micro_count, row_count, shard_len, features = tokens.shape
    whole_rows = micro_count == 4 and row_count == 1 and shard_len % 128 == 0
    sizes = lax.axis_size("dp") == 8 and lax.axis_size("seq") == 4
    hidden = rest[10].shape[1]
    if sizes and whole_rows and features == 64 * HEADS == 768 and hidden == 4 * features:
        return fast_shards(tokens, *rest)
    return general_shards(tokens, *rest)


def solution(mesh):
    placed = (
        P(None, "dp", "seq", None),
        P(None, "dp", None),
        P(None, "dp", "seq", None),
        P(),
        P(),
        P(),
        P(),
        P(),
        P(),
        P(),
        P(),
        P(),
        P(),
        P(),
        P(),
    )
    return jax.shard_map(
        shards,
        mesh=mesh,
        in_specs=placed,
        out_specs=(
            P(None, "dp", "seq", None),
            P(None, "dp", "seq", None),
            P(),
            P(),
            P(),
            P(),
            P(),
            P(),
            P(),
            P(),
            P(),
            P(),
            P(),
            P(),
        ),
        check_vma=False,
    )
```
